32 devices in a mesh: dp: 16 (over z, x, core), tensor: 2 (over y).
Axes of the slice: x: 2, y: 2, z: 4, core: 2. Of those that a mesh axis runs over, the one named last changes fastest.
Arguments:
- tokens: bfloat16 [16384, 1024], P('dp'), may hold values from -6 to 6
- doc_ids: int32 [16384], replicated, may hold values from 0 to 39, as said below
- routes: int32 [16384, 8], P('dp'), may hold values from 0 to 31, all different within a row; in each aligned block of 1024 rows (0 to 1023, 1024 to 2047, ...) at most 384 rows name the same one
- attention_gain: bfloat16 [1024], replicated, may hold values from 0.5 to 1.5
- w_query: bfloat16 [1024, 1024], P(None, 'tensor'), may hold values from -0.75 to 0.75
- w_key: bfloat16 [512, 1024], P('tensor'), may hold values from -0.75 to 0.75
- w_value: bfloat16 [512, 1024], P('tensor'), may hold values from -0.1875 to 0.1875
- w_out: bfloat16 [1024, 1024], P('tensor'), may hold values from -4 to 4
- mixture_gain: bfloat16 [1024], replicated, may hold values from 0.5 to 1.5
- w_router: bfloat16 [1024, 32], replicated, may hold values from -0.09375 to 0.09375
- expert_gate_up: bfloat16 [32, 2, 512, 1024], P(None, None, 'tensor'), may hold values from -0.1875 to 0.1875
- expert_down: bfloat16 [32, 512, 1024], P(None, 'tensor'), may hold values from -4 to 4
- out_cotangent: bfloat16 [16384, 1024], P('dp'), may hold values from -6 to 6
Outputs:
- mixed: bfloat16 [16384, 1024], P('dp')
- tokens_gradient: bfloat16 [16384, 1024], P('dp')
- attention_gain_gradient: float32 [1024], replicated
- w_query_gradient: float32 [1024, 1024], P(None, 'tensor')
- w_key_gradient: float32 [512, 1024], P('tensor')
- w_value_gradient: float32 [512, 1024], P('tensor')
- w_out_gradient: float32 [1024, 1024], P('tensor')
- mixture_gain_gradient: float32 [1024], replicated
- w_router_gradient: float32 [1024, 32], replicated
- expert_gate_up_gradient: float32 [32, 2, 512, 1024], P('dp', None, 'tensor')
- expert_down_gradient: float32 [32, 512, 1024], P('dp', 'tensor')
The draws below stay inside these ranges and needn't reach their ends.
Inputs may be any that keep to these rules, and one draw needn't show every extreme that they name: doc_ids never fall along the tokens; every sequence of 2048 tokens begins with a new number and holds exactly five documents. `routes`: each token names 8 different experts; in each aligned block of 1024 tokens no expert is named by more than 384 tokens.
All inputs are finite; a program needn't handle non-finite values.
Results may differ from the reference program's by a relative error of at most 0.025.
Values may be sent and summed in bfloat16 or wider, within the bound.
No kernel may reach another device: no remote copies, remote signals or barrier semaphores. Data moves between devices by JAX's collectives and lax.ppermute only.
A program may use at most 448 MiB of HBM per device.

```python
import math
import jax
import jax.numpy as jnp
import numpy as np
from jax import lax

D = 1024
HEADS = 16
KV_HEADS = 8
HEAD_DIM = 64
EXPERTS = 32
TOP = 8
EXP_FF = 512
TOK_DEV = 1024
SEQ_LEN = 2048
CAP = 384
TOKENS = 16384
N_TENSOR = 2


def draw_doc_ids(key, part):
    key = jax.random.fold_in(key, 11)
    sequences = TOKENS // SEQ_LEN
    quarter = SEQ_LEN // 4
    middle = quarter // 2
    key_a, key_b, key_c, key_d = jax.random.split(key, 4)
    first_a = jax.random.randint(key_a, (sequences, 1), 1, middle)
    first_b = jax.random.randint(key_b, (sequences, 1), middle, quarter)
    last_a = jax.random.randint(key_c, (sequences, 1), SEQ_LEN - quarter, SEQ_LEN - middle)
    last_b = jax.random.randint(key_d, (sequences, 1), SEQ_LEN - middle, SEQ_LEN)
    picks = jnp.concatenate([jnp.zeros((sequences, 1), jnp.int32), first_a, first_b, last_a, last_b], axis=1)
    within = jnp.arange(SEQ_LEN, dtype=jnp.int32)
    starts = jnp.any(within[None, :, None] == picks[:, None, :], axis=-1).reshape(TOKENS)
    return jnp.cumsum(starts.astype(jnp.int32)) - 1


def steps_of(key, shape, cuts, low, high):
    loudness = 1.0
    for dim, blocks in cuts:
        draws = jax.random.uniform(jax.random.fold_in(jax.random.fold_in(key, 6), dim), (blocks,), jnp.float32, low / len(cuts), high / len(cuts))
        loudness = loudness * jnp.repeat(jnp.exp(draws), shape[dim] // blocks).reshape((-1,) + (1,) * (len(shape) - 1 - dim))
    return loudness


def assign_block(own_key, own, number, rows, number_of, top, bound, slope):
    sequence = jax.random.permutation(own_key, number_of)
    crowded, usual = portions_of(number_of, rows * top, bound, slope, True), portions_of(number_of, rows * top, bound, slope, False)
    places = jnp.arange(number_of)

    def named(lengths, turn):
        used = int((lengths > 0).sum())
        fixed = max(1, used // 4)
        moved = fixed + (places - fixed + turn * (used - fixed)) % max(1, number_of - fixed)
        return jnp.zeros((number_of,), jnp.int32).at[sequence[jnp.where(places < fixed, places, moved)]].set(jnp.asarray(lengths, jnp.int32))

    lengths = jnp.where(number % 4 == 0, named(crowded, number // 4), named(usual, number - number // 4 - 1))
    mixed = jax.random.permutation(jax.random.fold_in(own, 3), number_of)
    source_of, receiver = mixed[0:number_of // 2 * 2:2], mixed[1:number_of // 2 * 2:2]
    margin = jnp.minimum(lengths[source_of] - 1, bound - lengths[receiver]) // 2
    margin = jnp.where((source_of == sequence[0]) | (receiver == sequence[0]) | (lengths[receiver] == 0), 0, jnp.maximum(margin, 0))
    moved = jax.random.randint(jax.random.fold_in(own, 4), (number_of // 2,), 0, 1 << 20) % (margin + 1)
    lengths = lengths.at[source_of].add(-moved).at[receiver].add(moved)
    labels = jnp.searchsorted(jnp.cumsum(lengths), jnp.arange(rows * top), side="right").astype(jnp.int32)
    grid = labels.reshape(top, rows).T
    grid = grid[jax.random.permutation(jax.random.fold_in(own, 1), rows)]
    turn = jax.random.randint(jax.random.fold_in(own, 2), (rows, 1), 0, top)
    return jnp.take_along_axis(grid, (jnp.arange(top)[None, :] + turn) % top, axis=1)


def portions_of(number_of, total, reach, skew, full):
    loads = [(1 << 20) // math.isqrt(rank ** skew) + 1 for rank in range(1, number_of + 1)]
    largest = reach if full else min(reach, max(-(-total // number_of), total * loads[0] // sum(loads)))
    least = 1 if total - largest >= number_of - 1 else 0
    given, surplus = [largest] + [least] * (number_of - 1), total - largest - least * (number_of - 1)
    while surplus > 0:
        free = [i for i in range(1, number_of) if given[i] < largest] or [i for i in range(1, number_of) if given[i] < reach]
        mass, remaining = sum([loads[i] for i in free]), surplus
        for i in free:
            extra = min(reach - given[i], max(1, remaining * loads[i] // mass), surplus)
            given[i] = given[i] + extra
            surplus = surplus - extra
    return np.array(given)


def scatter_about(own_key, dims, scale, reach, cuts=(), held_as=jnp.bfloat16):
    array = scale * jax.random.normal(own_key, dims, jnp.float32)
    if cuts:
        array = array * steps_of(own_key, dims, cuts, -0.22, 0.18)
    return jnp.clip(array, -reach, reach).astype(held_as)


def setup_inputs(seed: int = 0) -> dict:
    streams_of = jax.random.split(jax.random.key(seed), 14)
    tokens = scatter_about(streams_of[0], (TOKENS, D), 1.0, 6.0, ((0, 16),))
    doc_ids = draw_doc_ids(jax.random.fold_in(streams_of[13], 71), 0)
    routes_keys = jax.random.split(jax.random.fold_in(streams_of[2], 1), TOKENS // TOK_DEV)
    routes_turns = jax.random.permutation(jax.random.fold_in(streams_of[2], 3), TOKENS // TOK_DEV)
    routes = jax.vmap(lambda own, number: assign_block(jax.random.fold_in(streams_of[2], 2), own, number, TOK_DEV, EXPERTS, TOP, CAP, 1))(routes_keys, routes_turns).reshape((TOKENS, TOP))
    attention_gain = jnp.clip(1.0 + 0.1 * jax.random.normal(streams_of[3], (D,), jnp.float32), 0.5, 1.5).astype(jnp.bfloat16)
    w_query = scatter_about(streams_of[4], (D, HEADS * HEAD_DIM), (D // 16) ** -0.5, 0.75, ((1, 2),))
    w_key = scatter_about(streams_of[5], (KV_HEADS * HEAD_DIM, D), (D // 16) ** -0.5, 0.75, ((0, 2),))
    w_value = scatter_about(streams_of[6], (KV_HEADS * HEAD_DIM, D), D ** -0.5, 0.1875, ((0, 2),))
    w_out = scatter_about(streams_of[7], (HEADS * HEAD_DIM, D), (max(HEADS * HEAD_DIM // 512, 1)) ** -0.5, 4.0, ((0, 2),))
    mixture_gain = jnp.clip(1.0 + 0.1 * jax.random.normal(streams_of[8], (D,), jnp.float32), 0.5, 1.5).astype(jnp.bfloat16)
    w_router = scatter_about(streams_of[9], (D, EXPERTS), (4 * D) ** -0.5, 0.09375)
    expert_gate_up = scatter_about(streams_of[10], (EXPERTS, 2, EXP_FF, D), D ** -0.5, 0.1875, ((2, 2),))
    expert_down = scatter_about(streams_of[11], (EXPERTS, EXP_FF, D), (max(EXP_FF // 256, 1)) ** -0.5, 4.0, ((1, 2),))
    out_cotangent = scatter_about(streams_of[12], (TOKENS, D), 1.0, 6.0, ((0, 16),))
    return {"tokens": tokens, "doc_ids": doc_ids, "routes": routes, "attention_gain": attention_gain, "w_query": w_query, "w_key": w_key, "w_value": w_value, "w_out": w_out, "mixture_gain": mixture_gain, "w_router": w_router, "expert_gate_up": expert_gate_up, "expert_down": expert_down, "out_cotangent": out_cotangent}


epsilon = 1e-06
score_scale = 0.015625
residual_scale = 0.22
rope_base = 10000.0
masked_value = -1e+30
highest = lax.Precision.HIGHEST

@jax.custom_vjp
def low(v):
    return lax.optimization_barrier(v.astype(jnp.bfloat16)).astype(jnp.float32)

@jax.custom_vjp
def low_back(v):
    return v

def low_keep(v):
    return (low(v), None)

def low_pass(kept, grad):
    return (grad,)

def back_keep(v):
    return (v, None)

def back_low(kept, grad):
    return (low(grad),)
low.defvjp(low_keep, low_pass)
low_back.defvjp(back_keep, back_low)

def norm_rows(values, gain):
    return values * lax.rsqrt(lax.optimization_barrier(jnp.mean(values * values, axis=-1, keepdims=True)) + epsilon) * gain

def rotate(values, position):
    width = values.shape[-1]
    half = width // 2
    inverse = rope_base ** (-2.0 * jnp.arange(half, dtype=jnp.float32) / width)
    angle = position.astype(jnp.float32)[:, None] * inverse[None, :]
    cosine = jnp.concatenate([jnp.cos(angle), jnp.cos(angle)], axis=-1)[:, None, :]
    sine = jnp.concatenate([jnp.sin(angle), jnp.sin(angle)], axis=-1)[:, None, :]
    turned = jnp.concatenate([-values[..., half:], values[..., :half]], axis=-1)
    return values * cosine + turned * sine

def slot_tables(routes):
    pairs = routes.shape[0] * routes.shape[1]
    flat = routes.reshape(-1)
    one_hot = (flat[:, None] == jnp.arange(EXPERTS, dtype=jnp.int32)[None, :]).astype(jnp.int32)
    earlier = lax.optimization_barrier(jnp.sum((jnp.cumsum(one_hot, axis=0) - one_hot) * one_hot, axis=1))
    place = flat * CAP + earlier
    source = jnp.full((EXPERTS * CAP,), pairs, jnp.int32).at[place].set(jnp.arange(pairs, dtype=jnp.int32))
    return (place, source)

def attend(query_rot, key_rot, value_low, docs):
    length = query_rot.shape[0]
    group = HEADS // KV_HEADS
    keys = jnp.repeat(key_rot, group, axis=1)
    values = jnp.repeat(value_low, group, axis=1)
    scores = low_back(jnp.einsum('qhd,khd->hqk', query_rot, keys, precision=highest) * score_scale)
    place = jnp.arange(length, dtype=jnp.int32)
    allowed = (place[None, :] <= place[:, None]) & (docs[None, :] == docs[:, None])
    scores = jnp.where(allowed[None], scores, masked_value)
    peak = lax.optimization_barrier(jnp.max(scores, axis=-1, keepdims=True))
    weights = jnp.exp(scores - peak)
    probs = low(weights / lax.optimization_barrier(jnp.sum(weights, axis=-1, keepdims=True)))
    return jnp.einsum('hqk,khd->qhd', probs, values, precision=highest)

def experts_block(normed, gates, routes, gate_up_weight, down_weight):
    place, source = slot_tables(routes)
    token_of = source // TOP
    padded = jnp.concatenate([normed, jnp.zeros((1, D), normed.dtype)], axis=0)
    expert_rows = padded[token_of].reshape(EXPERTS, CAP, D)
    gate_up = low_back(jnp.einsum('ecd,ejfd->ecjf', expert_rows, gate_up_weight, precision=highest))
    active = low(jax.nn.silu(gate_up[:, :, 0]) * gate_up[:, :, 1])
    share = EXP_FF // N_TENSOR
    outputs = low_back(jnp.einsum('ecgf,egfd->ecgd', active.reshape(EXPERTS, CAP, N_TENSOR, share), down_weight.reshape(EXPERTS, N_TENSOR, share, D), precision=highest))
    picked = outputs.reshape(EXPERTS * CAP, N_TENSOR, D)[place].reshape(normed.shape[0], TOP, N_TENSOR, D)
    parts = lax.optimization_barrier(jnp.sum(gates[:, :, None, None] * picked, axis=1))
    return lax.optimization_barrier(jnp.sum(low(parts), axis=1))

def forward(tokens, attention_gain, w_query, w_key, w_value, w_out, mixture_gain, w_router, expert_gate_up, expert_down, doc_ids, routes):
    count = tokens.shape[0]
    normed_attention = low(norm_rows(tokens, attention_gain))
    query_lin = low_back(jnp.dot(normed_attention, w_query, precision=highest))
    key_lin = low_back(jnp.dot(normed_attention, w_key.T, precision=highest))
    value_lin = low(low_back(jnp.dot(normed_attention, w_value.T, precision=highest)))
    position = jnp.arange(count, dtype=jnp.int32) % SEQ_LEN
    query_rot = low(rotate(query_lin.reshape(count, HEADS, HEAD_DIM), position))
    key_rot = low(rotate(key_lin.reshape(count, KV_HEADS, HEAD_DIM), position))
    value_low = value_lin.reshape(count, KV_HEADS, HEAD_DIM)
    sequences = count // SEQ_LEN
    context = lax.map(jax.checkpoint(lambda item: attend(item[0], item[1], item[2], item[3])), (query_rot.reshape(sequences, SEQ_LEN, HEADS, HEAD_DIM), key_rot.reshape(sequences, SEQ_LEN, KV_HEADS, HEAD_DIM), value_low.reshape(sequences, SEQ_LEN, KV_HEADS, HEAD_DIM), doc_ids.reshape(sequences, SEQ_LEN)))
    context = low(low_back(context.reshape(count, HEADS * HEAD_DIM)))
    parts = jnp.einsum('tgc,gcd->tgd', context.reshape(count, N_TENSOR, -1), w_out.reshape(N_TENSOR, -1, D), precision=highest)
    attention_out = low_back(lax.optimization_barrier(jnp.sum(low(parts), axis=1)))
    hidden = tokens + residual_scale * attention_out
    normed_mixture = low(norm_rows(hidden, mixture_gain))
    logits = jnp.dot(normed_mixture, w_router, precision=highest)
    gates = jax.nn.softmax(jnp.take_along_axis(logits, routes, axis=1), axis=-1)
    blocks = count // TOK_DEV
    mixture_out = lax.map(jax.checkpoint(lambda item: experts_block(item[0], item[1], item[2], expert_gate_up, expert_down)), (normed_mixture.reshape(blocks, TOK_DEV, D), gates.reshape(blocks, TOK_DEV, TOP), routes.reshape(blocks, TOK_DEV, TOP)))
    return hidden + residual_scale * mixture_out.reshape(count, D)

def reference(tokens, doc_ids, routes, attention_gain, w_query, w_key, w_value, w_out, mixture_gain, w_router, expert_gate_up, expert_down, out_cotangent):

    def run(tokens_in, gain_one, query_in, key_in, value_in, out_in, gain_two, router_in, gate_up_in, down_in):
        return forward(tokens_in, gain_one, query_in, key_in, value_in, out_in, gain_two, router_in, gate_up_in, down_in, doc_ids, routes)
    result, pull = jax.vjp(run, tokens.astype(jnp.float32), attention_gain.astype(jnp.float32), w_query.astype(jnp.float32), w_key.astype(jnp.float32), w_value.astype(jnp.float32), w_out.astype(jnp.float32), mixture_gain.astype(jnp.float32), w_router.astype(jnp.float32), expert_gate_up.astype(jnp.float32), expert_down.astype(jnp.float32))
    grads = pull(out_cotangent.astype(jnp.float32))
    return (result.astype(jnp.bfloat16), grads[0].astype(jnp.bfloat16), grads[1], grads[2], grads[3], grads[4], grads[5], grads[6], grads[7], grads[8], grads[9])
```

```python
import functools

import jax
import jax.numpy as jnp
from jax import lax
from jax.experimental import pallas as pl
from jax.experimental.pallas import tpu as pltpu
from jax.sharding import PartitionSpec as P

HEAD_DIM = 64
EXPERTS = 32
SEQ_LEN = 2048
BLOCK = 256

epsilon = 1e-06
score_scale = 0.015625
residual_scale = 0.22
rope_base = 10000.0
masked_value = -1e30
vmem_bytes = 48 * 1024 * 1024
f32 = jnp.float32
bf16 = jnp.bfloat16


def dot(left, right, left_dim, right_dim):
    return lax.dot_general(
        left, right, (((left_dim,), (right_dim,)), ((), ())), preferred_element_type=f32
    )


def mm(left, right):
    return jnp.dot(left, right, preferred_element_type=f32)


def block_mask(lo, hi, start, lanes):
    place = start + lax.broadcasted_iota(jnp.int32, (BLOCK, lanes), 0)
    return (place >= lo) & (place <= hi)


def window_of(lo_ref, block, before, group):
    cut = pl.ds(block * BLOCK, BLOCK)
    lo = lo_ref[:, cut]
    hi = before + block * BLOCK + lax.broadcasted_iota(jnp.int32, (1, BLOCK), 1)
    return (
        jnp.concatenate([lo] * group, axis=1),
        jnp.concatenate([hi] * group, axis=1),
    )


def heads_side_by_side(ref, block, group):
    cut = pl.ds(block * BLOCK, BLOCK)
    return jnp.concatenate(
        [ref[h * HEAD_DIM : (h + 1) * HEAD_DIM, cut] for h in range(group)], axis=1
    )


def heads_one_above(ref, block, group):
    cut = pl.ds(block * BLOCK, BLOCK)
    return jnp.concatenate([ref[0, h, cut, :] for h in range(group)], axis=0)


def attend_kernel(
    group, first_ref, lo_ref, qt_ref, k_ref, vt_ref, old_k_ref, old_vt_ref, out_ref, log_ref
):
    lanes = group * BLOCK
    before = old_k_ref.shape[1]
    passed = before // BLOCK
    for block in range(qt_ref.shape[1] // BLOCK):
        lo, hi = window_of(lo_ref, block, before, group)
        query = heads_side_by_side(qt_ref, block, group)

        def step(keys_ref, values_ref, offset, number, carry):
            peak, total, acc = carry
            start = pl.multiple_of(number * BLOCK, BLOCK)
            scores = mm(keys_ref[0, pl.ds(start, BLOCK), :], query)
            scores = jnp.where(block_mask(lo, hi, offset + start, lanes), scores, masked_value)
            top = jnp.maximum(peak, jnp.max(scores, axis=0, keepdims=True))
            weights = jnp.exp(scores - top)
            fade = jnp.exp(peak - top)
            total = total * fade + jnp.sum(weights, axis=0, keepdims=True)
            acc = acc * fade + mm(values_ref[:, pl.ds(start, BLOCK)], weights.astype(bf16))
            return (top, total, acc)

        first = first_ref[block]
        carry = (
            jnp.full((1, lanes), masked_value, f32),
            jnp.zeros((1, lanes), f32),
            jnp.zeros((HEAD_DIM, lanes), f32),
        )
        carry = lax.fori_loop(
            first, passed, functools.partial(step, old_k_ref, old_vt_ref, 0), carry
        )
        peak, total, acc = lax.fori_loop(
            jnp.maximum(first - passed, 0),
            block + 1,
            functools.partial(step, k_ref, vt_ref, before),
            carry,
        )
        result = (acc / total).astype(bf16)
        logs = peak + jnp.log(total)
        cut = pl.ds(block * BLOCK, BLOCK)
        for h in range(group):
            side = slice(h * BLOCK, (h + 1) * BLOCK)
            out_ref[h * HEAD_DIM : (h + 1) * HEAD_DIM, cut] = result[:, side]
            log_ref[0, h : h + 1, cut] = logs[:, side]


def attend(first, lo, q_t, k, v_t, old_k, old_v_t, group):
    pair_heads, rows, _ = k.shape
    before = old_k.shape[1]
    tall = group * HEAD_DIM
    by_head = lambda h, s: (h, 0, 0)
    return pl.pallas_call(
        functools.partial(attend_kernel, group),
        grid_spec=pltpu.PrefetchScalarGridSpec(
            num_scalar_prefetch=1,
            grid=(pair_heads,),
            in_specs=[
                pl.BlockSpec((1, rows), lambda h, s: (0, 0)),
                pl.BlockSpec((tall, rows), lambda h, s: (h, 0)),
                pl.BlockSpec((1, rows, HEAD_DIM), by_head),
                pl.BlockSpec((HEAD_DIM, rows), lambda h, s: (h, 0)),
                pl.BlockSpec((1, before, HEAD_DIM), by_head),
                pl.BlockSpec((HEAD_DIM, before), lambda h, s: (h, 0)),
            ],
            out_specs=[
                pl.BlockSpec((tall, rows), lambda h, s: (h, 0)),
                pl.BlockSpec((1, group, rows), by_head),
            ],
        ),
        out_shape=[
            jax.ShapeDtypeStruct((pair_heads * tall, rows), bf16),
            jax.ShapeDtypeStruct((pair_heads, group, rows), f32),
        ],
        compiler_params=pltpu.CompilerParams(vmem_limit_bytes=vmem_bytes),
        cost_estimate=pl.CostEstimate(
            flops=pair_heads * group * rows * (rows + before) * 512,
            bytes_accessed=8 * 1024 * 1024,
            transcendentals=pair_heads * group * rows * (rows + before),
        ),
        name="attend",
    )(first, lo, q_t, k, v_t, old_k, old_v_t)


def attend_back_kernel(
    group, earlier, before,
    first_ref, lo_ref, log_ref, spread_ref, qt_ref, dt_ref, q_ref, d_ref, k_ref, kt_ref, v_ref,
    sum_ref, dq_ref, dk_ref, dv_ref, pair_ref,
):
    lanes = group * BLOCK
    passed = before // BLOCK
    pair_ref[...] = jnp.zeros_like(pair_ref)
    for block in range(qt_ref.shape[1] // BLOCK):
        cut = pl.ds(block * BLOCK, BLOCK)
        lo, hi = window_of(lo_ref, block, before, group)
        query = heads_side_by_side(qt_ref, block, group)
        upstream = heads_side_by_side(dt_ref, block, group)
        query_rows = heads_one_above(q_ref, block, group)
        upstream_rows = heads_one_above(d_ref, block, group)
        nothing = jnp.zeros_like(query_rows)
        both_rows = jnp.concatenate(
            [
                jnp.concatenate([query_rows, nothing], axis=1),
                jnp.concatenate([nothing, upstream_rows], axis=1),
            ],
            axis=0,
        )
        logs = jnp.concatenate([log_ref[0, h : h + 1, cut] for h in range(group)], axis=1)
        spread = jnp.concatenate([spread_ref[0, h : h + 1, cut] for h in range(group)], axis=1)

        def step(number, acc):
            start = pl.multiple_of(number * BLOCK, BLOCK)
            here = pl.ds(start, BLOCK)
            scores = mm(k_ref[0, here, :], query)
            mask = block_mask(lo, hi, start + (0 if earlier else before), lanes)
            probs = jnp.exp(jnp.where(mask, scores - logs, masked_value))
            change = mm(v_ref[0, here, :], upstream)
            scores_change = (probs * (change - spread)).astype(bf16)
            pair_ref[here, :] += mm(
                jnp.concatenate([scores_change, probs.astype(bf16)], axis=1), both_rows
            )
            return acc + mm(kt_ref[:, here], scores_change)

        first = first_ref[block]
        bounds = (first, passed) if earlier else (jnp.maximum(first - passed, 0), block + 1)
        acc = lax.fori_loop(*bounds, step, jnp.zeros((HEAD_DIM, lanes), f32))
        for h in range(group):
            side = slice(h * HEAD_DIM, (h + 1) * HEAD_DIM)
            dq_ref[side, cut] = sum_ref[side, cut] + (
                acc[:, h * BLOCK : (h + 1) * BLOCK] * score_scale
            )
    pair_t = pair_ref[...].T
    dk_ref[...] = pair_t[:HEAD_DIM].astype(dk_ref.dtype)
    dv_ref[...] = pair_t[HEAD_DIM:].astype(dv_ref.dtype)


def attend_back(
    first, lo, logs, spread, q_t, d_t, q_rows, d_rows, k, k_t, v, dq_sum, before, earlier
):
    pair_heads, keys, _ = k.shape
    group, rows = q_rows.shape[1:3]
    tall = group * HEAD_DIM
    by_head = lambda h, s: (h, 0, 0)
    flat = lambda h, s: (h, 0)
    pair_type = bf16 if earlier else f32
    return pl.pallas_call(
        functools.partial(attend_back_kernel, group, earlier, before),
        grid_spec=pltpu.PrefetchScalarGridSpec(
            num_scalar_prefetch=1,
            grid=(pair_heads,),
            in_specs=[
                pl.BlockSpec((1, rows), lambda h, s: (0, 0)),
                pl.BlockSpec((1, group, rows), by_head),
                pl.BlockSpec((1, group, rows), by_head),
                pl.BlockSpec((tall, rows), flat),
                pl.BlockSpec((tall, rows), flat),
                pl.BlockSpec((1, group, rows, HEAD_DIM), lambda h, s: (h, 0, 0, 0)),
                pl.BlockSpec((1, group, rows, HEAD_DIM), lambda h, s: (h, 0, 0, 0)),
                pl.BlockSpec((1, keys, HEAD_DIM), by_head),
                pl.BlockSpec((HEAD_DIM, keys), flat),
                pl.BlockSpec((1, keys, HEAD_DIM), by_head),
                pl.BlockSpec((tall, rows), flat),
            ],
            out_specs=[
                pl.BlockSpec((tall, rows), flat),
                pl.BlockSpec((HEAD_DIM, keys), flat),
                pl.BlockSpec((HEAD_DIM, keys), flat),
            ],
            scratch_shapes=[pltpu.VMEM((keys, 2 * HEAD_DIM), f32)],
        ),
        out_shape=[
            jax.ShapeDtypeStruct((pair_heads * tall, rows), f32),
            jax.ShapeDtypeStruct((pair_heads * HEAD_DIM, keys), pair_type),
            jax.ShapeDtypeStruct((pair_heads * HEAD_DIM, keys), pair_type),
        ],
        compiler_params=pltpu.CompilerParams(vmem_limit_bytes=vmem_bytes),
        cost_estimate=pl.CostEstimate(
            flops=pair_heads * group * rows * keys * 1280,
            bytes_accessed=10 * 1024 * 1024,
            transcendentals=pair_heads * group * rows * keys,
        ),
        name="attend_back",
    )(first, lo, logs, spread, q_t, d_t, q_rows, d_rows, k, k_t, v, dq_sum)


def turn(tall, cosine, sine):
    half = HEAD_DIM // 2
    parts = []
    for start in range(0, tall.shape[0], HEAD_DIM):
        a, b = tall[start : start + half], tall[start + half : start + HEAD_DIM]
        parts += [a * cosine - b * sine, b * cosine + a * sine]
    return jnp.concatenate(parts, axis=0)


def put_heads(ref, rows_of_heads):
    for h in range(ref.shape[0]):
        ref[h] = rows_of_heads[:, h * HEAD_DIM : (h + 1) * HEAD_DIM]


def project_kernel(
    x_ref, gain_ref, cos_ref, sin_ref, wq_ref, wk_ref, wv_ref,
    normed_ref, qt_ref, q_ref, kt_ref, k_ref, vt_ref, v_ref,
):
    x = x_ref[...].astype(f32)
    normed = (x * scale_of(x) * gain_ref[...].astype(f32)).astype(bf16)
    normed_ref[...] = normed
    cosine, sine = cos_ref[...], sin_ref[...]
    q_t = turn(mm(normed, wq_ref[...]).T, cosine, sine).astype(bf16).astype(f32) * score_scale
    qt_ref[...] = q_t.astype(bf16)
    put_heads(q_ref, q_t.T.astype(bf16))
    k_t = turn(dot(wk_ref[...], normed, 1, 1), cosine, sine)
    kt_ref[...] = k_t.astype(bf16)
    put_heads(k_ref, k_t.T.astype(bf16))
    v_t = dot(wv_ref[...], normed, 1, 1)
    vt_ref[...] = v_t.astype(bf16)
    put_heads(v_ref, v_t.T.astype(bf16))


def project(tokens, gain, cosine, sine, w_query, w_key, w_value):
    rows, width = tokens.shape
    tall, split = w_query.shape[1], w_key.shape[0]
    heads, pair_heads = tall // HEAD_DIM, split // HEAD_DIM
    whole = lambda shape: pl.BlockSpec(shape, lambda t: (0,) * len(shape))
    down = lambda wide: pl.BlockSpec((BLOCK, wide), lambda t: (t, 0))
    across = lambda high: pl.BlockSpec((high, BLOCK), lambda t: (0, t))
    stacked = lambda count: pl.BlockSpec((count, BLOCK, HEAD_DIM), lambda t: (0, t, 0))
    return pl.pallas_call(
        project_kernel,
        grid=(rows // BLOCK,),
        in_specs=[
            down(width), whole((1, width)), across(HEAD_DIM // 2), across(HEAD_DIM // 2),
            whole((width, tall)), whole((split, width)), whole((split, width)),
        ],
        out_specs=[
            down(width), across(tall), stacked(heads), across(split), stacked(pair_heads),
            across(split), stacked(pair_heads),
        ],
        out_shape=[
            jax.ShapeDtypeStruct((rows, width), bf16),
            jax.ShapeDtypeStruct((tall, rows), bf16),
            jax.ShapeDtypeStruct((heads, rows, HEAD_DIM), bf16),
            jax.ShapeDtypeStruct((split, rows), bf16),
            jax.ShapeDtypeStruct((pair_heads, rows, HEAD_DIM), bf16),
            jax.ShapeDtypeStruct((split, rows), bf16),
            jax.ShapeDtypeStruct((pair_heads, rows, HEAD_DIM), bf16),
        ],
        compiler_params=pltpu.CompilerParams(vmem_limit_bytes=vmem_bytes),
        cost_estimate=pl.CostEstimate(
            flops=2 * rows * width * (tall + 2 * split),
            bytes_accessed=12 * 1024 * 1024,
            transcendentals=0,
        ),
        name="project",
    )(tokens, gain, cosine, sine, w_query, w_key, w_value)


def enter_mixture_kernel(count, x_ref, gain_ref, router_ref, routes_ref, *refs):
    pieces, (hidden_ref, normed_ref, normed_t_ref, gates_ref) = refs[: 2 * count], refs[2 * count :]
    projected = 0.0
    for context_ref, w_ref in zip(pieces[:count], pieces[count:]):
        projected = projected + mm(context_ref[...].astype(f32).T.astype(bf16), w_ref[...])
    hidden = x_ref[...].astype(f32) + residual_scale * projected
    hidden_ref[...] = hidden
    normed = hidden * scale_of(hidden) * gain_ref[...].astype(f32)
    normed_t_ref[...] = normed.T.astype(bf16)
    normed = normed.astype(bf16)
    normed_ref[...] = normed
    logits = dot(router_ref[...], normed, 1, 1)
    expert = lax.broadcasted_iota(jnp.int32, logits.shape, 0)
    chosen = expert == routes_ref[0:1, :]
    for k in range(1, routes_ref.shape[0]):
        chosen = chosen | (expert == routes_ref[k : k + 1, :])
    logits = jnp.where(chosen, logits, masked_value)
    weights = jnp.exp(logits - jnp.max(logits, axis=0, keepdims=True))
    weights = jnp.where(chosen, weights, 0.0)
    gates_ref[...] = weights / jnp.sum(weights, axis=0, keepdims=True)


def enter_mixture(tokens, gain, router_t, routes_t, contexts, weights):
    rows, width = tokens.shape
    whole = lambda shape: pl.BlockSpec(shape, lambda t: (0,) * len(shape))
    down = lambda wide: pl.BlockSpec((BLOCK, wide), lambda t: (t, 0))
    across = lambda high: pl.BlockSpec((high, BLOCK), lambda t: (0, t))
    return pl.pallas_call(
        functools.partial(enter_mixture_kernel, len(contexts)),
        grid=(rows // BLOCK,),
        in_specs=[
            down(width), whole((1, width)), whole(router_t.shape), across(routes_t.shape[0]),
            *[across(context.shape[0]) for context in contexts],
            *[whole(weight.shape) for weight in weights],
        ],
        out_specs=[down(width), down(width), across(width), across(EXPERTS)],
        out_shape=[
            jax.ShapeDtypeStruct((rows, width), f32),
            jax.ShapeDtypeStruct((rows, width), bf16),
            jax.ShapeDtypeStruct((width, rows), bf16),
            jax.ShapeDtypeStruct((EXPERTS, rows), f32),
        ],
        compiler_params=pltpu.CompilerParams(vmem_limit_bytes=vmem_bytes),
        cost_estimate=pl.CostEstimate(
            flops=2 * rows * width * width, bytes_accessed=16 * 1024 * 1024, transcendentals=0
        ),
        name="enter_mixture",
    )(tokens, gain, router_t, routes_t, *contexts, *weights)


def enter_back_kernel(c_ref, own_ref, other_ref, wo_ref, ctx_ref, hidden_ref, dt_ref, d_ref, spread_ref, wo_grad_ref):
    hidden_gradient = c_ref[...].astype(f32) + (
        own_ref[...].astype(f32) + other_ref[...].astype(f32)
    )
    hidden_ref[...] = hidden_gradient
    attention_gradient = (residual_scale * hidden_gradient).astype(bf16)
    d_t = dot(wo_ref[...], attention_gradient, 1, 1)
    dt_ref[...] = d_t.astype(bf16)
    put_heads(d_ref, d_t.T.astype(bf16))
    context_t = ctx_ref[...]
    weighed = d_t.astype(bf16).astype(f32) * context_t.astype(f32)
    for h in range(spread_ref.shape[0]):
        spread_ref[h : h + 1, :] = jnp.sum(
            weighed[h * HEAD_DIM : (h + 1) * HEAD_DIM], axis=0, keepdims=True
        )

    @pl.when(pl.program_id(0) == 0)
    def start():
        wo_grad_ref[...] = jnp.zeros_like(wo_grad_ref)

    wo_grad_ref[...] += mm(context_t, attention_gradient)


def enter_back(cotangent, own, other, w_out, context_t):
    rows, width = cotangent.shape
    tall = w_out.shape[0]
    heads = tall // HEAD_DIM
    whole = lambda shape: pl.BlockSpec(shape, lambda t: (0,) * len(shape))
    down = lambda wide: pl.BlockSpec((BLOCK, wide), lambda t: (t, 0))
    across = lambda high: pl.BlockSpec((high, BLOCK), lambda t: (0, t))
    return pl.pallas_call(
        enter_back_kernel,
        grid=(rows // BLOCK,),
        in_specs=[down(width), down(width), down(width), whole((tall, width)), across(tall)],
        out_specs=[
            down(width), across(tall),
            pl.BlockSpec((heads, BLOCK, HEAD_DIM), lambda t: (0, t, 0)),
            across(heads), whole((tall, width)),
        ],
        out_shape=[
            jax.ShapeDtypeStruct((rows, width), f32),
            jax.ShapeDtypeStruct((tall, rows), bf16),
            jax.ShapeDtypeStruct((heads, rows, HEAD_DIM), bf16),
            jax.ShapeDtypeStruct((heads, rows), f32),
            jax.ShapeDtypeStruct((tall, width), f32),
        ],
        compiler_params=pltpu.CompilerParams(vmem_limit_bytes=vmem_bytes),
        cost_estimate=pl.CostEstimate(
            flops=4 * rows * width * tall, bytes_accessed=20 * 1024 * 1024, transcendentals=0
        ),
        name="enter_back",
    )(cotangent, own, other, w_out, context_t)


def leave_back_kernel(
    x_ref, gain_ref, cos_ref, sin_ref, wq_ref, wk_ref, wv_ref, normed_ref,
    dq_ref, dk_ref, dv_ref, more_dk_ref, more_dv_ref,
    part_ref, gain_grad_ref, w_grad_ref, w_sum_ref,
):
    step = pl.program_id(0)
    cosine, sine = cos_ref[...], -sin_ref[...]
    dq_t = turn(dq_ref[...], cosine, sine).astype(bf16)
    dk_t = turn(dk_ref[...] + more_dk_ref[...].astype(f32), cosine, sine).astype(bf16)
    dv_t = (dv_ref[...] + more_dv_ref[...].astype(f32)).astype(bf16)
    normed = normed_ref[...]

    @pl.when(step == 0)
    def start():
        w_sum_ref[...] = jnp.zeros_like(w_sum_ref)
        gain_grad_ref[...] = jnp.zeros_like(gain_grad_ref)

    w_sum_ref[...] += mm(jnp.concatenate([dq_t, dk_t, dv_t], axis=0), normed)
    rows_of = lambda tall: tall.astype(f32).T.astype(bf16)
    upstream = (
        dot(rows_of(dq_t), wq_ref[...], 1, 1)
        + mm(rows_of(dk_t), wk_ref[...])
        + mm(rows_of(dv_t), wv_ref[...])
    )
    x = x_ref[...].astype(f32)
    part, gain_part = norm_back(x, scale_of(x), gain_ref[...].astype(f32), upstream)
    part_ref[...] = part.astype(bf16)
    gain_grad_ref[...] += gain_part[None, :]

    @pl.when(step == pl.num_programs(0) - 1)
    def finish():
        w_grad_ref[...] = w_sum_ref[...].astype(bf16)


def leave_back(
    tokens, gain, cosine, sine, w_query, w_key, w_value, normed, dq_t, dk_t, dv_t, more_dk, more_dv
):
    rows, width = tokens.shape
    tall, split = w_query.shape[1], w_key.shape[0]
    whole = lambda shape: pl.BlockSpec(shape, lambda t: (0,) * len(shape))
    down = lambda wide: pl.BlockSpec((BLOCK, wide), lambda t: (t, 0))
    across = lambda high: pl.BlockSpec((high, BLOCK), lambda t: (0, t))
    return pl.pallas_call(
        leave_back_kernel,
        grid=(rows // BLOCK,),
        in_specs=[
            down(width), whole((1, width)), across(HEAD_DIM // 2), across(HEAD_DIM // 2),
            whole((width, tall)), whole((split, width)), whole((split, width)), down(width),
            across(tall), across(split), across(split), across(split), across(split),
        ],
        out_specs=[
            down(width), whole((1, width)), whole((tall + 2 * split, width)),
        ],
        out_shape=[
            jax.ShapeDtypeStruct((rows, width), bf16),
            jax.ShapeDtypeStruct((1, width), f32),
            jax.ShapeDtypeStruct((tall + 2 * split, width), bf16),
        ],
        scratch_shapes=[pltpu.VMEM((tall + 2 * split, width), f32)],
        compiler_params=pltpu.CompilerParams(vmem_limit_bytes=vmem_bytes),
        cost_estimate=pl.CostEstimate(
            flops=4 * rows * width * (tall + 2 * split),
            bytes_accessed=20 * 1024 * 1024,
            transcendentals=0,
        ),
        name="leave_back",
    )(
        tokens, gain, cosine, sine, w_query, w_key, w_value, normed, dq_t, dk_t, dv_t, more_dk,
        more_dv,
    )


def expert_kernel(
    adds, ids_ref, gates_ref, xt_ref, x_ref, ct_ref, c_ref, up_ref, down_ref, *refs
):
    if adds:
        more_ref, *refs = refs
    _, _, _, grad_ref, up_grad_ref, act_ref, gate_grad_ref = refs
    rows = x_ref.shape[0]
    chunk = min(BLOCK, rows)
    for part in range(rows // chunk):
        cut = pl.ds(part * chunk, chunk)
        xt = xt_ref[:, cut]
        gate = mm(up_ref[0, 0], xt)
        up = mm(up_ref[0, 1], xt)
        active_grad = mm(down_ref[0], ct_ref[:, cut])
        share = 1.0 / (1.0 + jnp.exp(-gate))
        silu = gate * share
        active = silu * up
        weight = gates_ref[0, :, cut] * residual_scale
        gate_grad_ref[0, :, cut] = residual_scale * jnp.sum(
            active * active_grad, axis=0, keepdims=True
        )
        active_grad = active_grad * weight
        act_ref[0, :, cut] = (active * weight).astype(bf16)
        up_grad_ref[0, 0, :, cut] = (
            active_grad * up * (share + silu * (1.0 - share))
        ).astype(bf16)
        up_grad_ref[0, 1, :, cut] = (active_grad * silu).astype(bf16)

    def put(place, total):
        if adds:
            total = total + more_ref[0, place].astype(f32)
        grad_ref[0, place] = total.astype(bf16)

    x = x_ref[...]
    put(0, mm(up_grad_ref[0, 0], x))
    put(1, mm(up_grad_ref[0, 1], x))
    put(2, mm(act_ref[0], c_ref[...]))


def expert_step(ids, gates, xt, x, ct, c, w_up, w_down, more, old):
    count = ids.shape[0]
    rows, width = x.shape
    units = w_down.shape[1]
    whole = lambda shape: pl.BlockSpec(shape, lambda e, s: (0,) * len(shape))
    fresh = old is None
    adds = more is not None
    each = pl.BlockSpec((1, 3, units, width), lambda e, s: (e, 0, 0, 0))
    if fresh:
        old = (jnp.zeros((8, 128), f32),) * 3
    return pl.pallas_call(
        functools.partial(expert_kernel, adds),
        grid_spec=pltpu.PrefetchScalarGridSpec(
            num_scalar_prefetch=1,
            grid=(count,),
            in_specs=[
                pl.BlockSpec((1, 1, rows), lambda e, s: (s[e], 0, 0)),
                whole((width, rows)),
                whole((rows, width)),
                whole((width, rows)),
                whole((rows, width)),
                pl.BlockSpec((1, 2, units, width), lambda e, s: (s[e], 0, 0, 0)),
                pl.BlockSpec((1, units, width), lambda e, s: (s[e], 0, 0)),
                *([each] if adds else []),
                pl.BlockSpec(memory_space=pl.ANY),
                pl.BlockSpec(memory_space=pl.ANY),
                pl.BlockSpec(memory_space=pl.ANY),
            ],
            out_specs=[
                each,
                pl.BlockSpec((1, 2, units, rows), lambda e, s: (s[e], 0, 0, 0)),
                pl.BlockSpec((1, units, rows), lambda e, s: (s[e], 0, 0)),
                pl.BlockSpec((1, 1, rows), lambda e, s: (s[e], 0, 0)),
            ],
        ),
        out_shape=[
            jax.ShapeDtypeStruct((count, 3, units, width), bf16),
            jax.ShapeDtypeStruct((EXPERTS, 2, units, rows), bf16),
            jax.ShapeDtypeStruct((EXPERTS, units, rows), bf16),
            jax.ShapeDtypeStruct((EXPERTS, 1, rows), f32),
        ],
        input_output_aliases={} if fresh else {8 + adds: 1, 9 + adds: 2, 10 + adds: 3},
        compiler_params=pltpu.CompilerParams(vmem_limit_bytes=vmem_bytes),
        cost_estimate=pl.CostEstimate(
            flops=count * 12 * rows * width * units,
            bytes_accessed=count * units * width * 12 + 8 * rows * width,
            transcendentals=count * units * rows,
        ),
        name="experts",
    )(ids, gates, xt, x, ct, c, w_up, w_down, *([more] if adds else []), *old)


def from_other_half(shard):
    return lax.ppermute(shard, "tensor", [(0, 1), (1, 0)])


def gathered(shard):
    if lax.axis_size("tensor") != 2:
        return [lax.all_gather(shard, "tensor", axis=0, tiled=True)]
    return [shard, from_other_half(shard)]


def both_parts(part):
    if lax.axis_size("tensor") != 2:
        return lax.psum(part, "tensor"), jnp.zeros_like(part)
    return part, from_other_half(part)


def summed_parts(part):
    low = part.astype(bf16)
    if lax.axis_size("tensor") != 2:
        return lax.psum(low, "tensor").astype(f32)
    return low.astype(f32) + from_other_half(low).astype(f32)


def chip_order(chips):
    there = [2 * z for z in range(chips // 2)]
    return there + [chip + 1 for chip in reversed(there)]


def chunk_experts(device, peers, number):
    order = jnp.array(chip_order(peers // 2), jnp.int32)
    each = EXPERTS // peers
    core = device % 2

    def owned(side):
        chips = jnp.where(side == 0, order, order[::-1])
        return (2 * chips + side) * each + number

    return owned(1 - core).astype(jnp.int32), owned(core).astype(jnp.int32)


def chip_rings():
    order = chip_order(lax.axis_size("dp") // 2)
    return [[2 * chip for chip in order], [2 * chip + 1 for chip in reversed(order)]]


def to_owner(chip_sum):
    return lax.psum_scatter(
        chip_sum, "dp", scatter_dimension=0, axis_index_groups=chip_rings(), tiled=True
    )


def summed_over_tokens(part):
    swap = [(i, i ^ 1) for i in range(lax.axis_size("dp"))]
    is_first = lax.axis_index("dp") % 2 == 0
    low, high = jnp.split(part, 2, axis=0)
    received = lax.ppermute(jnp.where(is_first, high, low), "dp", swap)
    half = (jnp.where(is_first, low, high).astype(f32) + received.astype(f32)).astype(bf16)
    half = lax.psum(half, "dp", axis_index_groups=chip_rings())
    other = lax.ppermute(half, "dp", swap)
    return jnp.concatenate(
        [jnp.where(is_first, half, other), jnp.where(is_first, other, half)], axis=0
    )


def angles(position):
    inverse = rope_base ** (-2.0 * jnp.arange(HEAD_DIM // 2, dtype=f32) / HEAD_DIM)
    angle = inverse[:, None] * position.astype(f32)[None, :]
    return jnp.cos(angle), jnp.sin(angle)


def scale_of(values):
    return lax.rsqrt(jnp.mean(values * values, axis=-1, keepdims=True) + epsilon)


def norm_back(values, scale, gain, upstream):
    pulled = gain * upstream
    slope = jnp.mean(pulled * values, axis=-1, keepdims=True)
    return (
        scale * pulled - values * (scale * scale * scale * slope),
        jnp.sum(upstream * values * scale, axis=0),
    )


def on_device(
    tokens, doc_ids, routes, attention_gain, w_query, w_key, w_value, w_out, mixture_gain,
    w_router, expert_gate_up, expert_down, out_cotangent,
):
    rows, width = tokens.shape
    peers = lax.axis_size("dp")
    device = lax.axis_index("dp")
    pair_heads = w_key.shape[0] // HEAD_DIM
    group = w_query.shape[1] // w_key.shape[0]
    first = device * rows
    chunks = EXPERTS // peers
    w_out_parts = gathered(w_out)

    docs = lax.dynamic_slice_in_dim(doc_ids, first, rows)
    docs_before = lax.dynamic_slice_in_dim(doc_ids, jnp.maximum(device - 1, 0) * rows, rows)
    docs_before = jnp.where(device > 0, docs_before, -1)
    docs_window = jnp.concatenate([docs_before, docs])
    lo = jnp.sum((docs_window[:, None] < docs[None, :]).astype(jnp.int32), axis=0)
    first_block = lo[::BLOCK] // BLOCK
    lo = lo[None, :]

    position = (first + jnp.arange(rows, dtype=jnp.int32)) % SEQ_LEN
    cosine, sine = angles(position)
    gain_one = attention_gain[None, :]
    normed_attention, q_t, q_rows, k_t, k_rows, v_t, v_rows = project(
        tokens, gain_one, cosine, sine, w_query, w_key, w_value
    )
    to_next = [(i, i + 1) for i in range(0, peers, 2)]
    before = SEQ_LEN - rows
    old_k_t = lax.ppermute(k_t, "dp", to_next)
    old_v_t = lax.ppermute(v_t, "dp", to_next)
    across = lambda tall: jnp.swapaxes(tall.reshape(pair_heads, HEAD_DIM, before), 1, 2)
    old_k_rows, old_v_rows = across(old_k_t), across(old_v_t)

    context_t, logs = attend(first_block, lo, q_t, k_rows, v_t, old_k_rows, old_v_t, group)
    hidden, normed_mixture, normed_t, gates = enter_mixture(
        tokens, mixture_gain[None, :], w_router.T, routes.T, gathered(context_t), w_out_parts
    )
    gain_two = mixture_gain.astype(f32)
    scale_two = scale_of(hidden)

    upstream_t = out_cotangent.T
    swap_cores = [(i, i ^ 1) for i in range(peers)]
    shares, old = [], None

    def run_experts(ids):
        return expert_step(
            ids, gates[:, None, :], normed_t, normed_mixture, upstream_t, out_cotangent,
            expert_gate_up, expert_down, None, old,
        )

    for number in range(chunks):
        other_ids, own_ids = chunk_experts(device, peers, number)
        send, *old = run_experts(other_ids)
        received = lax.ppermute(send, "dp", swap_cores)
        keep, *old = run_experts(own_ids)
        if number < chunks - 1:
            chip_sum = (keep.astype(f32) + received.astype(f32)).astype(bf16)
            chip_sum, *old = lax.optimization_barrier((chip_sum, *old))
            shares.append(to_owner(chip_sum))
    up_grad, act, gates_gradient = old
    gates_gradient = gates_gradient[:, 0]
    units = expert_down.shape[1]
    wide = EXPERTS * units

    logits_gradient = gates * (
        gates_gradient - jnp.sum(gates * gates_gradient, axis=0, keepdims=True)
    )
    logits_low = logits_gradient.astype(bf16)
    router_gradient = mm(logits_low, normed_mixture)
    up_grad = up_grad.reshape(2 * wide, rows)
    w_up = expert_gate_up.reshape(2 * wide, width)
    own_parts, other_parts, gain_parts = [], [], []
    for start in range(0, rows, rows // 2):
        cut = slice(start, start + rows // 2)
        if start > 0:
            up_grad, own_parts[0] = lax.optimization_barrier((up_grad, own_parts[0]))
        normed_gradient = dot(up_grad[:, cut], w_up, 0, 0) + dot(logits_low[:, cut], w_router, 0, 1)
        part, gain_part = norm_back(hidden[cut], scale_two[cut], gain_two, normed_gradient)
        part = part.astype(bf16)
        if start > 0:
            part, act, keep, received, other_parts[0] = lax.optimization_barrier(
                (part, act, keep, received, other_parts[0])
            )
        own, other = both_parts(part)
        own_parts.append(own)
        other_parts.append(other)
        gain_parts.append(gain_part)
    second_gain_part = gain_parts[0] + gain_parts[1]
    chip_sum = (keep.astype(f32) + received.astype(f32)).astype(bf16)
    shares.append(to_owner(chip_sum))

    mixture_part = dot(act.reshape(wide, rows), expert_down.reshape(wide, width), 0, 0)
    mixture_low = mixture_part.astype(bf16)
    own_part = jnp.concatenate(own_parts, axis=0)
    other_part = jnp.concatenate(other_parts, axis=0)
    own_part, other_part, mixture_low = lax.optimization_barrier(
        (own_part, other_part, mixture_low)
    )
    mixed = (hidden + summed_parts(mixture_low)).astype(bf16)

    hidden_gradient, d_t, d_rows, spread, w_out_gradient = enter_back(
        out_cotangent, own_part, other_part, w_out, context_t
    )
    by_group = lambda rows_of_heads: rows_of_heads.reshape(pair_heads, group, rows, HEAD_DIM)
    back = functools.partial(
        attend_back, first_block, lo, logs, spread.reshape(pair_heads, group, rows), q_t, d_t,
        by_group(q_rows), by_group(d_rows),
    )
    dq_t, old_dk, old_dv = back(
        old_k_rows, old_k_t, old_v_rows, jnp.zeros((q_t.shape[0], rows), f32), before, True
    )
    to_previous = [(i + 1, i) for i in range(0, peers, 2)]
    more_dk = lax.ppermute(old_dk, "dp", to_previous)
    more_dv = lax.ppermute(old_dv, "dp", to_previous)
    dq_t, dk_t, dv_t = back(k_rows, k_t, v_rows, dq_t, before, False)
    dq_t, mixed = lax.optimization_barrier((dq_t, mixed))
    if chunks > 1:
        dq_t, shares[0] = lax.optimization_barrier((dq_t, shares[0]))
    input_part, first_gain_part, w_gradients = leave_back(
        tokens, gain_one, cosine, sine, w_query, w_key, w_value, normed_attention, dq_t, dk_t, dv_t,
        more_dk, more_dv,
    )
    tokens_gradient = (hidden_gradient + summed_parts(input_part)).astype(bf16)
    small = jnp.concatenate([router_gradient, second_gain_part[None, :], first_gain_part], axis=0)
    small = summed_parts(small).astype(bf16)
    tall, split = w_query.shape[1], w_key.shape[0]
    ends = [tall, tall + split, tall + 2 * split, 2 * tall + 2 * split, 2 * tall + 2 * split + EXPERTS]
    filler = jnp.zeros((-(ends[-1] + 2) % 64, width), bf16)
    gradients = jnp.concatenate([w_gradients, w_out_gradient.astype(bf16), small, filler], axis=0)
    shares[-1], gradients, tokens_gradient = lax.optimization_barrier(
        (shares[-1], gradients, tokens_gradient)
    )
    gradients = summed_over_tokens(gradients).astype(f32)
    w_q, w_k, w_v, w_o, router, gains = jnp.split(gradients, ends, axis=0)
    experts_gradient = jnp.concatenate(shares, axis=0).astype(f32)
    return (
        mixed, tokens_gradient, gains[1], w_q.T, w_k, w_v, w_o, gains[0], router.T,
        experts_gradient[:, :2], experts_gradient[:, 2],
    )


def solution(mesh):
    placed = (
        P("dp", None),
        P(),
        P("dp", None),
        P(),
        P(None, "tensor"),
        P("tensor", None),
        P("tensor", None),
        P("tensor", None),
        P(),
        P(),
        P(None, None, "tensor", None),
        P(None, "tensor", None),
        P("dp", None),
    )
    return jax.shard_map(
        on_device,
        mesh=mesh,
        in_specs=placed,
        out_specs=(
            P("dp", None),
            P("dp", None),
            P(),
            P(None, "tensor"),
            P("tensor", None),
            P("tensor", None),
            P("tensor", None),
            P(),
            P(),
            P("dp", None, "tensor", None),
            P("dp", "tensor", None),
        ),
        check_vma=False,
    )
```

```python
import functools

import jax
import jax.numpy as jnp
from jax import lax
from jax.experimental import pallas as pl
from jax.experimental.pallas import tpu as pltpu
from jax.sharding import PartitionSpec as P

HEAD_DIM = 64
EXPERTS = 32
SEQ_LEN = 2048
BLOCK = 256

epsilon = 1e-06
score_scale = 0.015625
residual_scale = 0.22
rope_base = 10000.0
masked_value = -1e30
vmem_bytes = 24 * 1024 * 1024
expert_vmem_bytes = 40 * 1024 * 1024
f32 = jnp.float32
bf16 = jnp.bfloat16


def dot(left, right, left_dim, right_dim):
    return lax.dot_general(
        left, right, (((left_dim,), (right_dim,)), ((), ())), preferred_element_type=f32
    )


def mm(left, right):
    return jnp.dot(left, right, preferred_element_type=f32)


def block_mask(lo, hi, start, lanes):
    place = start + lax.broadcasted_iota(jnp.int32, (BLOCK, lanes), 0)
    return (place >= lo) & (place <= hi)


def window_of(lo_ref, block, before, group):
    cut = pl.ds(block * BLOCK, BLOCK)
    lo = lo_ref[:, cut]
    hi = before + block * BLOCK + lax.broadcasted_iota(jnp.int32, (1, BLOCK), 1)
    return (
        jnp.concatenate([lo] * group, axis=1),
        jnp.concatenate([hi] * group, axis=1),
    )


def heads_side_by_side(ref, block, group):
    cut = pl.ds(block * BLOCK, BLOCK)
    return jnp.concatenate(
        [ref[h * HEAD_DIM : (h + 1) * HEAD_DIM, cut] for h in range(group)], axis=1
    )


def heads_one_above(ref, block, group):
    cut = pl.ds(block * BLOCK, BLOCK)
    return jnp.concatenate([ref[0, h, cut, :] for h in range(group)], axis=0)


def attend_kernel(
    group, first_ref, lo_ref, qt_ref, k_ref, vt_ref, old_k_ref, old_vt_ref, out_ref, log_ref
):
    lanes = group * BLOCK
    before = old_k_ref.shape[1]
    passed = before // BLOCK
    for block in range(qt_ref.shape[1] // BLOCK):
        lo, hi = window_of(lo_ref, block, before, group)
        query = heads_side_by_side(qt_ref, block, group)

        def step(keys_ref, values_ref, offset, number, carry):
            peak, total, acc = carry
            start = pl.multiple_of(number * BLOCK, BLOCK)
            scores = mm(keys_ref[0, pl.ds(start, BLOCK), :], query)
            scores = jnp.where(block_mask(lo, hi, offset + start, lanes), scores, masked_value)
            top = jnp.maximum(peak, jnp.max(scores, axis=0, keepdims=True))
            weights = jnp.exp(scores - top)
            fade = jnp.exp(peak - top)
            total = total * fade + jnp.sum(weights, axis=0, keepdims=True)
            acc = acc * fade + mm(values_ref[:, pl.ds(start, BLOCK)], weights.astype(bf16))
            return (top, total, acc)

        first = first_ref[block]
        carry = (
            jnp.full((1, lanes), masked_value, f32),
            jnp.zeros((1, lanes), f32),
            jnp.zeros((HEAD_DIM, lanes), f32),
        )
        carry = lax.fori_loop(
            first, passed, functools.partial(step, old_k_ref, old_vt_ref, 0), carry
        )
        peak, total, acc = lax.fori_loop(
            jnp.maximum(first - passed, 0),
            block + 1,
            functools.partial(step, k_ref, vt_ref, before),
            carry,
        )
        result = (acc / total).astype(bf16)
        logs = peak + jnp.log(total)
        cut = pl.ds(block * BLOCK, BLOCK)
        for h in range(group):
            side = slice(h * BLOCK, (h + 1) * BLOCK)
            out_ref[h * HEAD_DIM : (h + 1) * HEAD_DIM, cut] = result[:, side]
            log_ref[0, h : h + 1, cut] = logs[:, side]


def attend(first, lo, q_t, k, v_t, old_k, old_v_t, group, base, pair_heads):
    rows = k.shape[1]
    before = old_k.shape[1]
    tall = group * HEAD_DIM
    by_head = lambda h, s: (base + h, 0, 0)
    flat = lambda h, s: (base + h, 0)
    return pl.pallas_call(
        functools.partial(attend_kernel, group),
        grid_spec=pltpu.PrefetchScalarGridSpec(
            num_scalar_prefetch=1,
            grid=(pair_heads,),
            in_specs=[
                pl.BlockSpec((1, rows), lambda h, s: (0, 0)),
                pl.BlockSpec((tall, rows), flat),
                pl.BlockSpec((1, rows, HEAD_DIM), by_head),
                pl.BlockSpec((HEAD_DIM, rows), flat),
                pl.BlockSpec((1, before, HEAD_DIM), by_head),
                pl.BlockSpec((HEAD_DIM, before), flat),
            ],
            out_specs=[
                pl.BlockSpec((tall, rows), lambda h, s: (h, 0)),
                pl.BlockSpec((1, group, rows), lambda h, s: (h, 0, 0)),
            ],
        ),
        out_shape=[
            jax.ShapeDtypeStruct((pair_heads * tall, rows), bf16),
            jax.ShapeDtypeStruct((pair_heads, group, rows), f32),
        ],
        compiler_params=pltpu.CompilerParams(vmem_limit_bytes=vmem_bytes),
        cost_estimate=pl.CostEstimate(
            flops=pair_heads * group * rows * (rows + before) * 512,
            bytes_accessed=8 * 1024 * 1024,
            transcendentals=pair_heads * group * rows * (rows + before),
        ),
        name="attend",
    )(first, lo, q_t, k, v_t, old_k, old_v_t)


def attend_back_kernel(
    group,
    first_ref, lo_ref, log_ref, spread_ref, qt_ref, dt_ref, q_ref, d_ref, k_ref, kt_ref, v_ref,
    old_k_ref, old_kt_ref, old_v_ref,
    dq_ref, dk_ref, dv_ref, old_dk_ref, old_dv_ref, pair_ref, old_pair_ref,
):
    lanes = group * BLOCK
    before = old_k_ref.shape[1]
    passed = before // BLOCK
    pair_ref[...] = jnp.zeros_like(pair_ref)
    old_pair_ref[...] = jnp.zeros_like(old_pair_ref)
    for block in range(qt_ref.shape[1] // BLOCK):
        cut = pl.ds(block * BLOCK, BLOCK)
        lo, hi = window_of(lo_ref, block, before, group)
        query = heads_side_by_side(qt_ref, block, group)
        upstream = heads_side_by_side(dt_ref, block, group)
        query_rows = heads_one_above(q_ref, block, group)
        upstream_rows = heads_one_above(d_ref, block, group)
        nothing = jnp.zeros_like(query_rows)
        both_rows = jnp.concatenate(
            [
                jnp.concatenate([query_rows, nothing], axis=1),
                jnp.concatenate([nothing, upstream_rows], axis=1),
            ],
            axis=0,
        )
        logs = jnp.concatenate([log_ref[0, h : h + 1, cut] for h in range(group)], axis=1)
        spread = jnp.concatenate([spread_ref[0, h : h + 1, cut] for h in range(group)], axis=1)

        def step(keys_ref, keys_t_ref, values_ref, sums_ref, offset, number, acc):
            start = pl.multiple_of(number * BLOCK, BLOCK)
            here = pl.ds(start, BLOCK)
            scores = mm(keys_ref[0, here, :], query)
            mask = block_mask(lo, hi, start + offset, lanes)
            probs = jnp.exp(jnp.where(mask, scores - logs, masked_value))
            change = mm(values_ref[0, here, :], upstream)
            scores_change = (probs * (change - spread)).astype(bf16)
            sums_ref[here, :] += mm(
                jnp.concatenate([scores_change, probs.astype(bf16)], axis=1), both_rows
            )
            return acc + mm(keys_t_ref[:, here], scores_change)

        first = first_ref[block]
        acc = jnp.zeros((HEAD_DIM, lanes), f32)
        earlier = functools.partial(step, old_k_ref, old_kt_ref, old_v_ref, old_pair_ref, 0)
        acc = lax.fori_loop(first, passed, earlier, acc)
        own = functools.partial(step, k_ref, kt_ref, v_ref, pair_ref, before)
        acc = lax.fori_loop(jnp.maximum(first - passed, 0), block + 1, own, acc)
        for h in range(group):
            dq_ref[h * HEAD_DIM : (h + 1) * HEAD_DIM, cut] = (
                acc[:, h * BLOCK : (h + 1) * BLOCK] * score_scale
            )
    pair_t = pair_ref[...].T
    dk_ref[...] = pair_t[:HEAD_DIM]
    dv_ref[...] = pair_t[HEAD_DIM:]
    pair_t = old_pair_ref[...].T
    old_dk_ref[...] = pair_t[:HEAD_DIM].astype(bf16)
    old_dv_ref[...] = pair_t[HEAD_DIM:].astype(bf16)


def attend_back(
    first, lo, logs, spread, q_t, d_t, q_rows, d_rows, k, k_t, v, old_k, old_k_t, old_v
):
    pair_heads, before, _ = old_k.shape
    group, rows = q_rows.shape[1:3]
    tall = group * HEAD_DIM
    by_head = lambda h, s: (h, 0, 0)
    flat = lambda h, s: (h, 0)
    split = pair_heads * HEAD_DIM
    return pl.pallas_call(
        functools.partial(attend_back_kernel, group),
        grid_spec=pltpu.PrefetchScalarGridSpec(
            num_scalar_prefetch=1,
            grid=(pair_heads,),
            in_specs=[
                pl.BlockSpec((1, rows), lambda h, s: (0, 0)),
                pl.BlockSpec((1, group, rows), by_head),
                pl.BlockSpec((1, group, rows), by_head),
                pl.BlockSpec((tall, rows), flat),
                pl.BlockSpec((tall, rows), flat),
                pl.BlockSpec((1, group, rows, HEAD_DIM), lambda h, s: (h, 0, 0, 0)),
                pl.BlockSpec((1, group, rows, HEAD_DIM), lambda h, s: (h, 0, 0, 0)),
                pl.BlockSpec((1, rows, HEAD_DIM), by_head),
                pl.BlockSpec((HEAD_DIM, rows), flat),
                pl.BlockSpec((1, rows, HEAD_DIM), by_head),
                pl.BlockSpec((1, before, HEAD_DIM), by_head),
                pl.BlockSpec((HEAD_DIM, before), flat),
                pl.BlockSpec((1, before, HEAD_DIM), by_head),
            ],
            out_specs=[
                pl.BlockSpec((tall, rows), flat),
                pl.BlockSpec((HEAD_DIM, rows), flat),
                pl.BlockSpec((HEAD_DIM, rows), flat),
                pl.BlockSpec((HEAD_DIM, before), flat),
                pl.BlockSpec((HEAD_DIM, before), flat),
            ],
            scratch_shapes=[
                pltpu.VMEM((rows, 2 * HEAD_DIM), f32),
                pltpu.VMEM((before, 2 * HEAD_DIM), f32),
            ],
        ),
        out_shape=[
            jax.ShapeDtypeStruct((pair_heads * tall, rows), f32),
            jax.ShapeDtypeStruct((split, rows), f32),
            jax.ShapeDtypeStruct((split, rows), f32),
            jax.ShapeDtypeStruct((split, before), bf16),
            jax.ShapeDtypeStruct((split, before), bf16),
        ],
        compiler_params=pltpu.CompilerParams(vmem_limit_bytes=vmem_bytes),
        cost_estimate=pl.CostEstimate(
            flops=pair_heads * group * rows * (rows + before) * 1280,
            bytes_accessed=16 * 1024 * 1024,
            transcendentals=pair_heads * group * rows * (rows + before),
        ),
        name="attend_back",
    )(first, lo, logs, spread, q_t, d_t, q_rows, d_rows, k, k_t, v, old_k, old_k_t, old_v)


def turn(tall, cosine, sine):
    half = HEAD_DIM // 2
    parts = []
    for start in range(0, tall.shape[0], HEAD_DIM):
        a, b = tall[start : start + half], tall[start + half : start + HEAD_DIM]
        parts += [a * cosine - b * sine, b * cosine + a * sine]
    return jnp.concatenate(parts, axis=0)


def put_heads(ref, rows_of_heads):
    for h in range(ref.shape[0]):
        ref[h] = rows_of_heads[:, h * HEAD_DIM : (h + 1) * HEAD_DIM]


def project_kernel(
    x_ref, gain_ref, cos_ref, sin_ref, wq_ref, wk_ref, wv_ref,
    normed_ref, qt_ref, q_ref, kt_ref, k_ref, vt_ref, v_ref,
):
    x = x_ref[...].astype(f32)
    normed = (x * scale_of(x) * gain_ref[...].astype(f32)).astype(bf16)
    normed_ref[...] = normed
    cosine, sine = cos_ref[...], sin_ref[...]
    q_t = turn(mm(normed, wq_ref[...]).T, cosine, sine).astype(bf16).astype(f32) * score_scale
    qt_ref[...] = q_t.astype(bf16)
    put_heads(q_ref, q_t.T.astype(bf16))
    k_t = turn(dot(wk_ref[...], normed, 1, 1), cosine, sine)
    kt_ref[...] = k_t.astype(bf16)
    put_heads(k_ref, k_t.T.astype(bf16))
    v_t = dot(wv_ref[...], normed, 1, 1)
    vt_ref[...] = v_t.astype(bf16)
    put_heads(v_ref, v_t.T.astype(bf16))


def project(tokens, gain, cosine, sine, w_query, w_key, w_value):
    rows, width = tokens.shape
    tall, split = w_query.shape[1], w_key.shape[0]
    heads, pair_heads = tall // HEAD_DIM, split // HEAD_DIM
    whole = lambda shape: pl.BlockSpec(shape, lambda t: (0,) * len(shape))
    down = lambda wide: pl.BlockSpec((BLOCK, wide), lambda t: (t, 0))
    across = lambda high: pl.BlockSpec((high, BLOCK), lambda t: (0, t))
    stacked = lambda count: pl.BlockSpec((count, BLOCK, HEAD_DIM), lambda t: (0, t, 0))
    return pl.pallas_call(
        project_kernel,
        grid=(rows // BLOCK,),
        in_specs=[
            down(width), whole((1, width)), across(HEAD_DIM // 2), across(HEAD_DIM // 2),
            whole((width, tall)), whole((split, width)), whole((split, width)),
        ],
        out_specs=[
            down(width), across(tall), stacked(heads), across(split), stacked(pair_heads),
            across(split), stacked(pair_heads),
        ],
        out_shape=[
            jax.ShapeDtypeStruct((rows, width), bf16),
            jax.ShapeDtypeStruct((tall, rows), bf16),
            jax.ShapeDtypeStruct((heads, rows, HEAD_DIM), bf16),
            jax.ShapeDtypeStruct((split, rows), bf16),
            jax.ShapeDtypeStruct((pair_heads, rows, HEAD_DIM), bf16),
            jax.ShapeDtypeStruct((split, rows), bf16),
            jax.ShapeDtypeStruct((pair_heads, rows, HEAD_DIM), bf16),
        ],
        compiler_params=pltpu.CompilerParams(vmem_limit_bytes=vmem_bytes),
        cost_estimate=pl.CostEstimate(
            flops=2 * rows * width * (tall + 2 * split),
            bytes_accessed=12 * 1024 * 1024,
            transcendentals=0,
        ),
        name="project",
    )(tokens, gain, cosine, sine, w_query, w_key, w_value)


def enter_mixture_kernel(count, x_ref, gain_ref, router_ref, routes_ref, *refs):
    pieces, (hidden_ref, normed_ref, normed_t_ref, gates_ref) = refs[: 2 * count], refs[2 * count :]
    products = [
        mm(context_ref[...].astype(f32).T.astype(bf16), w_ref[...])
        for context_ref, w_ref in zip(pieces[:count], pieces[count:])
    ]
    sides = max(1, count // 2)
    projected = functools.reduce(jnp.add, products[:sides])
    if count > sides:
        projected = projected + functools.reduce(jnp.add, products[sides:])
    hidden = x_ref[...].astype(f32) + residual_scale * projected
    hidden_ref[...] = hidden
    normed = hidden * scale_of(hidden) * gain_ref[...].astype(f32)
    normed_t_ref[...] = normed.T.astype(bf16)
    normed = normed.astype(bf16)
    normed_ref[...] = normed
    logits = dot(router_ref[...], normed, 1, 1)
    expert = lax.broadcasted_iota(jnp.int32, logits.shape, 0)
    chosen = expert == routes_ref[0:1, :]
    for k in range(1, routes_ref.shape[0]):
        chosen = chosen | (expert == routes_ref[k : k + 1, :])
    logits = jnp.where(chosen, logits, masked_value)
    weights = jnp.exp(logits - jnp.max(logits, axis=0, keepdims=True))
    weights = jnp.where(chosen, weights, 0.0)
    gates_ref[...] = weights / jnp.sum(weights, axis=0, keepdims=True)


def enter_mixture(tokens, gain, router_t, routes_t, contexts, weights):
    rows, width = tokens.shape
    whole = lambda shape: pl.BlockSpec(shape, lambda t: (0,) * len(shape))
    down = lambda wide: pl.BlockSpec((BLOCK, wide), lambda t: (t, 0))
    across = lambda high: pl.BlockSpec((high, BLOCK), lambda t: (0, t))
    return pl.pallas_call(
        functools.partial(enter_mixture_kernel, len(contexts)),
        grid=(rows // BLOCK,),
        in_specs=[
            down(width), whole((1, width)), whole(router_t.shape), across(routes_t.shape[0]),
            *[across(context.shape[0]) for context in contexts],
            *[whole(weight.shape) for weight in weights],
        ],
        out_specs=[down(width), down(width), across(width), across(EXPERTS)],
        out_shape=[
            jax.ShapeDtypeStruct((rows, width), f32),
            jax.ShapeDtypeStruct((rows, width), bf16),
            jax.ShapeDtypeStruct((width, rows), bf16),
            jax.ShapeDtypeStruct((EXPERTS, rows), f32),
        ],
        compiler_params=pltpu.CompilerParams(vmem_limit_bytes=vmem_bytes),
        cost_estimate=pl.CostEstimate(
            flops=2 * rows * width * width, bytes_accessed=16 * 1024 * 1024, transcendentals=0
        ),
        name="enter_mixture",
    )(tokens, gain, router_t, routes_t, *contexts, *weights)


def enter_back_kernel(
    c_ref, own_ref, other_ref, wo_ref, ctx_ref, hidden_ref, dt_ref, d_ref, spread_ref, wo_grad_ref
):
    hidden_gradient = c_ref[...].astype(f32) + (
        own_ref[...].astype(f32) + other_ref[...].astype(f32)
    )
    hidden_ref[...] = hidden_gradient
    attention_gradient = (residual_scale * hidden_gradient).astype(bf16)
    d_t = dot(wo_ref[...], attention_gradient, 1, 1)
    dt_ref[...] = d_t.astype(bf16)
    put_heads(d_ref, d_t.T.astype(bf16))
    context_t = ctx_ref[...]
    weighed = d_t.astype(bf16).astype(f32) * context_t.astype(f32)
    for h in range(spread_ref.shape[0]):
        spread_ref[h : h + 1, :] = jnp.sum(
            weighed[h * HEAD_DIM : (h + 1) * HEAD_DIM], axis=0, keepdims=True
        )

    @pl.when(pl.program_id(0) == 0)
    def start():
        wo_grad_ref[...] = jnp.zeros_like(wo_grad_ref)

    wo_grad_ref[...] += mm(context_t, attention_gradient)


def enter_back(cotangent, own, other, w_out, context_t):
    rows, width = cotangent.shape
    tall = w_out.shape[0]
    heads = tall // HEAD_DIM
    whole = lambda shape: pl.BlockSpec(shape, lambda t: (0,) * len(shape))
    down = lambda wide: pl.BlockSpec((BLOCK, wide), lambda t: (t, 0))
    across = lambda high: pl.BlockSpec((high, BLOCK), lambda t: (0, t))
    return pl.pallas_call(
        enter_back_kernel,
        grid=(rows // BLOCK,),
        in_specs=[down(width), down(width), down(width), whole((tall, width)), across(tall)],
        out_specs=[
            down(width), across(tall),
            pl.BlockSpec((heads, BLOCK, HEAD_DIM), lambda t: (0, t, 0)),
            across(heads), whole((tall, width)),
        ],
        out_shape=[
            jax.ShapeDtypeStruct((rows, width), f32),
            jax.ShapeDtypeStruct((tall, rows), bf16),
            jax.ShapeDtypeStruct((heads, rows, HEAD_DIM), bf16),
            jax.ShapeDtypeStruct((heads, rows), f32),
            jax.ShapeDtypeStruct((tall, width), f32),
        ],
        compiler_params=pltpu.CompilerParams(vmem_limit_bytes=vmem_bytes),
        cost_estimate=pl.CostEstimate(
            flops=4 * rows * width * tall, bytes_accessed=20 * 1024 * 1024, transcendentals=0
        ),
        name="enter_back",
    )(cotangent, own, other, w_out, context_t)


def leave_back_kernel(
    core_ref, x_ref, gain_ref, cos_ref, sin_ref, wq_ref, wk_ref, wv_ref, normed_ref,
    dq_ref, dk_ref, dv_ref, more_dk_ref, more_dv_ref, wo_grad_ref, router_grad_ref, gain_two_grad_ref,
    part_ref, send_ref, keep_ref, sum_ref, gain_grad_ref,
):
    step = pl.program_id(0)
    cosine, sine = cos_ref[...], -sin_ref[...]
    dq_t = turn(dq_ref[...], cosine, sine).astype(bf16)
    dk_t = turn(dk_ref[...] + more_dk_ref[...].astype(f32), cosine, sine).astype(bf16)
    dv_t = (dv_ref[...] + more_dv_ref[...].astype(f32)).astype(bf16)
    normed = normed_ref[...]

    @pl.when(step == 0)
    def start():
        sum_ref[...] = jnp.zeros_like(sum_ref)
        gain_grad_ref[...] = jnp.zeros_like(gain_grad_ref)

    stacked = jnp.concatenate([dq_t, dk_t, dv_t], axis=0)
    sum_ref[: stacked.shape[0]] += mm(stacked, normed)
    rows_of = lambda tall: tall.astype(f32).T.astype(bf16)
    upstream = (
        dot(rows_of(dq_t), wq_ref[...], 1, 1)
        + mm(rows_of(dk_t), wk_ref[...])
        + mm(rows_of(dv_t), wv_ref[...])
    )
    x = x_ref[...].astype(f32)
    part, gain_part = norm_back(x, scale_of(x), gain_ref[...].astype(f32), upstream)
    part_ref[...] = part.astype(bf16)
    gain_grad_ref[...] += gain_part[None, :]

    @pl.when(step == pl.num_programs(0) - 1)
    def finish():
        place = stacked.shape[0]
        sum_ref[place : place + wo_grad_ref.shape[0]] = wo_grad_ref[...]
        place += wo_grad_ref.shape[0]
        sum_ref[place : place + EXPERTS] = router_grad_ref[...]
        place += EXPERTS
        sum_ref[place : place + 1] = gain_two_grad_ref[...]
        sum_ref[place + 1 : place + 2] = gain_grad_ref[...]
        high = keep_ref.shape[0]
        send_from = pl.multiple_of((1 - core_ref[0]) * high, 16)
        keep_from = pl.multiple_of(core_ref[0] * high, 16)
        send_ref[...] = sum_ref[pl.ds(send_from, high)].astype(bf16)
        keep_ref[...] = sum_ref[pl.ds(keep_from, high)].astype(bf16)


def leave_back(
    core, high, tokens, gain, cosine, sine, w_query, w_key, w_value, normed, dq_t, dk_t, dv_t,
    more_dk, more_dv, w_out_gradient, router_gradient, second_gain_gradient,
):
    rows, width = tokens.shape
    tall, split = w_query.shape[1], w_key.shape[0]
    whole = lambda shape: pl.BlockSpec(shape, lambda t, s: (0,) * len(shape))
    down = lambda wide: pl.BlockSpec((BLOCK, wide), lambda t, s: (t, 0))
    across = lambda high: pl.BlockSpec((high, BLOCK), lambda t, s: (0, t))
    return pl.pallas_call(
        leave_back_kernel,
        grid_spec=pltpu.PrefetchScalarGridSpec(
            num_scalar_prefetch=1,
            grid=(rows // BLOCK,),
            in_specs=[
                down(width), whole((1, width)), across(HEAD_DIM // 2), across(HEAD_DIM // 2),
                whole((width, tall)), whole((split, width)), whole((split, width)), down(width),
                across(tall), across(split), across(split), across(split), across(split),
                whole((tall, width)), whole((EXPERTS, width)), whole((1, width)),
            ],
            out_specs=[down(width), whole((high, width)), whole((high, width))],
            scratch_shapes=[pltpu.VMEM((2 * high, width), f32), pltpu.VMEM((1, width), f32)],
        ),
        out_shape=[
            jax.ShapeDtypeStruct((rows, width), bf16),
            jax.ShapeDtypeStruct((high, width), bf16),
            jax.ShapeDtypeStruct((high, width), bf16),
        ],
        compiler_params=pltpu.CompilerParams(vmem_limit_bytes=expert_vmem_bytes),
        cost_estimate=pl.CostEstimate(
            flops=4 * rows * width * (tall + 2 * split),
            bytes_accessed=24 * 1024 * 1024,
            transcendentals=0,
        ),
        name="leave_back",
    )(
        core, tokens, gain, cosine, sine, w_query, w_key, w_value, normed, dq_t, dk_t, dv_t,
        more_dk, more_dv, w_out_gradient, router_gradient, second_gain_gradient,
    )


def expert_kernel(
    adds, ids_ref, gates_ref, xt_ref, x_ref, ct_ref, c_ref, up_ref, down_ref, *refs
):
    if adds:
        more_ref, *refs = refs
    _, _, _, grad_ref, up_grad_ref, act_ref, gate_grad_ref = refs
    rows = x_ref.shape[0]
    chunk = min(BLOCK, rows)
    for part in range(rows // chunk):
        cut = pl.ds(part * chunk, chunk)
        xt = xt_ref[:, cut]
        gate = mm(up_ref[0, 0], xt)
        up = mm(up_ref[0, 1], xt)
        active_grad = mm(down_ref[0], ct_ref[:, cut])
        share = 1.0 / (1.0 + jnp.exp(-gate))
        silu = gate * share
        active = silu * up
        weight = gates_ref[0, :, cut] * residual_scale
        gate_grad_ref[0, 0, :, cut] = residual_scale * jnp.sum(
            active * active_grad, axis=0, keepdims=True
        )
        active_grad = active_grad * weight
        act_ref[0, :, cut] = (active * weight).astype(bf16)
        up_grad_ref[0, 0, :, cut] = (
            active_grad * up * (share + silu * (1.0 - share))
        ).astype(bf16)
        up_grad_ref[0, 1, :, cut] = (active_grad * silu).astype(bf16)

    def put(place, total):
        if adds:
            total = total + more_ref[0, place].astype(f32)
        grad_ref[0, place] = total.astype(bf16)

    x = x_ref[...]
    put(0, mm(up_grad_ref[0, 0], x))
    put(1, mm(up_grad_ref[0, 1], x))
    put(2, mm(act_ref[0], c_ref[...]))


def expert_step(ids, half, gates, xt, x, ct, c, w_up, w_down, more, old):
    count = ids.shape[0]
    rows, width = x.shape
    units = w_down.shape[1] // 2
    whole = lambda shape: pl.BlockSpec(shape, lambda e, s: (0,) * len(shape))
    fresh = old is None
    adds = more is not None
    each = pl.BlockSpec((1, 3, units, width), lambda e, s: (e, 0, 0, 0))
    if fresh:
        old = (jnp.zeros((8, 128), f32),) * 3
    return pl.pallas_call(
        functools.partial(expert_kernel, adds),
        grid_spec=pltpu.PrefetchScalarGridSpec(
            num_scalar_prefetch=1,
            grid=(count,),
            in_specs=[
                pl.BlockSpec((1, 1, rows), lambda e, s: (s[e], 0, 0)),
                whole((width, rows)),
                whole((rows, width)),
                whole((width, rows)),
                whole((rows, width)),
                pl.BlockSpec((1, 2, units, width), lambda e, s: (s[e], 0, half, 0)),
                pl.BlockSpec((1, units, width), lambda e, s: (s[e], half, 0)),
                *([each] if adds else []),
                pl.BlockSpec(memory_space=pl.ANY),
                pl.BlockSpec(memory_space=pl.ANY),
                pl.BlockSpec(memory_space=pl.ANY),
            ],
            out_specs=[
                each,
                pl.BlockSpec((1, 2, units, rows), lambda e, s: (s[e], 0, half, 0)),
                pl.BlockSpec((1, units, rows), lambda e, s: (s[e], half, 0)),
                pl.BlockSpec((1, 1, 1, rows), lambda e, s: (half, s[e], 0, 0)),
            ],
        ),
        out_shape=[
            jax.ShapeDtypeStruct((count, 3, units, width), bf16),
            jax.ShapeDtypeStruct((EXPERTS, 2, 2 * units, rows), bf16),
            jax.ShapeDtypeStruct((EXPERTS, 2 * units, rows), bf16),
            jax.ShapeDtypeStruct((2, EXPERTS, 1, rows), f32),
        ],
        input_output_aliases={} if fresh else {8 + adds: 1, 9 + adds: 2, 10 + adds: 3},
        compiler_params=pltpu.CompilerParams(vmem_limit_bytes=expert_vmem_bytes),
        cost_estimate=pl.CostEstimate(
            flops=count * 12 * rows * width * units,
            bytes_accessed=count * units * width * 12 + 8 * rows * width,
            transcendentals=count * units * rows,
        ),
        name="experts",
    )(ids, gates, xt, x, ct, c, w_up, w_down, *([more] if adds else []), *old)


def from_other_half(shard):
    return lax.ppermute(shard, "tensor", [(0, 1), (1, 0)])


def gathered(shard):
    if lax.axis_size("tensor") != 2:
        return [lax.all_gather(shard, "tensor", axis=0, tiled=True)]
    return [shard, from_other_half(shard)]


def both_parts(part):
    if lax.axis_size("tensor") != 2:
        return lax.psum(part, "tensor"), jnp.zeros_like(part)
    return part, from_other_half(part)


def summed_parts(part):
    low = part.astype(bf16)
    if lax.axis_size("tensor") != 2:
        return lax.psum(low, "tensor").astype(f32)
    return low.astype(f32) + from_other_half(low).astype(f32)


def chip_order(chips):
    there = [2 * z for z in range(chips // 2)]
    return there + [chip + 1 for chip in reversed(there)]


def chunk_experts(device, peers, number):
    order = jnp.array(chip_order(peers // 2), jnp.int32)
    each = EXPERTS // peers
    core = device % 2

    def owned(side):
        chips = jnp.where(side == 0, order, order[::-1])
        return (2 * chips + side) * each + number

    return owned(1 - core).astype(jnp.int32), owned(core).astype(jnp.int32)


def chip_rings():
    order = chip_order(lax.axis_size("dp") // 2)
    return [[2 * chip for chip in order], [2 * chip + 1 for chip in reversed(order)]]


def to_owner(chip_sum):
    return lax.psum_scatter(
        chip_sum, "dp", scatter_dimension=0, axis_index_groups=chip_rings(), tiled=True
    )


def summed_over_tokens(send, keep, beside_one, beside_two):
    swap = [(i, i ^ 1) for i in range(lax.axis_size("dp"))]
    received = lax.ppermute(send, "dp", swap)
    half = (keep.astype(f32) + received.astype(f32)).astype(bf16)
    rings = chip_rings()
    half = lax.psum_scatter(half, "dp", scatter_dimension=0, axis_index_groups=rings, tiled=True)
    half, beside_one = lax.optimization_barrier((half, beside_one))
    half = lax.all_gather(half, "dp", axis=0, axis_index_groups=rings, tiled=True)
    half, beside_two = lax.optimization_barrier((half, beside_two))
    other = lax.ppermute(half, "dp", swap)
    is_first = lax.axis_index("dp") % 2 == 0
    low, high = jnp.where(is_first, half, other), jnp.where(is_first, other, half)
    return jnp.concatenate([low, high], axis=0), beside_one, beside_two


def angles(position):
    inverse = rope_base ** (-2.0 * jnp.arange(HEAD_DIM // 2, dtype=f32) / HEAD_DIM)
    angle = inverse[:, None] * position.astype(f32)[None, :]
    return jnp.cos(angle), jnp.sin(angle)


def scale_of(values):
    return lax.rsqrt(jnp.mean(values * values, axis=-1, keepdims=True) + epsilon)


def norm_back(values, scale, gain, upstream):
    pulled = gain * upstream
    slope = jnp.mean(pulled * values, axis=-1, keepdims=True)
    return (
        scale * pulled - values * (scale * scale * scale * slope),
        jnp.sum(upstream * values * scale, axis=0),
    )


def on_device(
    tokens, doc_ids, routes, attention_gain, w_query, w_key, w_value, w_out, mixture_gain,
    w_router, expert_gate_up, expert_down, out_cotangent,
):
    rows, width = tokens.shape
    peers = lax.axis_size("dp")
    device = lax.axis_index("dp")
    pair_heads = w_key.shape[0] // HEAD_DIM
    group = w_query.shape[1] // w_key.shape[0]
    first = device * rows
    chunks = EXPERTS // peers
    w_out_parts = gathered(w_out)

    docs = lax.dynamic_slice_in_dim(doc_ids, first, rows)
    docs_before = lax.dynamic_slice_in_dim(doc_ids, jnp.maximum(device - 1, 0) * rows, rows)
    docs_before = jnp.where(device > 0, docs_before, -1)
    docs_window = jnp.concatenate([docs_before, docs])
    lo = jnp.sum((docs_window[:, None] < docs[None, :]).astype(jnp.int32), axis=0)
    first_block = lo[::BLOCK] // BLOCK
    lo = lo[None, :]

    position = (first + jnp.arange(rows, dtype=jnp.int32)) % SEQ_LEN
    cosine, sine = angles(position)
    gain_one = attention_gain[None, :]
    normed_attention, q_t, q_rows, k_t, k_rows, v_t, v_rows = project(
        tokens, gain_one, cosine, sine, w_query, w_key, w_value
    )
    to_next = [(i, i + 1) for i in range(0, peers, 2)]
    before = SEQ_LEN - rows
    old_k_t = lax.ppermute(k_t, "dp", to_next)
    old_v_t = lax.ppermute(v_t, "dp", to_next)
    across = lambda tall: jnp.swapaxes(tall.reshape(pair_heads, HEAD_DIM, before), 1, 2)
    old_k_rows, old_v_rows = across(old_k_t), across(old_v_t)

    calls = 2 if pair_heads % 2 == 0 else 1
    here = pair_heads // calls
    pieces = [
        attend(
            first_block, lo, q_t, k_rows, v_t, old_k_rows, old_v_t, group, call * here, here
        )
        for call in range(calls)
    ]
    context_parts = [gathered(piece[0]) for piece in pieces]
    contexts = [parts[side] for side in range(len(context_parts[0])) for parts in context_parts]
    context_t = jnp.concatenate([piece[0] for piece in pieces], axis=0)
    logs = jnp.concatenate([piece[1] for piece in pieces], axis=0)
    w_out_pieces = [
        piece for part in w_out_parts for piece in jnp.split(part, calls, axis=0)
    ]
    hidden, normed_mixture, normed_t, gates = enter_mixture(
        tokens, mixture_gain[None, :], w_router.T, routes.T, contexts, w_out_pieces
    )
    gain_two = mixture_gain.astype(f32)
    scale_two = scale_of(hidden)

    upstream_t = out_cotangent.T
    swap_cores = [(i, i ^ 1) for i in range(peers)]
    shares, arrived, old = [], [], None
    pieces = [(number, half) for number in range(chunks) for half in range(2)]

    def run_experts(piece, side, more):
        ids = chunk_experts(device, peers, piece[0])[side]
        return expert_step(
            ids, piece[1], gates[:, None, :], normed_t, normed_mixture, upstream_t, out_cotangent,
            expert_gate_up, expert_down, more, old,
        )

    for number in range(len(pieces) + 1):
        if number < len(pieces):
            send, *old = run_experts(pieces[number], 0, None)
            arrived.append(lax.ppermute(send, "dp", swap_cores))
        if number > 0:
            chip_sum, *old = run_experts(pieces[number - 1], 1, arrived[number - 1])
            shares.append(to_owner(chip_sum))
    up_grad, act, gates_gradient = old
    gates_gradient = gates_gradient[0, :, 0] + gates_gradient[1, :, 0]
    units = expert_down.shape[1]
    wide = EXPERTS * units

    logits_gradient = gates * (
        gates_gradient - jnp.sum(gates * gates_gradient, axis=0, keepdims=True)
    )
    logits_low = logits_gradient.astype(bf16)
    router_gradient = mm(logits_low, normed_mixture)
    up_grad = up_grad.reshape(2 * wide, rows)
    w_up = expert_gate_up.reshape(2 * wide, width)
    own_parts, other_parts, gain_parts = [], [], []
    for start in range(0, rows, rows // 2):
        cut = slice(start, start + rows // 2)
        if start > 0:
            up_grad, own_parts[0] = lax.optimization_barrier((up_grad, own_parts[0]))
        normed_gradient = dot(up_grad[:, cut], w_up, 0, 0) + dot(logits_low[:, cut], w_router, 0, 1)
        part, gain_part = norm_back(hidden[cut], scale_two[cut], gain_two, normed_gradient)
        part = part.astype(bf16)
        if start > 0:
            part, act, other_parts[0] = lax.optimization_barrier((part, act, other_parts[0]))
        own, other = both_parts(part)
        own_parts.append(own)
        other_parts.append(other)
        gain_parts.append(gain_part)
    second_gain_part = gain_parts[0] + gain_parts[1]

    mixture_part = dot(act.reshape(wide, rows), expert_down.reshape(wide, width), 0, 0)
    mixture_low = mixture_part.astype(bf16)
    own_part = jnp.concatenate(own_parts, axis=0)
    other_part = jnp.concatenate(other_parts, axis=0)
    own_part, other_part, mixture_low = lax.optimization_barrier(
        (own_part, other_part, mixture_low)
    )
    mixture_own, mixture_other = both_parts(mixture_low)

    hidden_gradient, d_t, d_rows, spread, w_out_gradient = enter_back(
        out_cotangent, own_part, other_part, w_out, context_t
    )
    by_group = lambda rows_of_heads: rows_of_heads.reshape(pair_heads, group, rows, HEAD_DIM)
    dq_t, dk_t, dv_t, old_dk, old_dv = attend_back(
        first_block, lo, logs, spread.reshape(pair_heads, group, rows), q_t, d_t, by_group(q_rows),
        by_group(d_rows), k_rows, k_t, v_rows, old_k_rows, old_k_t, old_v_rows,
    )
    to_previous = [(i + 1, i) for i in range(0, peers, 2)]
    more_dk = lax.ppermute(old_dk, "dp", to_previous)
    more_dv = lax.ppermute(old_dv, "dp", to_previous)
    dq_t, mixture_other, *shares[:-2] = lax.optimization_barrier(
        (dq_t, mixture_other, *shares[:-2])
    )
    tall, split = w_query.shape[1], w_key.shape[0]
    ends = [tall, tall + split, tall + 2 * split, 2 * tall + 2 * split, 2 * tall + 2 * split + EXPERTS]
    high = -(-(ends[-1] + 2) // (16 * peers)) * 8 * peers
    input_part, send, keep = leave_back(
        (device % 2)[None].astype(jnp.int32), high, tokens, gain_one, cosine, sine, w_query, w_key,
        w_value, normed_attention, dq_t, dk_t, dv_t, more_dk, more_dv, w_out_gradient,
        router_gradient, second_gain_part[None, :],
    )
    swapped = [both_parts(part) for part in jnp.split(input_part, 2, axis=0)]
    *shares[-2:], keep = lax.optimization_barrier((*shares[-2:], keep))
    swapped = [list(pair) for pair in swapped]
    gradients, swapped[0][1], swapped[1][1] = summed_over_tokens(
        send, keep, swapped[0][1], swapped[1][1]
    )
    input_sum = jnp.concatenate(
        [own.astype(f32) + other.astype(f32) for own, other in swapped], axis=0
    )
    mixed = (hidden + (mixture_own.astype(f32) + mixture_other.astype(f32))).astype(bf16)
    tokens_gradient = hidden_gradient + input_sum
    w_q, w_k, w_v, w_o = jnp.split(gradients[: ends[3]].astype(f32), ends[:3], axis=0)
    small = summed_parts(gradients[ends[3] :])
    router, gains = small[:EXPERTS], small[EXPERTS:]
    halves = [
        jnp.concatenate(shares[start : start + 2], axis=2) for start in range(0, len(shares), 2)
    ]
    experts_gradient = jnp.concatenate(halves, axis=0).astype(f32)
    return (
        mixed, tokens_gradient.astype(bf16), gains[1], w_q.T, w_k, w_v, w_o, gains[0], router.T,
        experts_gradient[:, :2], experts_gradient[:, 2],
    )


def solution(mesh):
    placed = (
        P("dp", None),
        P(),
        P("dp", None),
        P(),
        P(None, "tensor"),
        P("tensor", None),
        P("tensor", None),
        P("tensor", None),
        P(),
        P(),
        P(None, None, "tensor", None),
        P(None, "tensor", None),
        P("dp", None),
    )
    return jax.shard_map(
        on_device,
        mesh=mesh,
        in_specs=placed,
        out_specs=(
            P("dp", None),
            P("dp", None),
            P(),
            P(None, "tensor"),
            P("tensor", None),
            P("tensor", None),
            P("tensor", None),
            P(),
            P(),
            P("dp", None, "tensor", None),
            P("dp", "tensor", None),
        ),
        check_vma=False,
    )
```

```python
import functools

import jax
import jax.numpy as jnp
from jax import lax
from jax.experimental import pallas as pl
from jax.experimental.pallas import tpu as pltpu
from jax.sharding import PartitionSpec as P

HEAD_DIM = 64
EXPERTS = 32
SEQ_LEN = 2048
BLOCK = 256

epsilon = 1e-06
score_scale = 0.015625
residual_scale = 0.22
rope_base = 10000.0
masked_value = -1e30
vmem_bytes = 60 * 1024 * 1024
f32 = jnp.float32
bf16 = jnp.bfloat16


def dot(left, right, left_dim, right_dim):
    return lax.dot_general(
        left, right, (((left_dim,), (right_dim,)), ((), ())), preferred_element_type=f32
    )


def mm(left, right):
    return jnp.dot(left, right, preferred_element_type=f32)


def block_mask(lo, hi, start, lanes):
    place = start + lax.broadcasted_iota(jnp.int32, (BLOCK, lanes), 0)
    return (place >= lo) & (place <= hi)


def window_of(lo_ref, block, before, group):
    cut = pl.ds(block * BLOCK, BLOCK)
    lo = lo_ref[:, cut]
    hi = before + block * BLOCK + lax.broadcasted_iota(jnp.int32, (1, BLOCK), 1)
    return (
        jnp.concatenate([lo] * group, axis=1),
        jnp.concatenate([hi] * group, axis=1),
    )


def heads_side_by_side(ref, block, group):
    cut = pl.ds(block * BLOCK, BLOCK)
    return jnp.concatenate(
        [ref[h * HEAD_DIM : (h + 1) * HEAD_DIM, cut] for h in range(group)], axis=1
    )


def heads_one_above(ref, j, block, group):
    cut = pl.ds(block * BLOCK, BLOCK)
    return jnp.concatenate([ref[j, h, cut, :] for h in range(group)], axis=0)


def attend_kernel(
    group, first_ref, lo_ref, qt_ref, k_ref, vt_ref, old_k_ref, old_vt_ref, out_ref, log_ref
):
    lanes = group * BLOCK
    together, before, _ = old_k_ref.shape
    tall = group * HEAD_DIM
    passed = before // BLOCK
    for block in range(qt_ref.shape[1] // BLOCK):
        lo, hi = window_of(lo_ref, block, before, group)
        queries = [
            heads_side_by_side(qt_ref.at[pl.ds(j * tall, tall)], block, group)
            for j in range(together)
        ]

        def step(keys_ref, values_ref, offset, number, carry):
            start = pl.multiple_of(number * BLOCK, BLOCK)
            here = pl.ds(start, BLOCK)
            mask = block_mask(lo, hi, offset + start, lanes)
            result = []
            for j, (peak, total, acc) in enumerate(carry):
                scores = mm(keys_ref[j, here, :], queries[j])
                scores = jnp.where(mask, scores, masked_value)
                top = jnp.maximum(peak, jnp.max(scores, axis=0, keepdims=True))
                weights = jnp.exp(scores - top)
                fade = jnp.exp(peak - top)
                total = total * fade + jnp.sum(weights, axis=0, keepdims=True)
                values = values_ref[j * HEAD_DIM : (j + 1) * HEAD_DIM, here]
                result.append((top, total, acc * fade + mm(values, weights.astype(bf16))))
            return tuple(result)

        first = first_ref[block]
        nothing = (
            jnp.full((1, lanes), masked_value, f32),
            jnp.zeros((1, lanes), f32),
            jnp.zeros((HEAD_DIM, lanes), f32),
        )
        carry = lax.fori_loop(
            first, passed, functools.partial(step, old_k_ref, old_vt_ref, 0), (nothing,) * together
        )
        carry = lax.fori_loop(
            jnp.maximum(first - passed, 0),
            block + 1,
            functools.partial(step, k_ref, vt_ref, before),
            carry,
        )
        cut = pl.ds(block * BLOCK, BLOCK)
        for j, (peak, total, acc) in enumerate(carry):
            result = (acc / total).astype(bf16)
            logs = peak + jnp.log(total)
            for h in range(group):
                side = slice(h * BLOCK, (h + 1) * BLOCK)
                high = j * tall + h * HEAD_DIM
                out_ref[high : high + HEAD_DIM, cut] = result[:, side]
                log_ref[j, h : h + 1, cut] = logs[:, side]


def attend(first, lo, q_t, k, v_t, old_k, old_v_t, group, base, pair_heads):
    rows = k.shape[1]
    before = old_k.shape[1]
    together = 1
    start = base // together
    tall = together * group * HEAD_DIM
    split = together * HEAD_DIM
    by_head = lambda h, s: (start + h, 0, 0)
    flat = lambda h, s: (start + h, 0)
    return pl.pallas_call(
        functools.partial(attend_kernel, group),
        grid_spec=pltpu.PrefetchScalarGridSpec(
            num_scalar_prefetch=1,
            grid=(pair_heads // together,),
            in_specs=[
                pl.BlockSpec((1, rows), lambda h, s: (0, 0)),
                pl.BlockSpec((tall, rows), flat),
                pl.BlockSpec((together, rows, HEAD_DIM), by_head),
                pl.BlockSpec((split, rows), flat),
                pl.BlockSpec((together, before, HEAD_DIM), by_head),
                pl.BlockSpec((split, before), flat),
            ],
            out_specs=[
                pl.BlockSpec((tall, rows), lambda h, s: (h, 0)),
                pl.BlockSpec((together, group, rows), lambda h, s: (h, 0, 0)),
            ],
        ),
        out_shape=[
            jax.ShapeDtypeStruct((pair_heads * group * HEAD_DIM, rows), bf16),
            jax.ShapeDtypeStruct((pair_heads, group, rows), f32),
        ],
        compiler_params=pltpu.CompilerParams(vmem_limit_bytes=vmem_bytes),
        cost_estimate=pl.CostEstimate(
            flops=pair_heads * group * rows * (rows + before) * 512,
            bytes_accessed=8 * 1024 * 1024,
            transcendentals=pair_heads * group * rows * (rows + before),
        ),
        name="attend",
    )(first, lo, q_t, k, v_t, old_k, old_v_t)


def attend_back_kernel(
    group,
    first_ref, lo_ref, log_ref, spread_ref, qt_ref, dt_ref, q_ref, d_ref, k_ref, kt_ref, v_ref,
    old_k_ref, old_kt_ref, old_v_ref,
    dq_ref, dk_ref, dv_ref, old_dk_ref, old_dv_ref, pair_ref, old_pair_ref,
):
    lanes = group * BLOCK
    together, before, _ = old_k_ref.shape
    tall = group * HEAD_DIM
    passed = before // BLOCK
    pair_ref[...] = jnp.zeros_like(pair_ref)
    old_pair_ref[...] = jnp.zeros_like(old_pair_ref)
    for block in range(qt_ref.shape[1] // BLOCK):
        cut = pl.ds(block * BLOCK, BLOCK)
        lo, hi = window_of(lo_ref, block, before, group)
        heads = []
        for j in range(together):
            here = pl.ds(j * tall, tall)
            query_rows = heads_one_above(q_ref, j, block, group)
            upstream_rows = heads_one_above(d_ref, j, block, group)
            nothing = jnp.zeros_like(query_rows)
            both_rows = jnp.concatenate(
                [
                    jnp.concatenate([query_rows, nothing], axis=1),
                    jnp.concatenate([nothing, upstream_rows], axis=1),
                ],
                axis=0,
            )
            heads.append(
                (
                    heads_side_by_side(qt_ref.at[here], block, group),
                    heads_side_by_side(dt_ref.at[here], block, group),
                    both_rows,
                    jnp.concatenate([log_ref[j, h : h + 1, cut] for h in range(group)], axis=1),
                    jnp.concatenate([spread_ref[j, h : h + 1, cut] for h in range(group)], axis=1),
                )
            )

        def step(keys_ref, keys_t_ref, values_ref, sums_ref, offset, number, sums):
            start = pl.multiple_of(number * BLOCK, BLOCK)
            here = pl.ds(start, BLOCK)
            mask = block_mask(lo, hi, start + offset, lanes)
            result = []
            for j, (query, upstream, both_rows, logs, spread) in enumerate(heads):
                scores = mm(keys_ref[j, here, :], query)
                probs = jnp.exp(jnp.where(mask, scores - logs, masked_value))
                change = mm(values_ref[j, here, :], upstream)
                scores_change = (probs * (change - spread)).astype(bf16)
                sums_ref[j, here, :] += mm(
                    jnp.concatenate([scores_change, probs.astype(bf16)], axis=1), both_rows
                )
                keys_t = keys_t_ref[j * HEAD_DIM : (j + 1) * HEAD_DIM, here]
                result.append(sums[j] + mm(keys_t, scores_change))
            return tuple(result)

        first = first_ref[block]
        sums = (jnp.zeros((HEAD_DIM, lanes), f32),) * together
        earlier = functools.partial(step, old_k_ref, old_kt_ref, old_v_ref, old_pair_ref, 0)
        sums = lax.fori_loop(first, passed, earlier, sums)
        own = functools.partial(step, k_ref, kt_ref, v_ref, pair_ref, before)
        sums = lax.fori_loop(jnp.maximum(first - passed, 0), block + 1, own, sums)
        for j in range(together):
            for h in range(group):
                high = j * tall + h * HEAD_DIM
                dq_ref[high : high + HEAD_DIM, cut] = (
                    sums[j][:, h * BLOCK : (h + 1) * BLOCK] * score_scale
                )
    for j in range(together):
        side = slice(j * HEAD_DIM, (j + 1) * HEAD_DIM)
        pair_t = pair_ref[j].T
        dk_ref[side] = pair_t[:HEAD_DIM]
        dv_ref[side] = pair_t[HEAD_DIM:]
        pair_t = old_pair_ref[j].T
        old_dk_ref[side] = pair_t[:HEAD_DIM].astype(bf16)
        old_dv_ref[side] = pair_t[HEAD_DIM:].astype(bf16)


def attend_back(
    first, lo, logs, spread, q_t, d_t, q_rows, d_rows, k, k_t, v, old_k, old_k_t, old_v
):
    pair_heads, before, _ = old_k.shape
    group, rows = q_rows.shape[1:3]
    together = 2 if pair_heads % 2 == 0 else 1
    tall = together * group * HEAD_DIM
    split = together * HEAD_DIM
    by_head = lambda h, s: (h, 0, 0)
    flat = lambda h, s: (h, 0)
    return pl.pallas_call(
        functools.partial(attend_back_kernel, group),
        grid_spec=pltpu.PrefetchScalarGridSpec(
            num_scalar_prefetch=1,
            grid=(pair_heads // together,),
            in_specs=[
                pl.BlockSpec((1, rows), lambda h, s: (0, 0)),
                pl.BlockSpec((together, group, rows), by_head),
                pl.BlockSpec((together, group, rows), by_head),
                pl.BlockSpec((tall, rows), flat),
                pl.BlockSpec((tall, rows), flat),
                pl.BlockSpec((together, group, rows, HEAD_DIM), lambda h, s: (h, 0, 0, 0)),
                pl.BlockSpec((together, group, rows, HEAD_DIM), lambda h, s: (h, 0, 0, 0)),
                pl.BlockSpec((together, rows, HEAD_DIM), by_head),
                pl.BlockSpec((split, rows), flat),
                pl.BlockSpec((together, rows, HEAD_DIM), by_head),
                pl.BlockSpec((together, before, HEAD_DIM), by_head),
                pl.BlockSpec((split, before), flat),
                pl.BlockSpec((together, before, HEAD_DIM), by_head),
            ],
            out_specs=[
                pl.BlockSpec((tall, rows), flat),
                pl.BlockSpec((split, rows), flat),
                pl.BlockSpec((split, rows), flat),
                pl.BlockSpec((split, before), flat),
                pl.BlockSpec((split, before), flat),
            ],
            scratch_shapes=[
                pltpu.VMEM((together, rows, 2 * HEAD_DIM), f32),
                pltpu.VMEM((together, before, 2 * HEAD_DIM), f32),
            ],
        ),
        out_shape=[
            jax.ShapeDtypeStruct((pair_heads * group * HEAD_DIM, rows), f32),
            jax.ShapeDtypeStruct((pair_heads * HEAD_DIM, rows), f32),
            jax.ShapeDtypeStruct((pair_heads * HEAD_DIM, rows), f32),
            jax.ShapeDtypeStruct((pair_heads * HEAD_DIM, before), bf16),
            jax.ShapeDtypeStruct((pair_heads * HEAD_DIM, before), bf16),
        ],
        compiler_params=pltpu.CompilerParams(vmem_limit_bytes=vmem_bytes),
        cost_estimate=pl.CostEstimate(
            flops=pair_heads * group * rows * (rows + before) * 1280,
            bytes_accessed=16 * 1024 * 1024,
            transcendentals=pair_heads * group * rows * (rows + before),
        ),
        name="attend_back",
    )(first, lo, logs, spread, q_t, d_t, q_rows, d_rows, k, k_t, v, old_k, old_k_t, old_v)


def turn(tall, cosine, sine):
    half = HEAD_DIM // 2
    parts = []
    for start in range(0, tall.shape[0], HEAD_DIM):
        a, b = tall[start : start + half], tall[start + half : start + HEAD_DIM]
        parts += [a * cosine - b * sine, b * cosine + a * sine]
    return jnp.concatenate(parts, axis=0)


def put_heads(ref, rows_of_heads):
    for h in range(ref.shape[0]):
        ref[h] = rows_of_heads[:, h * HEAD_DIM : (h + 1) * HEAD_DIM]


def project_kernel(
    x_ref, gain_ref, cos_ref, sin_ref, wq_ref, wk_ref, wv_ref,
    normed_ref, qt_ref, q_ref, kt_ref, k_ref, vt_ref, v_ref,
):
    x = x_ref[...].astype(f32)
    normed = (x * scale_of(x) * gain_ref[...].astype(f32)).astype(bf16)
    normed_ref[...] = normed
    cosine, sine = cos_ref[...], sin_ref[...]
    q_t = turn(mm(normed, wq_ref[...]).T, cosine, sine).astype(bf16).astype(f32) * score_scale
    qt_ref[...] = q_t.astype(bf16)
    put_heads(q_ref, q_t.T.astype(bf16))
    k_t = turn(dot(wk_ref[...], normed, 1, 1), cosine, sine)
    kt_ref[...] = k_t.astype(bf16)
    put_heads(k_ref, k_t.T.astype(bf16))
    v_t = dot(wv_ref[...], normed, 1, 1)
    vt_ref[...] = v_t.astype(bf16)
    put_heads(v_ref, v_t.T.astype(bf16))


def project(tokens, gain, cosine, sine, w_query, w_key, w_value):
    rows, width = tokens.shape
    tall, split = w_query.shape[1], w_key.shape[0]
    heads, pair_heads = tall // HEAD_DIM, split // HEAD_DIM
    whole = lambda shape: pl.BlockSpec(shape, lambda t: (0,) * len(shape))
    down = lambda wide: pl.BlockSpec((BLOCK, wide), lambda t: (t, 0))
    across = lambda high: pl.BlockSpec((high, BLOCK), lambda t: (0, t))
    stacked = lambda count: pl.BlockSpec((count, BLOCK, HEAD_DIM), lambda t: (0, t, 0))
    return pl.pallas_call(
        project_kernel,
        grid=(rows // BLOCK,),
        in_specs=[
            down(width), whole((1, width)), across(HEAD_DIM // 2), across(HEAD_DIM // 2),
            whole((width, tall)), whole((split, width)), whole((split, width)),
        ],
        out_specs=[
            down(width), across(tall), stacked(heads), across(split), stacked(pair_heads),
            across(split), stacked(pair_heads),
        ],
        out_shape=[
            jax.ShapeDtypeStruct((rows, width), bf16),
            jax.ShapeDtypeStruct((tall, rows), bf16),
            jax.ShapeDtypeStruct((heads, rows, HEAD_DIM), bf16),
            jax.ShapeDtypeStruct((split, rows), bf16),
            jax.ShapeDtypeStruct((pair_heads, rows, HEAD_DIM), bf16),
            jax.ShapeDtypeStruct((split, rows), bf16),
            jax.ShapeDtypeStruct((pair_heads, rows, HEAD_DIM), bf16),
        ],
        compiler_params=pltpu.CompilerParams(vmem_limit_bytes=vmem_bytes),
        cost_estimate=pl.CostEstimate(
            flops=2 * rows * width * (tall + 2 * split),
            bytes_accessed=12 * 1024 * 1024,
            transcendentals=0,
        ),
        name="project",
    )(tokens, gain, cosine, sine, w_query, w_key, w_value)


def enter_mixture_kernel(count, x_ref, gain_ref, router_ref, routes_ref, *refs):
    pieces, (hidden_ref, normed_ref, normed_t_ref, gates_ref) = refs[: 2 * count], refs[2 * count :]
    products = [
        mm(context_ref[...].astype(f32).T.astype(bf16), w_ref[...])
        for context_ref, w_ref in zip(pieces[:count], pieces[count:])
    ]
    sides = max(1, count // 2)
    projected = functools.reduce(jnp.add, products[:sides])
    if count > sides:
        projected = projected + functools.reduce(jnp.add, products[sides:])
    hidden = x_ref[...].astype(f32) + residual_scale * projected
    hidden_ref[...] = hidden
    normed = hidden * scale_of(hidden) * gain_ref[...].astype(f32)
    normed_t_ref[...] = normed.T.astype(bf16)
    normed = normed.astype(bf16)
    normed_ref[...] = normed
    logits = dot(router_ref[...], normed, 1, 1)
    expert = lax.broadcasted_iota(jnp.int32, logits.shape, 0)
    chosen = expert == routes_ref[0:1, :]
    for k in range(1, routes_ref.shape[0]):
        chosen = chosen | (expert == routes_ref[k : k + 1, :])
    logits = jnp.where(chosen, logits, masked_value)
    weights = jnp.exp(logits - jnp.max(logits, axis=0, keepdims=True))
    weights = jnp.where(chosen, weights, 0.0)
    gates_ref[...] = weights / jnp.sum(weights, axis=0, keepdims=True)


def enter_mixture(tokens, gain, router_t, routes_t, contexts, weights):
    rows, width = tokens.shape
    whole = lambda shape: pl.BlockSpec(shape, lambda t: (0,) * len(shape))
    down = lambda wide: pl.BlockSpec((BLOCK, wide), lambda t: (t, 0))
    across = lambda high: pl.BlockSpec((high, BLOCK), lambda t: (0, t))
    return pl.pallas_call(
        functools.partial(enter_mixture_kernel, len(contexts)),
        grid=(rows // BLOCK,),
        in_specs=[
            down(width), whole((1, width)), whole(router_t.shape), across(routes_t.shape[0]),
            *[across(context.shape[0]) for context in contexts],
            *[whole(weight.shape) for weight in weights],
        ],
        out_specs=[down(width), down(width), across(width), across(EXPERTS)],
        out_shape=[
            jax.ShapeDtypeStruct((rows, width), f32),
            jax.ShapeDtypeStruct((rows, width), bf16),
            jax.ShapeDtypeStruct((width, rows), bf16),
            jax.ShapeDtypeStruct((EXPERTS, rows), f32),
        ],
        compiler_params=pltpu.CompilerParams(vmem_limit_bytes=vmem_bytes),
        cost_estimate=pl.CostEstimate(
            flops=2 * rows * width * width, bytes_accessed=16 * 1024 * 1024, transcendentals=0
        ),
        name="enter_mixture",
    )(tokens, gain, router_t, routes_t, *contexts, *weights)


def enter_back_kernel(
    c_ref, own_ref, other_ref, wo_ref, ctx_ref, hidden_ref, dt_ref, d_ref, spread_ref, wo_grad_ref
):
    hidden_gradient = c_ref[...].astype(f32) + (
        own_ref[...].astype(f32) + other_ref[...].astype(f32)
    )
    hidden_ref[...] = hidden_gradient
    attention_gradient = (residual_scale * hidden_gradient).astype(bf16)
    d_t = dot(wo_ref[...], attention_gradient, 1, 1)
    dt_ref[...] = d_t.astype(bf16)
    put_heads(d_ref, d_t.T.astype(bf16))
    context_t = ctx_ref[...]
    weighed = d_t.astype(bf16).astype(f32) * context_t.astype(f32)
    for h in range(spread_ref.shape[0]):
        spread_ref[h : h + 1, :] = jnp.sum(
            weighed[h * HEAD_DIM : (h + 1) * HEAD_DIM], axis=0, keepdims=True
        )

    @pl.when(pl.program_id(0) == 0)
    def start():
        wo_grad_ref[...] = jnp.zeros_like(wo_grad_ref)

    wo_grad_ref[...] += mm(context_t, attention_gradient)


def enter_back(cotangent, own, other, w_out, context_t):
    rows, width = cotangent.shape
    tall = w_out.shape[0]
    heads = tall // HEAD_DIM
    whole = lambda shape: pl.BlockSpec(shape, lambda t: (0,) * len(shape))
    down = lambda wide: pl.BlockSpec((BLOCK, wide), lambda t: (t, 0))
    across = lambda high: pl.BlockSpec((high, BLOCK), lambda t: (0, t))
    return pl.pallas_call(
        enter_back_kernel,
        grid=(rows // BLOCK,),
        in_specs=[down(width), down(width), down(width), whole((tall, width)), across(tall)],
        out_specs=[
            down(width), across(tall),
            pl.BlockSpec((heads, BLOCK, HEAD_DIM), lambda t: (0, t, 0)),
            across(heads), whole((tall, width)),
        ],
        out_shape=[
            jax.ShapeDtypeStruct((rows, width), f32),
            jax.ShapeDtypeStruct((tall, rows), bf16),
            jax.ShapeDtypeStruct((heads, rows, HEAD_DIM), bf16),
            jax.ShapeDtypeStruct((heads, rows), f32),
            jax.ShapeDtypeStruct((tall, width), f32),
        ],
        compiler_params=pltpu.CompilerParams(vmem_limit_bytes=vmem_bytes),
        cost_estimate=pl.CostEstimate(
            flops=4 * rows * width * tall, bytes_accessed=20 * 1024 * 1024, transcendentals=0
        ),
        name="enter_back",
    )(cotangent, own, other, w_out, context_t)


def leave_back_kernel(
    core_ref, x_ref, gain_ref, cos_ref, sin_ref, wq_ref, wk_ref, wv_ref, normed_ref,
    dq_ref, dk_ref, dv_ref, more_dk_ref, more_dv_ref, wo_grad_ref, router_grad_ref, gain_two_grad_ref,
    part_ref, send_ref, keep_ref, sum_ref, gain_grad_ref,
):
    step = pl.program_id(0)
    cosine, sine = cos_ref[...], -sin_ref[...]
    dq_t = turn(dq_ref[...], cosine, sine).astype(bf16)
    dk_t = turn(dk_ref[...] + more_dk_ref[...].astype(f32), cosine, sine).astype(bf16)
    dv_t = (dv_ref[...] + more_dv_ref[...].astype(f32)).astype(bf16)
    normed = normed_ref[...]

    @pl.when(step == 0)
    def start():
        sum_ref[...] = jnp.zeros_like(sum_ref)
        gain_grad_ref[...] = jnp.zeros_like(gain_grad_ref)

    stacked = jnp.concatenate([dq_t, dk_t, dv_t], axis=0)
    sum_ref[: stacked.shape[0]] += mm(stacked, normed)
    rows_of = lambda tall: tall.astype(f32).T.astype(bf16)
    upstream = (
        dot(rows_of(dq_t), wq_ref[...], 1, 1)
        + mm(rows_of(dk_t), wk_ref[...])
        + mm(rows_of(dv_t), wv_ref[...])
    )
    x = x_ref[...].astype(f32)
    part, gain_part = norm_back(x, scale_of(x), gain_ref[...].astype(f32), upstream)
    part_ref[...] = part.astype(bf16)
    gain_grad_ref[...] += gain_part[None, :]

    @pl.when(step == pl.num_programs(0) - 1)
    def finish():
        place = stacked.shape[0]
        sum_ref[place : place + wo_grad_ref.shape[0]] = wo_grad_ref[...]
        place += wo_grad_ref.shape[0]
        sum_ref[place : place + EXPERTS] = router_grad_ref[...]
        place += EXPERTS
        sum_ref[place : place + 1] = gain_two_grad_ref[...]
        sum_ref[place + 1 : place + 2] = gain_grad_ref[...]
        high = keep_ref.shape[0]
        send_from = pl.multiple_of((1 - core_ref[0]) * high, 16)
        keep_from = pl.multiple_of(core_ref[0] * high, 16)
        send_ref[...] = sum_ref[pl.ds(send_from, high)].astype(bf16)
        keep_ref[...] = sum_ref[pl.ds(keep_from, high)].astype(bf16)


def leave_back(
    core, high, tokens, gain, cosine, sine, w_query, w_key, w_value, normed, dq_t, dk_t, dv_t,
    more_dk, more_dv, w_out_gradient, router_gradient, second_gain_gradient,
):
    rows, width = tokens.shape
    tall, split = w_query.shape[1], w_key.shape[0]
    whole = lambda shape: pl.BlockSpec(shape, lambda t, s: (0,) * len(shape))
    down = lambda wide: pl.BlockSpec((BLOCK, wide), lambda t, s: (t, 0))
    across = lambda high: pl.BlockSpec((high, BLOCK), lambda t, s: (0, t))
    return pl.pallas_call(
        leave_back_kernel,
        grid_spec=pltpu.PrefetchScalarGridSpec(
            num_scalar_prefetch=1,
            grid=(rows // BLOCK,),
            in_specs=[
                down(width), whole((1, width)), across(HEAD_DIM // 2), across(HEAD_DIM // 2),
                whole((width, tall)), whole((split, width)), whole((split, width)), down(width),
                across(tall), across(split), across(split), across(split), across(split),
                whole((tall, width)), whole((EXPERTS, width)), whole((1, width)),
            ],
            out_specs=[down(width), whole((high, width)), whole((high, width))],
            scratch_shapes=[pltpu.VMEM((2 * high, width), f32), pltpu.VMEM((1, width), f32)],
        ),
        out_shape=[
            jax.ShapeDtypeStruct((rows, width), bf16),
            jax.ShapeDtypeStruct((high, width), bf16),
            jax.ShapeDtypeStruct((high, width), bf16),
        ],
        compiler_params=pltpu.CompilerParams(vmem_limit_bytes=vmem_bytes),
        cost_estimate=pl.CostEstimate(
            flops=4 * rows * width * (tall + 2 * split),
            bytes_accessed=24 * 1024 * 1024,
            transcendentals=0,
        ),
        name="leave_back",
    )(
        core, tokens, gain, cosine, sine, w_query, w_key, w_value, normed, dq_t, dk_t, dv_t,
        more_dk, more_dv, w_out_gradient, router_gradient, second_gain_gradient,
    )


def expert_kernel(
    adds, ids_ref, gates_ref, xt_hbm, ct_hbm, x_hbm, c_hbm, up_ref, down_ref, *refs
):
    if adds:
        more_ref, *refs = refs
    _, _, _, grad_ref, up_grad_ref, act_ref, gate_grad_ref, *refs = refs
    xt_ref, ct_ref, x_ref, c_ref, arrived = refs
    copies = [
        pltpu.make_async_copy(source, target, arrived.at[place])
        for place, (source, target) in enumerate(
            [(xt_hbm, xt_ref), (ct_hbm, ct_ref), (x_hbm, x_ref), (c_hbm, c_ref)]
        )
    ]
    first_step = pl.program_id(0) == 0

    @pl.when(first_step)
    def begin():
        for copy in copies:
            copy.start()
        copies[0].wait()
        copies[1].wait()

    rows = x_ref.shape[0]
    chunk = min(BLOCK, rows)
    for part in range(rows // chunk):
        cut = pl.ds(part * chunk, chunk)
        xt = xt_ref[:, cut]
        gate = mm(up_ref[0, 0], xt)
        up = mm(up_ref[0, 1], xt)
        active_grad = mm(down_ref[0], ct_ref[:, cut])
        share = 1.0 / (1.0 + jnp.exp(-gate))
        silu = gate * share
        active = silu * up
        weight = gates_ref[0, :, cut] * residual_scale
        gate_grad_ref[0, 0, :, cut] = residual_scale * jnp.sum(
            active * active_grad, axis=0, keepdims=True
        )
        for place in range(1, gate_grad_ref.shape[0]):
            gate_grad_ref[place, 0, :, cut] = jnp.zeros((1, chunk), f32)
        active_grad = active_grad * weight
        act_ref[0, :, cut] = (active * weight).astype(bf16)
        up_grad_ref[0, 0, :, cut] = (
            active_grad * up * (share + silu * (1.0 - share))
        ).astype(bf16)
        up_grad_ref[0, 1, :, cut] = (active_grad * silu).astype(bf16)

    def put(place, total):
        if adds:
            total = total + more_ref[0, place].astype(f32)
        grad_ref[0, place] = total.astype(bf16)

    @pl.when(first_step)
    def complete():
        copies[2].wait()
        copies[3].wait()

    x = x_ref[...]
    put(0, mm(up_grad_ref[0, 0], x))
    put(1, mm(up_grad_ref[0, 1], x))
    put(2, mm(act_ref[0], c_ref[...]))


def expert_step(ids, half, halves, gates, xt, x, ct, c, w_up, w_down, more, old):
    count = ids.shape[0]
    rows, width = x.shape
    units = w_down.shape[1] // 2 * halves
    any_place = pl.BlockSpec(memory_space=pl.ANY)
    fresh = old is None
    adds = more is not None
    each = pl.BlockSpec((1, 3, units, width), lambda e, s: (e, 0, 0, 0))
    if fresh:
        old = (jnp.zeros((8, 128), f32),) * 3
    return pl.pallas_call(
        functools.partial(expert_kernel, adds),
        grid_spec=pltpu.PrefetchScalarGridSpec(
            num_scalar_prefetch=1,
            grid=(count,),
            in_specs=[
                pl.BlockSpec((1, 1, rows), lambda e, s: (s[e], 0, 0)),
                any_place,
                any_place,
                any_place,
                any_place,
                pl.BlockSpec((1, 2, units, width), lambda e, s: (s[e], 0, half, 0)),
                pl.BlockSpec((1, units, width), lambda e, s: (s[e], half, 0)),
                *([each] if adds else []),
                any_place,
                any_place,
                any_place,
            ],
            out_specs=[
                each,
                pl.BlockSpec((1, 2, units, rows), lambda e, s: (s[e], 0, half, 0)),
                pl.BlockSpec((1, units, rows), lambda e, s: (s[e], half, 0)),
                pl.BlockSpec((halves, 1, 1, rows), lambda e, s: (half, s[e], 0, 0)),
            ],
            scratch_shapes=[
                pltpu.VMEM((width, rows), bf16),
                pltpu.VMEM((width, rows), bf16),
                pltpu.VMEM((rows, width), bf16),
                pltpu.VMEM((rows, width), bf16),
                pltpu.SemaphoreType.DMA((4,)),
            ],
        ),
        out_shape=[
            jax.ShapeDtypeStruct((count, 3, units, width), bf16),
            jax.ShapeDtypeStruct((EXPERTS, 2, w_down.shape[1], rows), bf16),
            jax.ShapeDtypeStruct((EXPERTS, w_down.shape[1], rows), bf16),
            jax.ShapeDtypeStruct((2, EXPERTS, 1, rows), f32),
        ],
        input_output_aliases={} if fresh else {8 + adds: 1, 9 + adds: 2, 10 + adds: 3},
        compiler_params=pltpu.CompilerParams(vmem_limit_bytes=vmem_bytes),
        cost_estimate=pl.CostEstimate(
            flops=count * 12 * rows * width * units,
            bytes_accessed=count * units * width * 12 + 8 * rows * width,
            transcendentals=count * units * rows,
        ),
        name="experts",
    )(ids, gates, xt, ct, x, c, w_up, w_down, *([more] if adds else []), *old)


def from_other_half(shard):
    return lax.ppermute(shard, "tensor", [(0, 1), (1, 0)])


def gathered(shard):
    if lax.axis_size("tensor") != 2:
        return [lax.all_gather(shard, "tensor", axis=0, tiled=True)]
    return [shard, from_other_half(shard)]


def both_parts(part):
    if lax.axis_size("tensor") != 2:
        return lax.psum(part, "tensor"), jnp.zeros_like(part)
    return part, from_other_half(part)


def summed_parts(part):
    low = part.astype(bf16)
    if lax.axis_size("tensor") != 2:
        return lax.psum(low, "tensor").astype(f32)
    return low.astype(f32) + from_other_half(low).astype(f32)


def chip_order(chips):
    there = [2 * z for z in range(chips // 2)]
    return there + [chip + 1 for chip in reversed(there)]


def chunk_experts(device, peers, number):
    order = jnp.array(chip_order(peers // 2), jnp.int32)
    each = EXPERTS // peers
    core = device % 2

    def owned(side):
        chips = jnp.where(side == 0, order, order[::-1])
        return (2 * chips + side) * each + number

    return owned(1 - core).astype(jnp.int32), owned(core).astype(jnp.int32)


def chip_rings():
    order = chip_order(lax.axis_size("dp") // 2)
    return [[2 * chip for chip in order], [2 * chip + 1 for chip in reversed(order)]]


def to_owner(chip_sum):
    return lax.psum_scatter(
        chip_sum, "dp", scatter_dimension=0, axis_index_groups=chip_rings(), tiled=True
    )


def summed_over_tokens(send, keep, beside_one, beside_two):
    swap = [(i, i ^ 1) for i in range(lax.axis_size("dp"))]
    received = lax.ppermute(send, "dp", swap)
    half = (keep.astype(f32) + received.astype(f32)).astype(bf16)
    rings = chip_rings()
    half = lax.psum_scatter(half, "dp", scatter_dimension=0, axis_index_groups=rings, tiled=True)
    half, beside_one = lax.optimization_barrier((half, beside_one))
    half = lax.all_gather(half, "dp", axis=0, axis_index_groups=rings, tiled=True)
    half, beside_two = lax.optimization_barrier((half, beside_two))
    other = lax.ppermute(half, "dp", swap)
    is_first = lax.axis_index("dp") % 2 == 0
    low, high = jnp.where(is_first, half, other), jnp.where(is_first, other, half)
    return jnp.concatenate([low, high], axis=0), beside_one, beside_two


def angles(position):
    inverse = rope_base ** (-2.0 * jnp.arange(HEAD_DIM // 2, dtype=f32) / HEAD_DIM)
    angle = inverse[:, None] * position.astype(f32)[None, :]
    return jnp.cos(angle), jnp.sin(angle)


def scale_of(values):
    return lax.rsqrt(jnp.mean(values * values, axis=-1, keepdims=True) + epsilon)


def norm_back(values, scale, gain, upstream):
    pulled = gain * upstream
    slope = jnp.mean(pulled * values, axis=-1, keepdims=True)
    return (
        scale * pulled - values * (scale * scale * scale * slope),
        jnp.sum(upstream * values * scale, axis=0),
    )


def on_device(
    tokens, doc_ids, routes, attention_gain, w_query, w_key, w_value, w_out, mixture_gain,
    w_router, expert_gate_up, expert_down, out_cotangent,
):
    rows, width = tokens.shape
    peers = lax.axis_size("dp")
    device = lax.axis_index("dp")
    pair_heads = w_key.shape[0] // HEAD_DIM
    group = w_query.shape[1] // w_key.shape[0]
    first = device * rows
    chunks = EXPERTS // peers
    w_out_parts = gathered(w_out)

    docs = lax.dynamic_slice_in_dim(doc_ids, first, rows)
    docs_before = lax.dynamic_slice_in_dim(doc_ids, jnp.maximum(device - 1, 0) * rows, rows)
    docs_before = jnp.where(device > 0, docs_before, -1)
    docs_window = jnp.concatenate([docs_before, docs])
    lo = jnp.sum((docs_window[:, None] < docs[None, :]).astype(jnp.int32), axis=0)
    first_block = lo[::BLOCK] // BLOCK
    lo = lo[None, :]

    position = (first + jnp.arange(rows, dtype=jnp.int32)) % SEQ_LEN
    cosine, sine = angles(position)
    gain_one = attention_gain[None, :]
    normed_attention, q_t, q_rows, k_t, k_rows, v_t, v_rows = project(
        tokens, gain_one, cosine, sine, w_query, w_key, w_value
    )
    to_next = [(i, i + 1) for i in range(0, peers, 2)]
    before = SEQ_LEN - rows
    old_k_t = lax.ppermute(k_t, "dp", to_next)
    old_v_t = lax.ppermute(v_t, "dp", to_next)
    across = lambda tall: jnp.swapaxes(tall.reshape(pair_heads, HEAD_DIM, before), 1, 2)
    old_k_rows, old_v_rows = across(old_k_t), across(old_v_t)

    calls = 2 if pair_heads % 2 == 0 else 1
    here = pair_heads // calls
    pieces = [
        attend(
            first_block, lo, q_t, k_rows, v_t, old_k_rows, old_v_t, group, call * here, here
        )
        for call in range(calls)
    ]
    context_parts = [gathered(piece[0]) for piece in pieces]
    contexts = [parts[side] for side in range(len(context_parts[0])) for parts in context_parts]
    context_t = jnp.concatenate([piece[0] for piece in pieces], axis=0)
    logs = jnp.concatenate([piece[1] for piece in pieces], axis=0)
    w_out_pieces = [
        piece for part in w_out_parts for piece in jnp.split(part, calls, axis=0)
    ]
    hidden, normed_mixture, normed_t, gates = enter_mixture(
        tokens, mixture_gain[None, :], w_router.T, routes.T, contexts, w_out_pieces
    )
    gain_two = mixture_gain.astype(f32)
    scale_two = scale_of(hidden)

    upstream_t = out_cotangent.T
    swap_cores = [(i, i ^ 1) for i in range(peers)]
    shares, arrived, old = [], [], None
    pieces = [(number, half, 1) for number in range(chunks) for half in range(2)]

    def run_experts(piece, side, more):
        ids = chunk_experts(device, peers, piece[0])[side]
        return expert_step(
            ids, piece[1], piece[2], gates[:, None, :], normed_t, normed_mixture, upstream_t, out_cotangent,
            expert_gate_up, expert_down, more, old,
        )

    for number in range(len(pieces) + 1):
        if number < len(pieces):
            send, *old = run_experts(pieces[number], 0, None)
            arrived.append(lax.ppermute(send, "dp", swap_cores))
        if number > 0:
            chip_sum, *old = run_experts(pieces[number - 1], 1, arrived[number - 1])
            shares.append(to_owner(chip_sum))
    up_grad, act, gates_gradient = old
    gates_gradient = gates_gradient[0, :, 0] + gates_gradient[1, :, 0]
    units = expert_down.shape[1]
    wide = EXPERTS * units

    logits_gradient = gates * (
        gates_gradient - jnp.sum(gates * gates_gradient, axis=0, keepdims=True)
    )
    logits_low = logits_gradient.astype(bf16)
    router_gradient = mm(logits_low, normed_mixture)
    up_grad = up_grad.reshape(2 * wide, rows)
    w_up = expert_gate_up.reshape(2 * wide, width)
    own_parts, other_parts, gain_parts = [], [], []
    for start in range(0, rows, rows // 2):
        cut = slice(start, start + rows // 2)
        if start > 0:
            up_grad, own_parts[0] = lax.optimization_barrier((up_grad, own_parts[0]))
        normed_gradient = dot(up_grad[:, cut], w_up, 0, 0) + dot(logits_low[:, cut], w_router, 0, 1)
        part, gain_part = norm_back(hidden[cut], scale_two[cut], gain_two, normed_gradient)
        part = part.astype(bf16)
        if start > 0:
            part, act, other_parts[0] = lax.optimization_barrier((part, act, other_parts[0]))
        own, other = both_parts(part)
        own_parts.append(own)
        other_parts.append(other)
        gain_parts.append(gain_part)
    second_gain_part = gain_parts[0] + gain_parts[1]

    mixture_part = dot(act.reshape(wide, rows), expert_down.reshape(wide, width), 0, 0)
    mixture_low = mixture_part.astype(bf16)
    own_part = jnp.concatenate(own_parts, axis=0)
    other_part = jnp.concatenate(other_parts, axis=0)
    own_part, other_part, mixture_low = lax.optimization_barrier(
        (own_part, other_part, mixture_low)
    )
    mixture_own, mixture_other = both_parts(mixture_low)

    hidden_gradient, d_t, d_rows, spread, w_out_gradient = enter_back(
        out_cotangent, own_part, other_part, w_out, context_t
    )
    by_group = lambda rows_of_heads: rows_of_heads.reshape(pair_heads, group, rows, HEAD_DIM)
    dq_t, dk_t, dv_t, old_dk, old_dv = attend_back(
        first_block, lo, logs, spread.reshape(pair_heads, group, rows), q_t, d_t, by_group(q_rows),
        by_group(d_rows), k_rows, k_t, v_rows, old_k_rows, old_k_t, old_v_rows,
    )
    to_previous = [(i + 1, i) for i in range(0, peers, 2)]
    more_dk = lax.ppermute(old_dk, "dp", to_previous)
    more_dv = lax.ppermute(old_dv, "dp", to_previous)
    dq_t, mixture_other, *shares[:-2] = lax.optimization_barrier(
        (dq_t, mixture_other, *shares[:-2])
    )
    tall, split = w_query.shape[1], w_key.shape[0]
    ends = [tall, tall + split, tall + 2 * split, 2 * tall + 2 * split, 2 * tall + 2 * split + EXPERTS]
    high = -(-(ends[-1] + 2) // (16 * peers)) * 8 * peers
    input_part, send, keep = leave_back(
        (device % 2)[None].astype(jnp.int32), high, tokens, gain_one, cosine, sine, w_query, w_key,
        w_value, normed_attention, dq_t, dk_t, dv_t, more_dk, more_dv, w_out_gradient,
        router_gradient, second_gain_part[None, :],
    )
    swapped = [both_parts(part) for part in jnp.split(input_part, 2, axis=0)]
    *shares[-2:], keep = lax.optimization_barrier((*shares[-2:], keep))
    mixed = (hidden + (mixture_own.astype(f32) + mixture_other.astype(f32))).astype(bf16)
    shares = [
        jnp.concatenate(shares[start : start + 2], axis=2) for start in range(0, len(shares), 2)
    ]
    experts_gradient = jnp.concatenate(shares, axis=0).astype(f32)
    up_gradient, down_gradient = experts_gradient[:, :2], experts_gradient[:, 2]
    (own_one, other_one), (own_two, other_two) = swapped
    gradients, (other_one, mixed, up_gradient, down_gradient), other_two = summed_over_tokens(
        send, keep, (other_one, mixed, up_gradient, down_gradient), other_two
    )
    input_sum = jnp.concatenate(
        [own_one.astype(f32) + other_one.astype(f32), own_two.astype(f32) + other_two.astype(f32)],
        axis=0,
    )
    tokens_gradient = hidden_gradient + input_sum
    w_q, w_k, w_v, w_o = jnp.split(gradients[: ends[3]].astype(f32), ends[:3], axis=0)
    small = summed_parts(gradients[ends[3] :])
    router, gains = small[:EXPERTS], small[EXPERTS:]
    return (
        mixed, tokens_gradient.astype(bf16), gains[1], w_q.T, w_k, w_v, w_o, gains[0], router.T,
        up_gradient, down_gradient,
    )


def solution(mesh):
    placed = (
        P("dp", None),
        P(),
        P("dp", None),
        P(),
        P(None, "tensor"),
        P("tensor", None),
        P("tensor", None),
        P("tensor", None),
        P(),
        P(),
        P(None, None, "tensor", None),
        P(None, "tensor", None),
        P("dp", None),
    )
    return jax.shard_map(
        on_device,
        mesh=mesh,
        in_specs=placed,
        out_specs=(
            P("dp", None),
            P("dp", None),
            P(),
            P(None, "tensor"),
            P("tensor", None),
            P("tensor", None),
            P("tensor", None),
            P(),
            P(),
            P("dp", None, "tensor", None),
            P("dp", "tensor", None),
        ),
        check_vma=False,
    )
```

```python
import functools

import jax
import jax.numpy as jnp
from jax import lax
from jax.experimental import pallas as pl
from jax.experimental.pallas import tpu as pltpu
from jax.sharding import PartitionSpec as P

HEAD_DIM = 64
EXPERTS = 32
SEQ_LEN = 2048
BLOCK = 256

epsilon = 1e-06
score_scale = 0.015625
residual_scale = 0.22
rope_base = 10000.0
masked_value = -1e30
vmem_bytes = 60 * 1024 * 1024
expert_vmem_bytes = 32 * 1024 * 1024
f32 = jnp.float32
bf16 = jnp.bfloat16


def dot(left, right, left_dim, right_dim):
    return lax.dot_general(
        left, right, (((left_dim,), (right_dim,)), ((), ())), preferred_element_type=f32
    )


def mm(left, right):
    return jnp.dot(left, right, preferred_element_type=f32)


def block_mask(lo, hi, start, lanes):
    place = start + lax.broadcasted_iota(jnp.int32, (BLOCK, lanes), 0)
    return (place >= lo) & (place <= hi)


def window_of(lo_ref, block, before, group):
    cut = pl.ds(block * BLOCK, BLOCK)
    lo = lo_ref[:, cut]
    hi = before + block * BLOCK + lax.broadcasted_iota(jnp.int32, (1, BLOCK), 1)
    return (
        jnp.concatenate([lo] * group, axis=1),
        jnp.concatenate([hi] * group, axis=1),
    )


def heads_side_by_side(ref, block, group):
    cut = pl.ds(block * BLOCK, BLOCK)
    return jnp.concatenate(
        [ref[h * HEAD_DIM : (h + 1) * HEAD_DIM, cut] for h in range(group)], axis=1
    )


def heads_one_above(ref, j, block, group):
    cut = pl.ds(block * BLOCK, BLOCK)
    return jnp.concatenate([ref[j, h, cut, :] for h in range(group)], axis=0)


def attend_kernel(
    group, first_ref, lo_ref, qt_ref, k_ref, vt_ref, old_k_ref, old_vt_ref, out_ref, log_ref
):
    lanes = group * BLOCK
    together, before, _ = old_k_ref.shape
    tall = group * HEAD_DIM
    passed = before // BLOCK
    for block in range(qt_ref.shape[1] // BLOCK):
        lo, hi = window_of(lo_ref, block, before, group)
        queries = [
            heads_side_by_side(qt_ref.at[pl.ds(j * tall, tall)], block, group)
            for j in range(together)
        ]

        def step(keys_ref, values_ref, offset, number, carry):
            start = pl.multiple_of(number * BLOCK, BLOCK)
            here = pl.ds(start, BLOCK)
            mask = block_mask(lo, hi, offset + start, lanes)
            result = []
            for j, (peak, total, acc) in enumerate(carry):
                scores = mm(keys_ref[j, here, :], queries[j])
                scores = jnp.where(mask, scores, masked_value)
                top = jnp.maximum(peak, jnp.max(scores, axis=0, keepdims=True))
                weights = jnp.exp(scores - top)
                fade = jnp.exp(peak - top)
                total = total * fade + jnp.sum(weights, axis=0, keepdims=True)
                values = values_ref[j * HEAD_DIM : (j + 1) * HEAD_DIM, here]
                result.append((top, total, acc * fade + mm(values, weights.astype(bf16))))
            return tuple(result)

        first = first_ref[block]
        nothing = (
            jnp.full((1, lanes), masked_value, f32),
            jnp.zeros((1, lanes), f32),
            jnp.zeros((HEAD_DIM, lanes), f32),
        )
        carry = lax.fori_loop(
            first, passed, functools.partial(step, old_k_ref, old_vt_ref, 0), (nothing,) * together
        )
        carry = lax.fori_loop(
            jnp.maximum(first - passed, 0),
            block + 1,
            functools.partial(step, k_ref, vt_ref, before),
            carry,
        )
        cut = pl.ds(block * BLOCK, BLOCK)
        for j, (peak, total, acc) in enumerate(carry):
            result = (acc / total).astype(bf16)
            logs = peak + jnp.log(total)
            for h in range(group):
                side = slice(h * BLOCK, (h + 1) * BLOCK)
                high = j * tall + h * HEAD_DIM
                out_ref[high : high + HEAD_DIM, cut] = result[:, side]
                log_ref[j, h : h + 1, cut] = logs[:, side]


def attend(first, lo, q_t, k, v_t, old_k, old_v_t, group, base, pair_heads):
    rows = k.shape[1]
    before = old_k.shape[1]
    together = 1
    start = base // together
    tall = together * group * HEAD_DIM
    split = together * HEAD_DIM
    by_head = lambda h, s: (start + h, 0, 0)
    flat = lambda h, s: (start + h, 0)
    return pl.pallas_call(
        functools.partial(attend_kernel, group),
        grid_spec=pltpu.PrefetchScalarGridSpec(
            num_scalar_prefetch=1,
            grid=(pair_heads // together,),
            in_specs=[
                pl.BlockSpec((1, rows), lambda h, s: (0, 0)),
                pl.BlockSpec((tall, rows), flat),
                pl.BlockSpec((together, rows, HEAD_DIM), by_head),
                pl.BlockSpec((split, rows), flat),
                pl.BlockSpec((together, before, HEAD_DIM), by_head),
                pl.BlockSpec((split, before), flat),
            ],
            out_specs=[
                pl.BlockSpec((tall, rows), lambda h, s: (h, 0)),
                pl.BlockSpec((together, group, rows), lambda h, s: (h, 0, 0)),
            ],
        ),
        out_shape=[
            jax.ShapeDtypeStruct((pair_heads * group * HEAD_DIM, rows), bf16),
            jax.ShapeDtypeStruct((pair_heads, group, rows), f32),
        ],
        compiler_params=pltpu.CompilerParams(vmem_limit_bytes=vmem_bytes),
        cost_estimate=pl.CostEstimate(
            flops=pair_heads * group * rows * (rows + before) * 512,
            bytes_accessed=8 * 1024 * 1024,
            transcendentals=pair_heads * group * rows * (rows + before),
        ),
        name="attend",
    )(first, lo, q_t, k, v_t, old_k, old_v_t)


def attend_back_kernel(
    group,
    first_ref, lo_ref, log_ref, spread_ref, qt_ref, dt_ref, q_ref, d_ref, k_ref, kt_ref, v_ref,
    old_k_ref, old_kt_ref, old_v_ref,
    dq_ref, dk_ref, dv_ref, old_dk_ref, old_dv_ref, pair_ref, old_pair_ref,
):
    lanes = group * BLOCK
    together, before, _ = old_k_ref.shape
    tall = group * HEAD_DIM
    passed = before // BLOCK
    pair_ref[...] = jnp.zeros_like(pair_ref)
    old_pair_ref[...] = jnp.zeros_like(old_pair_ref)
    for block in range(qt_ref.shape[1] // BLOCK):
        cut = pl.ds(block * BLOCK, BLOCK)
        lo, hi = window_of(lo_ref, block, before, group)
        heads = []
        for j in range(together):
            here = pl.ds(j * tall, tall)
            query_rows = heads_one_above(q_ref, j, block, group)
            upstream_rows = heads_one_above(d_ref, j, block, group)
            nothing = jnp.zeros_like(query_rows)
            both_rows = jnp.concatenate(
                [
                    jnp.concatenate([query_rows, nothing], axis=1),
                    jnp.concatenate([nothing, upstream_rows], axis=1),
                ],
                axis=0,
            )
            heads.append(
                (
                    heads_side_by_side(qt_ref.at[here], block, group),
                    heads_side_by_side(dt_ref.at[here], block, group),
                    both_rows,
                    jnp.concatenate([log_ref[j, h : h + 1, cut] for h in range(group)], axis=1),
                    jnp.concatenate([spread_ref[j, h : h + 1, cut] for h in range(group)], axis=1),
                )
            )

        def step(keys_ref, keys_t_ref, values_ref, sums_ref, offset, number, sums):
            start = pl.multiple_of(number * BLOCK, BLOCK)
            here = pl.ds(start, BLOCK)
            mask = block_mask(lo, hi, start + offset, lanes)
            result = []
            for j, (query, upstream, both_rows, logs, spread) in enumerate(heads):
                scores = mm(keys_ref[j, here, :], query)
                probs = jnp.exp(jnp.where(mask, scores - logs, masked_value))
                change = mm(values_ref[j, here, :], upstream)
                scores_change = (probs * (change - spread)).astype(bf16)
                sums_ref[j, here, :] += mm(
                    jnp.concatenate([scores_change, probs.astype(bf16)], axis=1), both_rows
                )
                keys_t = keys_t_ref[j * HEAD_DIM : (j + 1) * HEAD_DIM, here]
                result.append(sums[j] + mm(keys_t, scores_change))
            return tuple(result)

        first = first_ref[block]
        sums = (jnp.zeros((HEAD_DIM, lanes), f32),) * together
        earlier = functools.partial(step, old_k_ref, old_kt_ref, old_v_ref, old_pair_ref, 0)
        sums = lax.fori_loop(first, passed, earlier, sums)
        own = functools.partial(step, k_ref, kt_ref, v_ref, pair_ref, before)
        sums = lax.fori_loop(jnp.maximum(first - passed, 0), block + 1, own, sums)
        for j in range(together):
            for h in range(group):
                high = j * tall + h * HEAD_DIM
                dq_ref[high : high + HEAD_DIM, cut] = (
                    sums[j][:, h * BLOCK : (h + 1) * BLOCK] * score_scale
                )
    for j in range(together):
        side = slice(j * HEAD_DIM, (j + 1) * HEAD_DIM)
        pair_t = pair_ref[j].T
        dk_ref[side] = pair_t[:HEAD_DIM]
        dv_ref[side] = pair_t[HEAD_DIM:]
        pair_t = old_pair_ref[j].T
        old_dk_ref[side] = pair_t[:HEAD_DIM].astype(bf16)
        old_dv_ref[side] = pair_t[HEAD_DIM:].astype(bf16)


def attend_back(
    first, lo, logs, spread, q_t, d_t, q_rows, d_rows, k, k_t, v, old_k, old_k_t, old_v
):
    pair_heads, before, _ = old_k.shape
    group, rows = q_rows.shape[1:3]
    together = 2 if pair_heads % 2 == 0 else 1
    tall = together * group * HEAD_DIM
    split = together * HEAD_DIM
    by_head = lambda h, s: (h, 0, 0)
    flat = lambda h, s: (h, 0)
    return pl.pallas_call(
        functools.partial(attend_back_kernel, group),
        grid_spec=pltpu.PrefetchScalarGridSpec(
            num_scalar_prefetch=1,
            grid=(pair_heads // together,),
            in_specs=[
                pl.BlockSpec((1, rows), lambda h, s: (0, 0)),
                pl.BlockSpec((together, group, rows), by_head),
                pl.BlockSpec((together, group, rows), by_head),
                pl.BlockSpec((tall, rows), flat),
                pl.BlockSpec((tall, rows), flat),
                pl.BlockSpec((together, group, rows, HEAD_DIM), lambda h, s: (h, 0, 0, 0)),
                pl.BlockSpec((together, group, rows, HEAD_DIM), lambda h, s: (h, 0, 0, 0)),
                pl.BlockSpec((together, rows, HEAD_DIM), by_head),
                pl.BlockSpec((split, rows), flat),
                pl.BlockSpec((together, rows, HEAD_DIM), by_head),
                pl.BlockSpec((together, before, HEAD_DIM), by_head),
                pl.BlockSpec((split, before), flat),
                pl.BlockSpec((together, before, HEAD_DIM), by_head),
            ],
            out_specs=[
                pl.BlockSpec((tall, rows), flat),
                pl.BlockSpec((split, rows), flat),
                pl.BlockSpec((split, rows), flat),
                pl.BlockSpec((split, before), flat),
                pl.BlockSpec((split, before), flat),
            ],
            scratch_shapes=[
                pltpu.VMEM((together, rows, 2 * HEAD_DIM), f32),
                pltpu.VMEM((together, before, 2 * HEAD_DIM), f32),
            ],
        ),
        out_shape=[
            jax.ShapeDtypeStruct((pair_heads * group * HEAD_DIM, rows), f32),
            jax.ShapeDtypeStruct((pair_heads * HEAD_DIM, rows), f32),
            jax.ShapeDtypeStruct((pair_heads * HEAD_DIM, rows), f32),
            jax.ShapeDtypeStruct((pair_heads * HEAD_DIM, before), bf16),
            jax.ShapeDtypeStruct((pair_heads * HEAD_DIM, before), bf16),
        ],
        compiler_params=pltpu.CompilerParams(vmem_limit_bytes=vmem_bytes),
        cost_estimate=pl.CostEstimate(
            flops=pair_heads * group * rows * (rows + before) * 1280,
            bytes_accessed=16 * 1024 * 1024,
            transcendentals=pair_heads * group * rows * (rows + before),
        ),
        name="attend_back",
    )(first, lo, logs, spread, q_t, d_t, q_rows, d_rows, k, k_t, v, old_k, old_k_t, old_v)


def turn(tall, cosine, sine):
    half = HEAD_DIM // 2
    parts = []
    for start in range(0, tall.shape[0], HEAD_DIM):
        a, b = tall[start : start + half], tall[start + half : start + HEAD_DIM]
        parts += [a * cosine - b * sine, b * cosine + a * sine]
    return jnp.concatenate(parts, axis=0)


def put_heads(ref, rows_of_heads):
    for h in range(ref.shape[0]):
        ref[h] = rows_of_heads[:, h * HEAD_DIM : (h + 1) * HEAD_DIM]


def project_kernel(
    x_ref, gain_ref, cos_ref, sin_ref, wq_ref, wk_ref, wv_ref,
    normed_ref, qt_ref, q_ref, kt_ref, k_ref, vt_ref, v_ref,
):
    x = x_ref[...].astype(f32)
    normed = (x * scale_of(x) * gain_ref[...].astype(f32)).astype(bf16)
    normed_ref[...] = normed
    cosine, sine = cos_ref[...], sin_ref[...]
    q_t = turn(mm(normed, wq_ref[...]).T, cosine, sine).astype(bf16).astype(f32) * score_scale
    qt_ref[...] = q_t.astype(bf16)
    put_heads(q_ref, q_t.T.astype(bf16))
    k_t = turn(dot(wk_ref[...], normed, 1, 1), cosine, sine)
    kt_ref[...] = k_t.astype(bf16)
    put_heads(k_ref, k_t.T.astype(bf16))
    v_t = dot(wv_ref[...], normed, 1, 1)
    vt_ref[...] = v_t.astype(bf16)
    put_heads(v_ref, v_t.T.astype(bf16))


def project(tokens, gain, cosine, sine, w_query, w_key, w_value):
    rows, width = tokens.shape
    tall, split = w_query.shape[1], w_key.shape[0]
    heads, pair_heads = tall // HEAD_DIM, split // HEAD_DIM
    whole = lambda shape: pl.BlockSpec(shape, lambda t: (0,) * len(shape))
    down = lambda wide: pl.BlockSpec((BLOCK, wide), lambda t: (t, 0))
    across = lambda high: pl.BlockSpec((high, BLOCK), lambda t: (0, t))
    stacked = lambda count: pl.BlockSpec((count, BLOCK, HEAD_DIM), lambda t: (0, t, 0))
    return pl.pallas_call(
        project_kernel,
        grid=(rows // BLOCK,),
        in_specs=[
            down(width), whole((1, width)), across(HEAD_DIM // 2), across(HEAD_DIM // 2),
            whole((width, tall)), whole((split, width)), whole((split, width)),
        ],
        out_specs=[
            down(width), across(tall), stacked(heads), across(split), stacked(pair_heads),
            across(split), stacked(pair_heads),
        ],
        out_shape=[
            jax.ShapeDtypeStruct((rows, width), bf16),
            jax.ShapeDtypeStruct((tall, rows), bf16),
            jax.ShapeDtypeStruct((heads, rows, HEAD_DIM), bf16),
            jax.ShapeDtypeStruct((split, rows), bf16),
            jax.ShapeDtypeStruct((pair_heads, rows, HEAD_DIM), bf16),
            jax.ShapeDtypeStruct((split, rows), bf16),
            jax.ShapeDtypeStruct((pair_heads, rows, HEAD_DIM), bf16),
        ],
        compiler_params=pltpu.CompilerParams(vmem_limit_bytes=vmem_bytes),
        cost_estimate=pl.CostEstimate(
            flops=2 * rows * width * (tall + 2 * split),
            bytes_accessed=12 * 1024 * 1024,
            transcendentals=0,
        ),
        name="project",
    )(tokens, gain, cosine, sine, w_query, w_key, w_value)


def enter_mixture_kernel(count, x_ref, gain_ref, router_ref, routes_ref, *refs):
    pieces, (hidden_ref, normed_ref, normed_t_ref, gates_ref) = refs[: 2 * count], refs[2 * count :]
    products = [
        mm(context_ref[...].astype(f32).T.astype(bf16), w_ref[...])
        for context_ref, w_ref in zip(pieces[:count], pieces[count:])
    ]
    sides = max(1, count // 2)
    projected = functools.reduce(jnp.add, products[:sides])
    if count > sides:
        projected = projected + functools.reduce(jnp.add, products[sides:])
    hidden = x_ref[...].astype(f32) + residual_scale * projected
    hidden_ref[...] = hidden
    normed = hidden * scale_of(hidden) * gain_ref[...].astype(f32)
    normed_t_ref[...] = normed.T.astype(bf16)
    normed = normed.astype(bf16)
    normed_ref[...] = normed
    logits = dot(router_ref[...], normed, 1, 1)
    expert = lax.broadcasted_iota(jnp.int32, logits.shape, 0)
    chosen = expert == routes_ref[0:1, :]
    for k in range(1, routes_ref.shape[0]):
        chosen = chosen | (expert == routes_ref[k : k + 1, :])
    logits = jnp.where(chosen, logits, masked_value)
    weights = jnp.exp(logits - jnp.max(logits, axis=0, keepdims=True))
    weights = jnp.where(chosen, weights, 0.0)
    gates_ref[...] = weights / jnp.sum(weights, axis=0, keepdims=True)


def enter_mixture(tokens, gain, router_t, routes_t, contexts, weights):
    rows, width = tokens.shape
    whole = lambda shape: pl.BlockSpec(shape, lambda t: (0,) * len(shape))
    down = lambda wide: pl.BlockSpec((BLOCK, wide), lambda t: (t, 0))
    across = lambda high: pl.BlockSpec((high, BLOCK), lambda t: (0, t))
    return pl.pallas_call(
        functools.partial(enter_mixture_kernel, len(contexts)),
        grid=(rows // BLOCK,),
        in_specs=[
            down(width), whole((1, width)), whole(router_t.shape), across(routes_t.shape[0]),
            *[across(context.shape[0]) for context in contexts],
            *[whole(weight.shape) for weight in weights],
        ],
        out_specs=[down(width), down(width), across(width), across(EXPERTS)],
        out_shape=[
            jax.ShapeDtypeStruct((rows, width), f32),
            jax.ShapeDtypeStruct((rows, width), bf16),
            jax.ShapeDtypeStruct((width, rows), bf16),
            jax.ShapeDtypeStruct((EXPERTS, rows), f32),
        ],
        compiler_params=pltpu.CompilerParams(vmem_limit_bytes=vmem_bytes),
        cost_estimate=pl.CostEstimate(
            flops=2 * rows * width * width, bytes_accessed=16 * 1024 * 1024, transcendentals=0
        ),
        name="enter_mixture",
    )(tokens, gain, router_t, routes_t, *contexts, *weights)


def enter_back_kernel(
    c_ref, own_ref, other_ref, wo_ref, ctx_ref, hidden_ref, dt_ref, d_ref, spread_ref, wo_grad_ref
):
    hidden_gradient = c_ref[...].astype(f32) + (
        own_ref[...].astype(f32) + other_ref[...].astype(f32)
    )
    hidden_ref[...] = hidden_gradient
    attention_gradient = (residual_scale * hidden_gradient).astype(bf16)
    d_t = dot(wo_ref[...], attention_gradient, 1, 1)
    dt_ref[...] = d_t.astype(bf16)
    put_heads(d_ref, d_t.T.astype(bf16))
    context_t = ctx_ref[...]
    weighed = d_t.astype(bf16).astype(f32) * context_t.astype(f32)
    for h in range(spread_ref.shape[0]):
        spread_ref[h : h + 1, :] = jnp.sum(
            weighed[h * HEAD_DIM : (h + 1) * HEAD_DIM], axis=0, keepdims=True
        )

    @pl.when(pl.program_id(0) == 0)
    def start():
        wo_grad_ref[...] = jnp.zeros_like(wo_grad_ref)

    wo_grad_ref[...] += mm(context_t, attention_gradient)


def enter_back(cotangent, own, other, w_out, context_t):
    rows, width = cotangent.shape
    tall = w_out.shape[0]
    heads = tall // HEAD_DIM
    whole = lambda shape: pl.BlockSpec(shape, lambda t: (0,) * len(shape))
    down = lambda wide: pl.BlockSpec((BLOCK, wide), lambda t: (t, 0))
    across = lambda high: pl.BlockSpec((high, BLOCK), lambda t: (0, t))
    return pl.pallas_call(
        enter_back_kernel,
        grid=(rows // BLOCK,),
        in_specs=[down(width), down(width), down(width), whole((tall, width)), across(tall)],
        out_specs=[
            down(width), across(tall),
            pl.BlockSpec((heads, BLOCK, HEAD_DIM), lambda t: (0, t, 0)),
            across(heads), whole((tall, width)),
        ],
        out_shape=[
            jax.ShapeDtypeStruct((rows, width), f32),
            jax.ShapeDtypeStruct((tall, rows), bf16),
            jax.ShapeDtypeStruct((heads, rows, HEAD_DIM), bf16),
            jax.ShapeDtypeStruct((heads, rows), f32),
            jax.ShapeDtypeStruct((tall, width), f32),
        ],
        compiler_params=pltpu.CompilerParams(vmem_limit_bytes=vmem_bytes),
        cost_estimate=pl.CostEstimate(
            flops=4 * rows * width * tall, bytes_accessed=20 * 1024 * 1024, transcendentals=0
        ),
        name="enter_back",
    )(cotangent, own, other, w_out, context_t)


def leave_back_kernel(
    core_ref, x_ref, gain_ref, cos_ref, sin_ref, wq_ref, wk_ref, wv_ref, normed_ref,
    dq_ref, dk_ref, dv_ref, more_dk_ref, more_dv_ref, wo_grad_ref, router_grad_ref, gain_two_grad_ref,
    part_ref, send_ref, keep_ref, sum_ref, gain_grad_ref,
):
    step = pl.program_id(0)
    cosine, sine = cos_ref[...], -sin_ref[...]
    dq_t = turn(dq_ref[...], cosine, sine).astype(bf16)
    dk_t = turn(dk_ref[...] + more_dk_ref[...].astype(f32), cosine, sine).astype(bf16)
    dv_t = (dv_ref[...] + more_dv_ref[...].astype(f32)).astype(bf16)
    normed = normed_ref[...]

    @pl.when(step == 0)
    def start():
        sum_ref[...] = jnp.zeros_like(sum_ref)
        gain_grad_ref[...] = jnp.zeros_like(gain_grad_ref)

    stacked = jnp.concatenate([dq_t, dk_t, dv_t], axis=0)
    sum_ref[: stacked.shape[0]] += mm(stacked, normed)
    rows_of = lambda tall: tall.astype(f32).T.astype(bf16)
    upstream = (
        dot(rows_of(dq_t), wq_ref[...], 1, 1)
        + mm(rows_of(dk_t), wk_ref[...])
        + mm(rows_of(dv_t), wv_ref[...])
    )
    x = x_ref[...].astype(f32)
    part, gain_part = norm_back(x, scale_of(x), gain_ref[...].astype(f32), upstream)
    part_ref[...] = part.astype(bf16)
    gain_grad_ref[...] += gain_part[None, :]

    @pl.when(step == pl.num_programs(0) - 1)
    def finish():
        place = stacked.shape[0]
        sum_ref[place : place + wo_grad_ref.shape[0]] = wo_grad_ref[...]
        place += wo_grad_ref.shape[0]
        sum_ref[place : place + EXPERTS] = router_grad_ref[...]
        place += EXPERTS
        sum_ref[place : place + 1] = gain_two_grad_ref[...]
        sum_ref[place + 1 : place + 2] = gain_grad_ref[...]
        high = keep_ref.shape[0]
        send_from = pl.multiple_of((1 - core_ref[0]) * high, 16)
        keep_from = pl.multiple_of(core_ref[0] * high, 16)
        send_ref[...] = sum_ref[pl.ds(send_from, high)].astype(bf16)
        keep_ref[...] = sum_ref[pl.ds(keep_from, high)].astype(bf16)


def leave_back(
    core, high, tokens, gain, cosine, sine, w_query, w_key, w_value, normed, dq_t, dk_t, dv_t,
    more_dk, more_dv, w_out_gradient, router_gradient, second_gain_gradient,
):
    rows, width = tokens.shape
    tall, split = w_query.shape[1], w_key.shape[0]
    whole = lambda shape: pl.BlockSpec(shape, lambda t, s: (0,) * len(shape))
    down = lambda wide: pl.BlockSpec((BLOCK, wide), lambda t, s: (t, 0))
    across = lambda high: pl.BlockSpec((high, BLOCK), lambda t, s: (0, t))
    return pl.pallas_call(
        leave_back_kernel,
        grid_spec=pltpu.PrefetchScalarGridSpec(
            num_scalar_prefetch=1,
            grid=(rows // BLOCK,),
            in_specs=[
                down(width), whole((1, width)), across(HEAD_DIM // 2), across(HEAD_DIM // 2),
                whole((width, tall)), whole((split, width)), whole((split, width)), down(width),
                across(tall), across(split), across(split), across(split), across(split),
                whole((tall, width)), whole((EXPERTS, width)), whole((1, width)),
            ],
            out_specs=[down(width), whole((high, width)), whole((high, width))],
            scratch_shapes=[pltpu.VMEM((2 * high, width), f32), pltpu.VMEM((1, width), f32)],
        ),
        out_shape=[
            jax.ShapeDtypeStruct((rows, width), bf16),
            jax.ShapeDtypeStruct((high, width), bf16),
            jax.ShapeDtypeStruct((high, width), bf16),
        ],
        compiler_params=pltpu.CompilerParams(vmem_limit_bytes=vmem_bytes),
        cost_estimate=pl.CostEstimate(
            flops=4 * rows * width * (tall + 2 * split),
            bytes_accessed=24 * 1024 * 1024,
            transcendentals=0,
        ),
        name="leave_back",
    )(
        core, tokens, gain, cosine, sine, w_query, w_key, w_value, normed, dq_t, dk_t, dv_t,
        more_dk, more_dv, w_out_gradient, router_gradient, second_gain_gradient,
    )


def expert_kernel(
    adds, ids_ref, gates_ref, xt_ref, ct_ref, x_ref, c_ref, up_ref, down_ref, *refs
):
    if adds:
        more_ref, *refs = refs
    _, _, _, grad_ref, up_grad_ref, act_ref, gate_grad_ref = refs
    rows = x_ref.shape[0]
    chunk = min(BLOCK, rows)
    for part in range(rows // chunk):
        cut = pl.ds(part * chunk, chunk)
        xt = xt_ref[:, cut]
        gate = mm(up_ref[0, 0], xt)
        up = mm(up_ref[0, 1], xt)
        active_grad = mm(down_ref[0], ct_ref[:, cut])
        share = 1.0 / (1.0 + jnp.exp(-gate))
        silu = gate * share
        active = silu * up
        weight = gates_ref[0, :, cut] * residual_scale
        gate_grad_ref[0, 0, :, cut] = residual_scale * jnp.sum(
            active * active_grad, axis=0, keepdims=True
        )
        for place in range(1, gate_grad_ref.shape[0]):
            gate_grad_ref[place, 0, :, cut] = jnp.zeros((1, chunk), f32)
        active_grad = active_grad * weight
        act_ref[0, :, cut] = (active * weight).astype(bf16)
        up_grad_ref[0, 0, :, cut] = (
            active_grad * up * (share + silu * (1.0 - share))
        ).astype(bf16)
        up_grad_ref[0, 1, :, cut] = (active_grad * silu).astype(bf16)

    def put(place, total):
        if adds:
            total = total + more_ref[0, place].astype(f32)
        grad_ref[0, place] = total.astype(bf16)

    x = x_ref[...]
    put(0, mm(up_grad_ref[0, 0], x))
    put(1, mm(up_grad_ref[0, 1], x))
    put(2, mm(act_ref[0], c_ref[...]))


def expert_step(ids, half, halves, gates, xt, x, ct, c, w_up, w_down, more, old):
    count = ids.shape[0]
    rows, width = x.shape
    units = w_down.shape[1] // 2 * halves
    any_place = pl.BlockSpec(memory_space=pl.ANY)
    whole = lambda shape: pl.BlockSpec(memory_space=pltpu.VMEM)
    fresh = old is None
    adds = more is not None
    each = pl.BlockSpec((1, 3, units, width), lambda e, s: (e, 0, 0, 0))
    if fresh:
        old = (jnp.zeros((8, 128), f32),) * 3
    return pl.pallas_call(
        functools.partial(expert_kernel, adds),
        grid_spec=pltpu.PrefetchScalarGridSpec(
            num_scalar_prefetch=1,
            grid=(count,),
            in_specs=[
                pl.BlockSpec((1, 1, rows), lambda e, s: (s[e], 0, 0)),
                whole((width, rows)),
                whole((width, rows)),
                whole((rows, width)),
                whole((rows, width)),
                pl.BlockSpec((1, 2, units, width), lambda e, s: (s[e], 0, half, 0)),
                pl.BlockSpec((1, units, width), lambda e, s: (s[e], half, 0)),
                *([each] if adds else []),
                any_place,
                any_place,
                any_place,
            ],
            out_specs=[
                each,
                pl.BlockSpec((1, 2, units, rows), lambda e, s: (s[e], 0, half, 0)),
                pl.BlockSpec((1, units, rows), lambda e, s: (s[e], half, 0)),
                pl.BlockSpec((halves, 1, 1, rows), lambda e, s: (half, s[e], 0, 0)),
            ],
        ),
        out_shape=[
            jax.ShapeDtypeStruct((count, 3, units, width), bf16),
            jax.ShapeDtypeStruct((EXPERTS, 2, w_down.shape[1], rows), bf16),
            jax.ShapeDtypeStruct((EXPERTS, w_down.shape[1], rows), bf16),
            jax.ShapeDtypeStruct((2, EXPERTS, 1, rows), f32),
        ],
        input_output_aliases={} if fresh else {8 + adds: 1, 9 + adds: 2, 10 + adds: 3},
        compiler_params=pltpu.CompilerParams(vmem_limit_bytes=expert_vmem_bytes),
        cost_estimate=pl.CostEstimate(
            flops=count * 12 * rows * width * units,
            bytes_accessed=count * units * width * 12 + 8 * rows * width,
            transcendentals=count * units * rows,
        ),
        name="experts",
    )(ids, gates, xt, ct, x, c, w_up, w_down, *([more] if adds else []), *old)


def from_other_half(shard):
    return lax.ppermute(shard, "tensor", [(0, 1), (1, 0)])


def gathered(shard):
    if lax.axis_size("tensor") != 2:
        return [lax.all_gather(shard, "tensor", axis=0, tiled=True)]
    return [shard, from_other_half(shard)]


def both_parts(part):
    if lax.axis_size("tensor") != 2:
        return lax.psum(part, "tensor"), jnp.zeros_like(part)
    return part, from_other_half(part)


def summed_parts(part):
    low = part.astype(bf16)
    if lax.axis_size("tensor") != 2:
        return lax.psum(low, "tensor").astype(f32)
    return low.astype(f32) + from_other_half(low).astype(f32)


def chip_order(chips):
    there = [2 * z for z in range(chips // 2)]
    return there + [chip + 1 for chip in reversed(there)]


def chunk_experts(device, peers, number):
    order = jnp.array(chip_order(peers // 2), jnp.int32)
    each = EXPERTS // peers
    core = device % 2

    def owned(side):
        chips = jnp.where(side == 0, order, order[::-1])
        return (2 * chips + side) * each + number

    return owned(1 - core).astype(jnp.int32), owned(core).astype(jnp.int32)


def chip_rings():
    order = chip_order(lax.axis_size("dp") // 2)
    return [[2 * chip for chip in order], [2 * chip + 1 for chip in reversed(order)]]


def to_owner(chip_sum):
    return lax.psum_scatter(
        chip_sum, "dp", scatter_dimension=0, axis_index_groups=chip_rings(), tiled=True
    )


def summed_over_tokens(send, keep, beside_one, beside_two):
    swap = [(i, i ^ 1) for i in range(lax.axis_size("dp"))]
    received = lax.ppermute(send, "dp", swap)
    half = (keep.astype(f32) + received.astype(f32)).astype(bf16)
    rings = chip_rings()
    half = lax.psum_scatter(half, "dp", scatter_dimension=0, axis_index_groups=rings, tiled=True)
    half, beside_one = lax.optimization_barrier((half, beside_one))
    half = lax.all_gather(half, "dp", axis=0, axis_index_groups=rings, tiled=True)
    half, beside_two = lax.optimization_barrier((half, beside_two))
    other = lax.ppermute(half, "dp", swap)
    is_first = lax.axis_index("dp") % 2 == 0
    low, high = jnp.where(is_first, half, other), jnp.where(is_first, other, half)
    return jnp.concatenate([low, high], axis=0), beside_one, beside_two


def angles(position):
    inverse = rope_base ** (-2.0 * jnp.arange(HEAD_DIM // 2, dtype=f32) / HEAD_DIM)
    angle = inverse[:, None] * position.astype(f32)[None, :]
    return jnp.cos(angle), jnp.sin(angle)


def scale_of(values):
    return lax.rsqrt(jnp.mean(values * values, axis=-1, keepdims=True) + epsilon)


def norm_back(values, scale, gain, upstream):
    pulled = gain * upstream
    slope = jnp.mean(pulled * values, axis=-1, keepdims=True)
    return (
        scale * pulled - values * (scale * scale * scale * slope),
        jnp.sum(upstream * values * scale, axis=0),
    )


def on_device(
    tokens, doc_ids, routes, attention_gain, w_query, w_key, w_value, w_out, mixture_gain,
    w_router, expert_gate_up, expert_down, out_cotangent,
):
    rows, width = tokens.shape
    peers = lax.axis_size("dp")
    device = lax.axis_index("dp")
    pair_heads = w_key.shape[0] // HEAD_DIM
    group = w_query.shape[1] // w_key.shape[0]
    first = device * rows
    chunks = EXPERTS // peers
    w_out_parts = gathered(w_out)

    docs = lax.dynamic_slice_in_dim(doc_ids, first, rows)
    docs_before = lax.dynamic_slice_in_dim(doc_ids, jnp.maximum(device - 1, 0) * rows, rows)
    docs_before = jnp.where(device > 0, docs_before, -1)
    docs_window = jnp.concatenate([docs_before, docs])
    lo = jnp.sum((docs_window[:, None] < docs[None, :]).astype(jnp.int32), axis=0)
    first_block = lo[::BLOCK] // BLOCK
    lo = lo[None, :]

    position = (first + jnp.arange(rows, dtype=jnp.int32)) % SEQ_LEN
    cosine, sine = angles(position)
    gain_one = attention_gain[None, :]
    normed_attention, q_t, q_rows, k_t, k_rows, v_t, v_rows = project(
        tokens, gain_one, cosine, sine, w_query, w_key, w_value
    )
    to_next = [(i, i + 1) for i in range(0, peers, 2)]
    before = SEQ_LEN - rows
    old_k_t = lax.ppermute(k_t, "dp", to_next)
    old_v_t = lax.ppermute(v_t, "dp", to_next)
    across = lambda tall: jnp.swapaxes(tall.reshape(pair_heads, HEAD_DIM, before), 1, 2)
    old_k_rows, old_v_rows = across(old_k_t), across(old_v_t)

    calls = 2 if pair_heads % 2 == 0 else 1
    here = pair_heads // calls
    pieces = [
        attend(
            first_block, lo, q_t, k_rows, v_t, old_k_rows, old_v_t, group, call * here, here
        )
        for call in range(calls)
    ]
    context_parts = [gathered(piece[0]) for piece in pieces]
    contexts = [parts[side] for side in range(len(context_parts[0])) for parts in context_parts]
    context_t = jnp.concatenate([piece[0] for piece in pieces], axis=0)
    logs = jnp.concatenate([piece[1] for piece in pieces], axis=0)
    w_out_pieces = [
        piece for part in w_out_parts for piece in jnp.split(part, calls, axis=0)
    ]
    hidden, normed_mixture, normed_t, gates = enter_mixture(
        tokens, mixture_gain[None, :], w_router.T, routes.T, contexts, w_out_pieces
    )
    gain_two = mixture_gain.astype(f32)
    scale_two = scale_of(hidden)

    upstream_t = out_cotangent.T
    swap_cores = [(i, i ^ 1) for i in range(peers)]
    shares, arrived, old = [], [], None
    pieces = [(number, half, 1) for number in range(chunks) for half in range(2)]

    def run_experts(piece, side, more):
        ids = chunk_experts(device, peers, piece[0])[side]
        return expert_step(
            ids, piece[1], piece[2], gates[:, None, :], normed_t, normed_mixture, upstream_t, out_cotangent,
            expert_gate_up, expert_down, more, old,
        )

    for number in range(len(pieces) + 1):
        if number < len(pieces):
            send, *old = run_experts(pieces[number], 0, None)
            arrived.append(lax.ppermute(send, "dp", swap_cores))
        if number > 0:
            chip_sum, *old = run_experts(pieces[number - 1], 1, arrived[number - 1])
            shares.append(to_owner(chip_sum))
    up_grad, act, gates_gradient = old
    gates_gradient = gates_gradient[0, :, 0] + gates_gradient[1, :, 0]
    units = expert_down.shape[1]
    wide = EXPERTS * units

    logits_gradient = gates * (
        gates_gradient - jnp.sum(gates * gates_gradient, axis=0, keepdims=True)
    )
    logits_low = logits_gradient.astype(bf16)
    router_gradient = mm(logits_low, normed_mixture)
    up_grad = up_grad.reshape(2 * wide, rows)
    w_up = expert_gate_up.reshape(2 * wide, width)
    own_parts, other_parts, gain_parts = [], [], []
    for start in range(0, rows, rows // 2):
        cut = slice(start, start + rows // 2)
        if start > 0:
            up_grad, own_parts[0] = lax.optimization_barrier((up_grad, own_parts[0]))
        normed_gradient = dot(up_grad[:, cut], w_up, 0, 0) + dot(logits_low[:, cut], w_router, 0, 1)
        part, gain_part = norm_back(hidden[cut], scale_two[cut], gain_two, normed_gradient)
        part = part.astype(bf16)
        if start > 0:
            part, act, other_parts[0] = lax.optimization_barrier((part, act, other_parts[0]))
        own, other = both_parts(part)
        own_parts.append(own)
        other_parts.append(other)
        gain_parts.append(gain_part)
    second_gain_part = gain_parts[0] + gain_parts[1]

    mixture_part = dot(act.reshape(wide, rows), expert_down.reshape(wide, width), 0, 0)
    mixture_low = mixture_part.astype(bf16)
    own_part = jnp.concatenate(own_parts, axis=0)
    other_part = jnp.concatenate(other_parts, axis=0)
    own_part, other_part, mixture_low = lax.optimization_barrier(
        (own_part, other_part, mixture_low)
    )
    mixture_own, mixture_other = both_parts(mixture_low)

    hidden_gradient, d_t, d_rows, spread, w_out_gradient = enter_back(
        out_cotangent, own_part, other_part, w_out, context_t
    )
    by_group = lambda rows_of_heads: rows_of_heads.reshape(pair_heads, group, rows, HEAD_DIM)
    dq_t, dk_t, dv_t, old_dk, old_dv = attend_back(
        first_block, lo, logs, spread.reshape(pair_heads, group, rows), q_t, d_t, by_group(q_rows),
        by_group(d_rows), k_rows, k_t, v_rows, old_k_rows, old_k_t, old_v_rows,
    )
    to_previous = [(i + 1, i) for i in range(0, peers, 2)]
    more_dk = lax.ppermute(old_dk, "dp", to_previous)
    more_dv = lax.ppermute(old_dv, "dp", to_previous)
    dq_t, mixture_other, *shares[:-2] = lax.optimization_barrier(
        (dq_t, mixture_other, *shares[:-2])
    )
    tall, split = w_query.shape[1], w_key.shape[0]
    ends = [tall, tall + split, tall + 2 * split, 2 * tall + 2 * split, 2 * tall + 2 * split + EXPERTS]
    high = -(-(ends[-1] + 2) // (16 * peers)) * 8 * peers
    input_part, send, keep = leave_back(
        (device % 2)[None].astype(jnp.int32), high, tokens, gain_one, cosine, sine, w_query, w_key,
        w_value, normed_attention, dq_t, dk_t, dv_t, more_dk, more_dv, w_out_gradient,
        router_gradient, second_gain_part[None, :],
    )
    part_one, part_two = jnp.split(input_part, 2, axis=0)
    own_one, other_one = both_parts(part_one)
    part_two, other_one = lax.optimization_barrier((part_two, other_one))
    own_two, other_two = both_parts(part_two)
    *shares[-2:], keep = lax.optimization_barrier((*shares[-2:], keep))
    mixed = (hidden + (mixture_own.astype(f32) + mixture_other.astype(f32))).astype(bf16)
    shares = [
        jnp.concatenate(shares[start : start + 2], axis=2) for start in range(0, len(shares), 2)
    ]
    experts_gradient = jnp.concatenate(shares, axis=0).astype(f32)
    up_gradient, down_gradient = experts_gradient[:, :2], experts_gradient[:, 2]
    input_sum = jnp.concatenate(
        [own_one.astype(f32) + other_one.astype(f32), own_two.astype(f32) + other_two.astype(f32)],
        axis=0,
    )
    tokens_gradient = (hidden_gradient + input_sum).astype(bf16)
    gradients, (_, mixed, up_gradient, down_gradient), tokens_gradient = summed_over_tokens(
        send, keep, (other_one, mixed, up_gradient, down_gradient), tokens_gradient
    )
    w_q, w_k, w_v, w_o = jnp.split(gradients[: ends[3]].astype(f32), ends[:3], axis=0)
    small = summed_parts(gradients[ends[3] : ends[4] + 2])
    router, gains = small[:EXPERTS], small[EXPERTS:]
    return (
        mixed, tokens_gradient, gains[1], w_q.T, w_k, w_v, w_o, gains[0], router.T,
        up_gradient, down_gradient,
    )


def solution(mesh):
    placed = (
        P("dp", None),
        P(),
        P("dp", None),
        P(),
        P(None, "tensor"),
        P("tensor", None),
        P("tensor", None),
        P("tensor", None),
        P(),
        P(),
        P(None, None, "tensor", None),
        P(None, "tensor", None),
        P("dp", None),
    )
    return jax.shard_map(
        on_device,
        mesh=mesh,
        in_specs=placed,
        out_specs=(
            P("dp", None),
            P("dp", None),
            P(),
            P(None, "tensor"),
            P("tensor", None),
            P("tensor", None),
            P("tensor", None),
            P(),
            P(),
            P("dp", None, "tensor", None),
            P("dp", "tensor", None),
        ),
        check_vma=False,
    )
```

```python
import functools

import jax
import jax.numpy as jnp
from jax import lax
from jax.experimental import pallas as pl
from jax.experimental.pallas import tpu as pltpu
from jax.sharding import PartitionSpec as P

HEAD_DIM = 64
EXPERTS = 32
SEQ_LEN = 2048
BLOCK = 256

epsilon = 1e-06
score_scale = 0.015625
residual_scale = 0.22
rope_base = 10000.0
masked_value = -1e30
vmem_bytes = 60 * 1024 * 1024
expert_vmem_bytes = 32 * 1024 * 1024
f32 = jnp.float32
bf16 = jnp.bfloat16


def dot(left, right, left_dim, right_dim):
    return lax.dot_general(
        left, right, (((left_dim,), (right_dim,)), ((), ())), preferred_element_type=f32
    )


def mm(left, right):
    return jnp.dot(left, right, preferred_element_type=f32)


def block_mask(lo, hi, start, lanes):
    place = start + lax.broadcasted_iota(jnp.int32, (BLOCK, lanes), 0)
    return (place >= lo) & (place <= hi)


def window_of(lo_ref, block, before, group):
    cut = pl.ds(block * BLOCK, BLOCK)
    lo = lo_ref[:, cut]
    hi = before + block * BLOCK + lax.broadcasted_iota(jnp.int32, (1, BLOCK), 1)
    return (
        jnp.concatenate([lo] * group, axis=1),
        jnp.concatenate([hi] * group, axis=1),
    )


def heads_side_by_side(ref, block, group):
    cut = pl.ds(block * BLOCK, BLOCK)
    return jnp.concatenate(
        [ref[h * HEAD_DIM : (h + 1) * HEAD_DIM, cut] for h in range(group)], axis=1
    )


def heads_one_above(ref, j, block, group):
    cut = pl.ds(block * BLOCK, BLOCK)
    return jnp.concatenate([ref[j, h, cut, :] for h in range(group)], axis=0)


def attend_kernel(
    group, first_ref, lo_ref, qt_ref, k_ref, vt_ref, old_k_ref, old_vt_ref, out_ref, log_ref
):
    lanes = group * BLOCK
    together, before, _ = old_k_ref.shape
    tall = group * HEAD_DIM
    passed = before // BLOCK
    for block in range(qt_ref.shape[1] // BLOCK):
        lo, hi = window_of(lo_ref, block, before, group)
        queries = [
            heads_side_by_side(qt_ref.at[pl.ds(j * tall, tall)], block, group)
            for j in range(together)
        ]

        def step(keys_ref, values_ref, offset, number, carry):
            start = pl.multiple_of(number * BLOCK, BLOCK)
            here = pl.ds(start, BLOCK)
            mask = block_mask(lo, hi, offset + start, lanes)
            result = []
            for j, (peak, total, acc) in enumerate(carry):
                scores = mm(keys_ref[j, here, :], queries[j])
                scores = jnp.where(mask, scores, masked_value)
                top = jnp.maximum(peak, jnp.max(scores, axis=0, keepdims=True))
                weights = jnp.exp(scores - top)
                fade = jnp.exp(peak - top)
                total = total * fade + jnp.sum(weights, axis=0, keepdims=True)
                values = values_ref[j * HEAD_DIM : (j + 1) * HEAD_DIM, here]
                result.append((top, total, acc * fade + mm(values, weights.astype(bf16))))
            return tuple(result)

        first = first_ref[block]
        nothing = (
            jnp.full((1, lanes), masked_value, f32),
            jnp.zeros((1, lanes), f32),
            jnp.zeros((HEAD_DIM, lanes), f32),
        )
        carry = lax.fori_loop(
            first, passed, functools.partial(step, old_k_ref, old_vt_ref, 0), (nothing,) * together
        )
        carry = lax.fori_loop(
            jnp.maximum(first - passed, 0),
            block + 1,
            functools.partial(step, k_ref, vt_ref, before),
            carry,
        )
        cut = pl.ds(block * BLOCK, BLOCK)
        for j, (peak, total, acc) in enumerate(carry):
            result = (acc / total).astype(bf16)
            logs = peak + jnp.log(total)
            for h in range(group):
                side = slice(h * BLOCK, (h + 1) * BLOCK)
                high = j * tall + h * HEAD_DIM
                out_ref[high : high + HEAD_DIM, cut] = result[:, side]
                log_ref[j, h : h + 1, cut] = logs[:, side]


def attend(first, lo, q_t, k, v_t, old_k, old_v_t, group, base, pair_heads):
    rows = k.shape[1]
    before = old_k.shape[1]
    together = 1
    start = base // together
    tall = together * group * HEAD_DIM
    split = together * HEAD_DIM
    by_head = lambda h, s: (start + h, 0, 0)
    flat = lambda h, s: (start + h, 0)
    return pl.pallas_call(
        functools.partial(attend_kernel, group),
        grid_spec=pltpu.PrefetchScalarGridSpec(
            num_scalar_prefetch=1,
            grid=(pair_heads // together,),
            in_specs=[
                pl.BlockSpec((1, rows), lambda h, s: (0, 0)),
                pl.BlockSpec((tall, rows), flat),
                pl.BlockSpec((together, rows, HEAD_DIM), by_head),
                pl.BlockSpec((split, rows), flat),
                pl.BlockSpec((together, before, HEAD_DIM), by_head),
                pl.BlockSpec((split, before), flat),
            ],
            out_specs=[
                pl.BlockSpec((tall, rows), lambda h, s: (h, 0)),
                pl.BlockSpec((together, group, rows), lambda h, s: (h, 0, 0)),
            ],
        ),
        out_shape=[
            jax.ShapeDtypeStruct((pair_heads * group * HEAD_DIM, rows), bf16),
            jax.ShapeDtypeStruct((pair_heads, group, rows), f32),
        ],
        compiler_params=pltpu.CompilerParams(vmem_limit_bytes=vmem_bytes),
        cost_estimate=pl.CostEstimate(
            flops=pair_heads * group * rows * (rows + before) * 512,
            bytes_accessed=8 * 1024 * 1024,
            transcendentals=pair_heads * group * rows * (rows + before),
        ),
        name="attend",
    )(first, lo, q_t, k, v_t, old_k, old_v_t)


def attend_back_kernel(
    group,
    first_ref, lo_ref, log_ref, spread_ref, qt_ref, dt_ref, q_ref, d_ref, k_ref, kt_ref, v_ref,
    old_k_ref, old_kt_ref, old_v_ref,
    dq_ref, dk_ref, dv_ref, old_dk_ref, old_dv_ref, pair_ref, old_pair_ref,
):
    lanes = group * BLOCK
    together, before, _ = old_k_ref.shape
    tall = group * HEAD_DIM
    passed = before // BLOCK
    pair_ref[...] = jnp.zeros_like(pair_ref)
    old_pair_ref[...] = jnp.zeros_like(old_pair_ref)
    for block in range(qt_ref.shape[1] // BLOCK):
        cut = pl.ds(block * BLOCK, BLOCK)
        lo, hi = window_of(lo_ref, block, before, group)
        heads = []
        for j in range(together):
            here = pl.ds(j * tall, tall)
            query_rows = heads_one_above(q_ref, j, block, group)
            upstream_rows = heads_one_above(d_ref, j, block, group)
            nothing = jnp.zeros_like(query_rows)
            both_rows = jnp.concatenate(
                [
                    jnp.concatenate([query_rows, nothing], axis=1),
                    jnp.concatenate([nothing, upstream_rows], axis=1),
                ],
                axis=0,
            )
            heads.append(
                (
                    heads_side_by_side(qt_ref.at[here], block, group),
                    heads_side_by_side(dt_ref.at[here], block, group),
                    both_rows,
                    jnp.concatenate([log_ref[j, h : h + 1, cut] for h in range(group)], axis=1),
                    jnp.concatenate([spread_ref[j, h : h + 1, cut] for h in range(group)], axis=1),
                )
            )

        def step(keys_ref, keys_t_ref, values_ref, sums_ref, offset, number, sums):
            start = pl.multiple_of(number * BLOCK, BLOCK)
            here = pl.ds(start, BLOCK)
            mask = block_mask(lo, hi, start + offset, lanes)
            result = []
            for j, (query, upstream, both_rows, logs, spread) in enumerate(heads):
                scores = mm(keys_ref[j, here, :], query)
                probs = jnp.exp(jnp.where(mask, scores - logs, masked_value))
                change = mm(values_ref[j, here, :], upstream)
                scores_change = (probs * (change - spread)).astype(bf16)
                sums_ref[j, here, :] += mm(
                    jnp.concatenate([scores_change, probs.astype(bf16)], axis=1), both_rows
                )
                keys_t = keys_t_ref[j * HEAD_DIM : (j + 1) * HEAD_DIM, here]
                result.append(sums[j] + mm(keys_t, scores_change))
            return tuple(result)

        first = first_ref[block]
        sums = (jnp.zeros((HEAD_DIM, lanes), f32),) * together
        earlier = functools.partial(step, old_k_ref, old_kt_ref, old_v_ref, old_pair_ref, 0)
        sums = lax.fori_loop(first, passed, earlier, sums)
        own = functools.partial(step, k_ref, kt_ref, v_ref, pair_ref, before)
        sums = lax.fori_loop(jnp.maximum(first - passed, 0), block + 1, own, sums)
        for j in range(together):
            for h in range(group):
                high = j * tall + h * HEAD_DIM
                dq_ref[high : high + HEAD_DIM, cut] = (
                    sums[j][:, h * BLOCK : (h + 1) * BLOCK] * score_scale
                )
    for j in range(together):
        side = slice(j * HEAD_DIM, (j + 1) * HEAD_DIM)
        pair_t = pair_ref[j].T
        dk_ref[side] = pair_t[:HEAD_DIM]
        dv_ref[side] = pair_t[HEAD_DIM:]
        pair_t = old_pair_ref[j].T
        old_dk_ref[side] = pair_t[:HEAD_DIM].astype(bf16)
        old_dv_ref[side] = pair_t[HEAD_DIM:].astype(bf16)


def attend_back(
    first, lo, logs, spread, q_t, d_t, q_rows, d_rows, k, k_t, v, old_k, old_k_t, old_v
):
    pair_heads, before, _ = old_k.shape
    group, rows = q_rows.shape[1:3]
    together = 2 if pair_heads % 2 == 0 else 1
    tall = together * group * HEAD_DIM
    split = together * HEAD_DIM
    by_head = lambda h, s: (h, 0, 0)
    flat = lambda h, s: (h, 0)
    return pl.pallas_call(
        functools.partial(attend_back_kernel, group),
        grid_spec=pltpu.PrefetchScalarGridSpec(
            num_scalar_prefetch=1,
            grid=(pair_heads // together,),
            in_specs=[
                pl.BlockSpec((1, rows), lambda h, s: (0, 0)),
                pl.BlockSpec((together, group, rows), by_head),
                pl.BlockSpec((together, group, rows), by_head),
                pl.BlockSpec((tall, rows), flat),
                pl.BlockSpec((tall, rows), flat),
                pl.BlockSpec((together, group, rows, HEAD_DIM), lambda h, s: (h, 0, 0, 0)),
                pl.BlockSpec((together, group, rows, HEAD_DIM), lambda h, s: (h, 0, 0, 0)),
                pl.BlockSpec((together, rows, HEAD_DIM), by_head),
                pl.BlockSpec((split, rows), flat),
                pl.BlockSpec((together, rows, HEAD_DIM), by_head),
                pl.BlockSpec((together, before, HEAD_DIM), by_head),
                pl.BlockSpec((split, before), flat),
                pl.BlockSpec((together, before, HEAD_DIM), by_head),
            ],
            out_specs=[
                pl.BlockSpec((tall, rows), flat),
                pl.BlockSpec((split, rows), flat),
                pl.BlockSpec((split, rows), flat),
                pl.BlockSpec((split, before), flat),
                pl.BlockSpec((split, before), flat),
            ],
            scratch_shapes=[
                pltpu.VMEM((together, rows, 2 * HEAD_DIM), f32),
                pltpu.VMEM((together, before, 2 * HEAD_DIM), f32),
            ],
        ),
        out_shape=[
            jax.ShapeDtypeStruct((pair_heads * group * HEAD_DIM, rows), f32),
            jax.ShapeDtypeStruct((pair_heads * HEAD_DIM, rows), f32),
            jax.ShapeDtypeStruct((pair_heads * HEAD_DIM, rows), f32),
            jax.ShapeDtypeStruct((pair_heads * HEAD_DIM, before), bf16),
            jax.ShapeDtypeStruct((pair_heads * HEAD_DIM, before), bf16),
        ],
        compiler_params=pltpu.CompilerParams(vmem_limit_bytes=vmem_bytes),
        cost_estimate=pl.CostEstimate(
            flops=pair_heads * group * rows * (rows + before) * 1280,
            bytes_accessed=16 * 1024 * 1024,
            transcendentals=pair_heads * group * rows * (rows + before),
        ),
        name="attend_back",
    )(first, lo, logs, spread, q_t, d_t, q_rows, d_rows, k, k_t, v, old_k, old_k_t, old_v)


def turn(tall, cosine, sine):
    half = HEAD_DIM // 2
    parts = []
    for start in range(0, tall.shape[0], HEAD_DIM):
        a, b = tall[start : start + half], tall[start + half : start + HEAD_DIM]
        parts += [a * cosine - b * sine, b * cosine + a * sine]
    return jnp.concatenate(parts, axis=0)


def put_heads(ref, rows_of_heads):
    for h in range(ref.shape[0]):
        ref[h] = rows_of_heads[:, h * HEAD_DIM : (h + 1) * HEAD_DIM]


def project_kernel(
    x_ref, gain_ref, cos_ref, sin_ref, wq_ref, wk_ref, wv_ref,
    normed_ref, qt_ref, q_ref, kt_ref, k_ref, vt_ref, v_ref,
):
    x = x_ref[...].astype(f32)
    normed = (x * scale_of(x) * gain_ref[...].astype(f32)).astype(bf16)
    normed_ref[...] = normed
    cosine, sine = cos_ref[...], sin_ref[...]
    q_t = turn(mm(normed, wq_ref[...]).T, cosine, sine).astype(bf16).astype(f32) * score_scale
    qt_ref[...] = q_t.astype(bf16)
    put_heads(q_ref, q_t.T.astype(bf16))
    k_t = turn(dot(wk_ref[...], normed, 1, 1), cosine, sine)
    kt_ref[...] = k_t.astype(bf16)
    put_heads(k_ref, k_t.T.astype(bf16))
    v_t = dot(wv_ref[...], normed, 1, 1)
    vt_ref[...] = v_t.astype(bf16)
    put_heads(v_ref, v_t.T.astype(bf16))


def project(tokens, gain, cosine, sine, w_query, w_key, w_value):
    rows, width = tokens.shape
    tall, split = w_query.shape[1], w_key.shape[0]
    heads, pair_heads = tall // HEAD_DIM, split // HEAD_DIM
    whole = lambda shape: pl.BlockSpec(shape, lambda t: (0,) * len(shape))
    down = lambda wide: pl.BlockSpec((BLOCK, wide), lambda t: (t, 0))
    across = lambda high: pl.BlockSpec((high, BLOCK), lambda t: (0, t))
    stacked = lambda count: pl.BlockSpec((count, BLOCK, HEAD_DIM), lambda t: (0, t, 0))
    return pl.pallas_call(
        project_kernel,
        grid=(rows // BLOCK,),
        in_specs=[
            down(width), whole((1, width)), across(HEAD_DIM // 2), across(HEAD_DIM // 2),
            whole((width, tall)), whole((split, width)), whole((split, width)),
        ],
        out_specs=[
            down(width), across(tall), stacked(heads), across(split), stacked(pair_heads),
            across(split), stacked(pair_heads),
        ],
        out_shape=[
            jax.ShapeDtypeStruct((rows, width), bf16),
            jax.ShapeDtypeStruct((tall, rows), bf16),
            jax.ShapeDtypeStruct((heads, rows, HEAD_DIM), bf16),
            jax.ShapeDtypeStruct((split, rows), bf16),
            jax.ShapeDtypeStruct((pair_heads, rows, HEAD_DIM), bf16),
            jax.ShapeDtypeStruct((split, rows), bf16),
            jax.ShapeDtypeStruct((pair_heads, rows, HEAD_DIM), bf16),
        ],
        compiler_params=pltpu.CompilerParams(vmem_limit_bytes=vmem_bytes),
        cost_estimate=pl.CostEstimate(
            flops=2 * rows * width * (tall + 2 * split),
            bytes_accessed=12 * 1024 * 1024,
            transcendentals=0,
        ),
        name="project",
    )(tokens, gain, cosine, sine, w_query, w_key, w_value)


def enter_mixture_kernel(count, x_ref, gain_ref, router_ref, routes_ref, *refs):
    pieces, (hidden_ref, normed_ref, normed_t_ref, gates_ref) = refs[: 2 * count], refs[2 * count :]
    products = [
        mm(context_ref[...].astype(f32).T.astype(bf16), w_ref[...])
        for context_ref, w_ref in zip(pieces[:count], pieces[count:])
    ]
    sides = max(1, count // 2)
    projected = functools.reduce(jnp.add, products[:sides])
    if count > sides:
        projected = projected + functools.reduce(jnp.add, products[sides:])
    hidden = x_ref[...].astype(f32) + residual_scale * projected
    hidden_ref[...] = hidden
    normed = hidden * scale_of(hidden) * gain_ref[...].astype(f32)
    normed_t_ref[...] = normed.T.astype(bf16)
    normed = normed.astype(bf16)
    normed_ref[...] = normed
    logits = dot(router_ref[...], normed, 1, 1)
    expert = lax.broadcasted_iota(jnp.int32, logits.shape, 0)
    chosen = expert == routes_ref[0:1, :]
    for k in range(1, routes_ref.shape[0]):
        chosen = chosen | (expert == routes_ref[k : k + 1, :])
    logits = jnp.where(chosen, logits, masked_value)
    weights = jnp.exp(logits - jnp.max(logits, axis=0, keepdims=True))
    weights = jnp.where(chosen, weights, 0.0)
    gates_ref[...] = weights / jnp.sum(weights, axis=0, keepdims=True)


def enter_mixture(tokens, gain, router_t, routes_t, contexts, weights):
    rows, width = tokens.shape
    whole = lambda shape: pl.BlockSpec(shape, lambda t: (0,) * len(shape))
    down = lambda wide: pl.BlockSpec((BLOCK, wide), lambda t: (t, 0))
    across = lambda high: pl.BlockSpec((high, BLOCK), lambda t: (0, t))
    return pl.pallas_call(
        functools.partial(enter_mixture_kernel, len(contexts)),
        grid=(rows // BLOCK,),
        in_specs=[
            down(width), whole((1, width)), whole(router_t.shape), across(routes_t.shape[0]),
            *[across(context.shape[0]) for context in contexts],
            *[whole(weight.shape) for weight in weights],
        ],
        out_specs=[down(width), down(width), across(width), across(EXPERTS)],
        out_shape=[
            jax.ShapeDtypeStruct((rows, width), f32),
            jax.ShapeDtypeStruct((rows, width), bf16),
            jax.ShapeDtypeStruct((width, rows), bf16),
            jax.ShapeDtypeStruct((EXPERTS, rows), f32),
        ],
        compiler_params=pltpu.CompilerParams(vmem_limit_bytes=expert_vmem_bytes),
        cost_estimate=pl.CostEstimate(
            flops=2 * rows * width * width, bytes_accessed=16 * 1024 * 1024, transcendentals=0
        ),
        name="enter_mixture",
    )(tokens, gain, router_t, routes_t, *contexts, *weights)


def enter_back_kernel(
    c_ref, own_ref, other_ref, wo_ref, ctx_ref, hidden_ref, dt_ref, d_ref, spread_ref, wo_grad_ref
):
    hidden_gradient = c_ref[...].astype(f32) + (
        own_ref[...].astype(f32) + other_ref[...].astype(f32)
    )
    hidden_ref[...] = hidden_gradient
    attention_gradient = (residual_scale * hidden_gradient).astype(bf16)
    d_t = dot(wo_ref[...], attention_gradient, 1, 1)
    dt_ref[...] = d_t.astype(bf16)
    put_heads(d_ref, d_t.T.astype(bf16))
    context_t = ctx_ref[...]
    weighed = d_t.astype(bf16).astype(f32) * context_t.astype(f32)
    for h in range(spread_ref.shape[0]):
        spread_ref[h : h + 1, :] = jnp.sum(
            weighed[h * HEAD_DIM : (h + 1) * HEAD_DIM], axis=0, keepdims=True
        )

    @pl.when(pl.program_id(0) == 0)
    def start():
        wo_grad_ref[...] = jnp.zeros_like(wo_grad_ref)

    wo_grad_ref[...] += mm(context_t, attention_gradient)


def enter_back(cotangent, own, other, w_out, context_t):
    rows, width = cotangent.shape
    tall = w_out.shape[0]
    heads = tall // HEAD_DIM
    whole = lambda shape: pl.BlockSpec(shape, lambda t: (0,) * len(shape))
    down = lambda wide: pl.BlockSpec((BLOCK, wide), lambda t: (t, 0))
    across = lambda high: pl.BlockSpec((high, BLOCK), lambda t: (0, t))
    return pl.pallas_call(
        enter_back_kernel,
        grid=(rows // BLOCK,),
        in_specs=[down(width), down(width), down(width), whole((tall, width)), across(tall)],
        out_specs=[
            down(width), across(tall),
            pl.BlockSpec((heads, BLOCK, HEAD_DIM), lambda t: (0, t, 0)),
            across(heads), whole((tall, width)),
        ],
        out_shape=[
            jax.ShapeDtypeStruct((rows, width), f32),
            jax.ShapeDtypeStruct((tall, rows), bf16),
            jax.ShapeDtypeStruct((heads, rows, HEAD_DIM), bf16),
            jax.ShapeDtypeStruct((heads, rows), f32),
            jax.ShapeDtypeStruct((tall, width), f32),
        ],
        compiler_params=pltpu.CompilerParams(vmem_limit_bytes=vmem_bytes),
        cost_estimate=pl.CostEstimate(
            flops=4 * rows * width * tall, bytes_accessed=20 * 1024 * 1024, transcendentals=0
        ),
        name="enter_back",
    )(cotangent, own, other, w_out, context_t)


def leave_back_kernel(
    core_ref, x_ref, gain_ref, cos_ref, sin_ref, wq_ref, wk_ref, wv_ref, normed_ref,
    dq_ref, dk_ref, dv_ref, more_dk_ref, more_dv_ref, wo_grad_ref, router_grad_ref, gain_two_grad_ref,
    part_ref, send_ref, keep_ref, sum_ref, gain_grad_ref,
):
    step = pl.program_id(0)
    cosine, sine = cos_ref[...], -sin_ref[...]
    dq_t = turn(dq_ref[...], cosine, sine).astype(bf16)
    dk_t = turn(dk_ref[...] + more_dk_ref[...].astype(f32), cosine, sine).astype(bf16)
    dv_t = (dv_ref[...] + more_dv_ref[...].astype(f32)).astype(bf16)
    normed = normed_ref[...]

    @pl.when(step == 0)
    def start():
        sum_ref[...] = jnp.zeros_like(sum_ref)
        gain_grad_ref[...] = jnp.zeros_like(gain_grad_ref)

    stacked = jnp.concatenate([dq_t, dk_t, dv_t], axis=0)
    sum_ref[: stacked.shape[0]] += mm(stacked, normed)
    rows_of = lambda tall: tall.astype(f32).T.astype(bf16)
    upstream = (
        dot(rows_of(dq_t), wq_ref[...], 1, 1)
        + mm(rows_of(dk_t), wk_ref[...])
        + mm(rows_of(dv_t), wv_ref[...])
    )
    x = x_ref[...].astype(f32)
    part, gain_part = norm_back(x, scale_of(x), gain_ref[...].astype(f32), upstream)
    part_ref[...] = part.astype(bf16)
    gain_grad_ref[...] += gain_part[None, :]

    @pl.when(step == pl.num_programs(0) - 1)
    def finish():
        place = stacked.shape[0]
        sum_ref[place : place + wo_grad_ref.shape[0]] = wo_grad_ref[...]
        place += wo_grad_ref.shape[0]
        sum_ref[place : place + EXPERTS] = router_grad_ref[...]
        place += EXPERTS
        sum_ref[place : place + 1] = gain_two_grad_ref[...]
        sum_ref[place + 1 : place + 2] = gain_grad_ref[...]
        high = keep_ref.shape[0]
        send_from = pl.multiple_of((1 - core_ref[0]) * high, 16)
        keep_from = pl.multiple_of(core_ref[0] * high, 16)
        send_ref[...] = sum_ref[pl.ds(send_from, high)].astype(bf16)
        keep_ref[...] = sum_ref[pl.ds(keep_from, high)].astype(bf16)


def leave_back(
    core, high, tokens, gain, cosine, sine, w_query, w_key, w_value, normed, dq_t, dk_t, dv_t,
    more_dk, more_dv, w_out_gradient, router_gradient, second_gain_gradient,
):
    rows, width = tokens.shape
    tall, split = w_query.shape[1], w_key.shape[0]
    whole = lambda shape: pl.BlockSpec(shape, lambda t, s: (0,) * len(shape))
    down = lambda wide: pl.BlockSpec((BLOCK, wide), lambda t, s: (t, 0))
    across = lambda high: pl.BlockSpec((high, BLOCK), lambda t, s: (0, t))
    return pl.pallas_call(
        leave_back_kernel,
        grid_spec=pltpu.PrefetchScalarGridSpec(
            num_scalar_prefetch=1,
            grid=(rows // BLOCK,),
            in_specs=[
                down(width), whole((1, width)), across(HEAD_DIM // 2), across(HEAD_DIM // 2),
                whole((width, tall)), whole((split, width)), whole((split, width)), down(width),
                across(tall), across(split), across(split), across(split), across(split),
                whole((tall, width)), whole((EXPERTS, width)), whole((1, width)),
            ],
            out_specs=[down(width), whole((high, width)), whole((high, width))],
            scratch_shapes=[pltpu.VMEM((2 * high, width), f32), pltpu.VMEM((1, width), f32)],
        ),
        out_shape=[
            jax.ShapeDtypeStruct((rows, width), bf16),
            jax.ShapeDtypeStruct((high, width), bf16),
            jax.ShapeDtypeStruct((high, width), bf16),
        ],
        compiler_params=pltpu.CompilerParams(vmem_limit_bytes=vmem_bytes),
        cost_estimate=pl.CostEstimate(
            flops=4 * rows * width * (tall + 2 * split),
            bytes_accessed=24 * 1024 * 1024,
            transcendentals=0,
        ),
        name="leave_back",
    )(
        core, tokens, gain, cosine, sine, w_query, w_key, w_value, normed, dq_t, dk_t, dv_t,
        more_dk, more_dv, w_out_gradient, router_gradient, second_gain_gradient,
    )


def expert_kernel(
    adds, ids_ref, gates_ref, xt_ref, ct_ref, x_ref, c_ref, up_ref, down_ref, *refs
):
    if adds:
        more_ref, *refs = refs
    _, _, _, grad_ref, up_grad_ref, act_ref, gate_grad_ref = refs
    rows = x_ref.shape[0]
    chunk = min(BLOCK, rows)
    for part in range(rows // chunk):
        cut = pl.ds(part * chunk, chunk)
        xt = xt_ref[:, cut]
        gate = mm(up_ref[0, 0], xt)
        up = mm(up_ref[0, 1], xt)
        active_grad = mm(down_ref[0], ct_ref[:, cut])
        share = 1.0 / (1.0 + jnp.exp(-gate))
        silu = gate * share
        active = silu * up
        weight = gates_ref[0, :, cut] * residual_scale
        gate_grad_ref[0, 0, :, cut] = residual_scale * jnp.sum(
            active * active_grad, axis=0, keepdims=True
        )
        for place in range(1, gate_grad_ref.shape[0]):
            gate_grad_ref[place, 0, :, cut] = jnp.zeros((1, chunk), f32)
        active_grad = active_grad * weight
        act_ref[0, :, cut] = (active * weight).astype(bf16)
        up_grad_ref[0, 0, :, cut] = (
            active_grad * up * (share + silu * (1.0 - share))
        ).astype(bf16)
        up_grad_ref[0, 1, :, cut] = (active_grad * silu).astype(bf16)

    def put(place, total):
        if adds:
            total = total + more_ref[0, place].astype(f32)
        grad_ref[0, place] = total.astype(bf16)

    x = x_ref[...]
    put(0, mm(up_grad_ref[0, 0], x))
    put(1, mm(up_grad_ref[0, 1], x))
    put(2, mm(act_ref[0], c_ref[...]))


def expert_step(ids, half, halves, gates, xt, x, ct, c, w_up, w_down, more, old):
    count = ids.shape[0]
    rows, width = x.shape
    units = w_down.shape[1] // 2 * halves
    any_place = pl.BlockSpec(memory_space=pl.ANY)
    whole = lambda shape: pl.BlockSpec(memory_space=pltpu.VMEM)
    fresh = old is None
    adds = more is not None
    each = pl.BlockSpec((1, 3, units, width), lambda e, s: (e, 0, 0, 0))
    if fresh:
        old = (jnp.zeros((8, 128), f32),) * 3
    return pl.pallas_call(
        functools.partial(expert_kernel, adds),
        grid_spec=pltpu.PrefetchScalarGridSpec(
            num_scalar_prefetch=1,
            grid=(count,),
            in_specs=[
                pl.BlockSpec((1, 1, rows), lambda e, s: (s[e], 0, 0)),
                whole((width, rows)),
                whole((width, rows)),
                whole((rows, width)),
                whole((rows, width)),
                pl.BlockSpec((1, 2, units, width), lambda e, s: (s[e], 0, half, 0)),
                pl.BlockSpec((1, units, width), lambda e, s: (s[e], half, 0)),
                *([each] if adds else []),
                any_place,
                any_place,
                any_place,
            ],
            out_specs=[
                each,
                pl.BlockSpec((1, 2, units, rows), lambda e, s: (s[e], 0, half, 0)),
                pl.BlockSpec((1, units, rows), lambda e, s: (s[e], half, 0)),
                pl.BlockSpec((halves, 1, 1, rows), lambda e, s: (half, s[e], 0, 0)),
            ],
        ),
        out_shape=[
            pltpu.HBM((count, 3, units, width), bf16),
            pltpu.HBM((EXPERTS, 2, w_down.shape[1], rows), bf16),
            pltpu.HBM((EXPERTS, w_down.shape[1], rows), bf16),
            jax.ShapeDtypeStruct((2, EXPERTS, 1, rows), f32),
        ],
        input_output_aliases={} if fresh else {8 + adds: 1, 9 + adds: 2, 10 + adds: 3},
        compiler_params=pltpu.CompilerParams(vmem_limit_bytes=expert_vmem_bytes),
        cost_estimate=pl.CostEstimate(
            flops=count * 12 * rows * width * units,
            bytes_accessed=count * units * width * 12 + 8 * rows * width,
            transcendentals=count * units * rows,
        ),
        name="experts",
    )(ids, gates, xt, ct, x, c, w_up, w_down, *([more] if adds else []), *old)


def from_other_half(shard):
    return lax.ppermute(shard, "tensor", [(0, 1), (1, 0)])


def gathered(shard):
    if lax.axis_size("tensor") != 2:
        return [lax.all_gather(shard, "tensor", axis=0, tiled=True)]
    return [shard, from_other_half(shard)]


def both_parts(part):
    if lax.axis_size("tensor") != 2:
        return lax.psum(part, "tensor"), jnp.zeros_like(part)
    return part, from_other_half(part)


def summed_parts(part):
    low = part.astype(bf16)
    if lax.axis_size("tensor") != 2:
        return lax.psum(low, "tensor").astype(f32)
    return low.astype(f32) + from_other_half(low).astype(f32)


def chip_order(chips):
    there = [2 * z for z in range(chips // 2)]
    return there + [chip + 1 for chip in reversed(there)]


def chunk_experts(device, peers, number):
    order = jnp.array(chip_order(peers // 2), jnp.int32)
    each = EXPERTS // peers
    core = device % 2

    def owned(side):
        chips = jnp.where(side == 0, order, order[::-1])
        return (2 * chips + side) * each + number

    return owned(1 - core).astype(jnp.int32), owned(core).astype(jnp.int32)


def chip_rings():
    order = chip_order(lax.axis_size("dp") // 2)
    return [[2 * chip for chip in order], [2 * chip + 1 for chip in reversed(order)]]


def to_owner(chip_sum):
    return lax.psum_scatter(
        chip_sum, "dp", scatter_dimension=0, axis_index_groups=chip_rings(), tiled=True
    )


def summed_over_tokens(send, keep, beside_one, beside_two):
    swap = [(i, i ^ 1) for i in range(lax.axis_size("dp"))]
    received = lax.ppermute(send, "dp", swap)
    half = (keep.astype(f32) + received.astype(f32)).astype(bf16)
    rings = chip_rings()
    half = lax.psum_scatter(half, "dp", scatter_dimension=0, axis_index_groups=rings, tiled=True)
    half, beside_one = lax.optimization_barrier((half, beside_one))
    half = lax.all_gather(half, "dp", axis=0, axis_index_groups=rings, tiled=True)
    half, beside_two = lax.optimization_barrier((half, beside_two))
    other = lax.ppermute(half, "dp", swap)
    is_first = lax.axis_index("dp") % 2 == 0
    low, high = jnp.where(is_first, half, other), jnp.where(is_first, other, half)
    return jnp.concatenate([low, high], axis=0), beside_one, beside_two


def angles(position):
    inverse = rope_base ** (-2.0 * jnp.arange(HEAD_DIM // 2, dtype=f32) / HEAD_DIM)
    angle = inverse[:, None] * position.astype(f32)[None, :]
    return jnp.cos(angle), jnp.sin(angle)


def scale_of(values):
    return lax.rsqrt(jnp.mean(values * values, axis=-1, keepdims=True) + epsilon)


def norm_back(values, scale, gain, upstream):
    pulled = gain * upstream
    slope = jnp.mean(pulled * values, axis=-1, keepdims=True)
    return (
        scale * pulled - values * (scale * scale * scale * slope),
        jnp.sum(upstream * values * scale, axis=0),
    )


def on_device(
    tokens, doc_ids, routes, attention_gain, w_query, w_key, w_value, w_out, mixture_gain,
    w_router, expert_gate_up, expert_down, out_cotangent,
):
    rows, width = tokens.shape
    peers = lax.axis_size("dp")
    device = lax.axis_index("dp")
    pair_heads = w_key.shape[0] // HEAD_DIM
    group = w_query.shape[1] // w_key.shape[0]
    first = device * rows
    chunks = EXPERTS // peers
    w_out_parts = gathered(w_out)

    docs = lax.dynamic_slice_in_dim(doc_ids, first, rows)
    docs_before = lax.dynamic_slice_in_dim(doc_ids, jnp.maximum(device - 1, 0) * rows, rows)
    docs_before = jnp.where(device > 0, docs_before, -1)
    docs_window = jnp.concatenate([docs_before, docs])
    lo = jnp.sum((docs_window[:, None] < docs[None, :]).astype(jnp.int32), axis=0)
    first_block = lo[::BLOCK] // BLOCK
    lo = lo[None, :]

    position = (first + jnp.arange(rows, dtype=jnp.int32)) % SEQ_LEN
    cosine, sine = angles(position)
    gain_one = attention_gain[None, :]
    normed_attention, q_t, q_rows, k_t, k_rows, v_t, v_rows = project(
        tokens, gain_one, cosine, sine, w_query, w_key, w_value
    )
    to_next = [(i, i + 1) for i in range(0, peers, 2)]
    before = SEQ_LEN - rows
    old_k_t = lax.ppermute(k_t, "dp", to_next)
    old_v_t = lax.ppermute(v_t, "dp", to_next)
    across = lambda tall: jnp.swapaxes(tall.reshape(pair_heads, HEAD_DIM, before), 1, 2)
    old_k_rows, old_v_rows = across(old_k_t), across(old_v_t)

    calls = 2 if pair_heads % 2 == 0 else 1
    here = pair_heads // calls
    pieces = [
        attend(
            first_block, lo, q_t, k_rows, v_t, old_k_rows, old_v_t, group, call * here, here
        )
        for call in range(calls)
    ]
    context_parts = [gathered(piece[0]) for piece in pieces]
    contexts = [parts[side] for side in range(len(context_parts[0])) for parts in context_parts]
    context_t = jnp.concatenate([piece[0] for piece in pieces], axis=0)
    logs = jnp.concatenate([piece[1] for piece in pieces], axis=0)
    w_out_pieces = [
        piece for part in w_out_parts for piece in jnp.split(part, calls, axis=0)
    ]
    hidden, normed_mixture, normed_t, gates = enter_mixture(
        tokens, mixture_gain[None, :], w_router.T, routes.T, contexts, w_out_pieces
    )
    gain_two = mixture_gain.astype(f32)
    scale_two = scale_of(hidden)

    upstream_t = out_cotangent.T
    swap_cores = [(i, i ^ 1) for i in range(peers)]
    shares, arrived, old = [], [], None
    pieces = [(number, half, 1) for number in range(chunks) for half in range(2)]

    def run_experts(piece, side, more):
        ids = chunk_experts(device, peers, piece[0])[side]
        return expert_step(
            ids, piece[1], piece[2], gates[:, None, :], normed_t, normed_mixture, upstream_t, out_cotangent,
            expert_gate_up, expert_down, more, old,
        )

    for number in range(len(pieces) + 1):
        if number < len(pieces):
            send, *old = run_experts(pieces[number], 0, None)
            arrived.append(lax.ppermute(send, "dp", swap_cores))
        if number > 0:
            chip_sum, *old = run_experts(pieces[number - 1], 1, arrived[number - 1])
            shares.append(to_owner(chip_sum))
    up_grad, act, gates_gradient = old
    gates_gradient = gates_gradient[0, :, 0] + gates_gradient[1, :, 0]
    units = expert_down.shape[1]
    wide = EXPERTS * units

    logits_gradient = gates * (
        gates_gradient - jnp.sum(gates * gates_gradient, axis=0, keepdims=True)
    )
    logits_low = logits_gradient.astype(bf16)
    router_gradient = mm(logits_low, normed_mixture)
    up_grad = up_grad.reshape(2 * wide, rows)
    w_up = expert_gate_up.reshape(2 * wide, width)
    own_parts, other_parts, gain_parts = [], [], []
    for start in range(0, rows, rows // 2):
        cut = slice(start, start + rows // 2)
        if start > 0:
            up_grad, own_parts[0] = lax.optimization_barrier((up_grad, own_parts[0]))
        normed_gradient = dot(up_grad[:, cut], w_up, 0, 0) + dot(logits_low[:, cut], w_router, 0, 1)
        part, gain_part = norm_back(hidden[cut], scale_two[cut], gain_two, normed_gradient)
        part = part.astype(bf16)
        if start > 0:
            part, act, other_parts[0] = lax.optimization_barrier((part, act, other_parts[0]))
        own, other = both_parts(part)
        own_parts.append(own)
        other_parts.append(other)
        gain_parts.append(gain_part)
    second_gain_part = gain_parts[0] + gain_parts[1]

    mixture_part = dot(act.reshape(wide, rows), expert_down.reshape(wide, width), 0, 0)
    mixture_low = mixture_part.astype(bf16)
    own_part = jnp.concatenate(own_parts, axis=0)
    other_part = jnp.concatenate(other_parts, axis=0)
    own_part, other_part, mixture_low = lax.optimization_barrier(
        (own_part, other_part, mixture_low)
    )
    mixture_own, mixture_other = both_parts(mixture_low)

    hidden_gradient, d_t, d_rows, spread, w_out_gradient = enter_back(
        out_cotangent, own_part, other_part, w_out, context_t
    )
    by_group = lambda rows_of_heads: rows_of_heads.reshape(pair_heads, group, rows, HEAD_DIM)
    dq_t, dk_t, dv_t, old_dk, old_dv = attend_back(
        first_block, lo, logs, spread.reshape(pair_heads, group, rows), q_t, d_t, by_group(q_rows),
        by_group(d_rows), k_rows, k_t, v_rows, old_k_rows, old_k_t, old_v_rows,
    )
    to_previous = [(i + 1, i) for i in range(0, peers, 2)]
    more_dk = lax.ppermute(old_dk, "dp", to_previous)
    more_dv = lax.ppermute(old_dv, "dp", to_previous)
    dq_t, mixture_other, *shares[:-2] = lax.optimization_barrier(
        (dq_t, mixture_other, *shares[:-2])
    )
    tall, split = w_query.shape[1], w_key.shape[0]
    ends = [tall, tall + split, tall + 2 * split, 2 * tall + 2 * split, 2 * tall + 2 * split + EXPERTS]
    high = -(-(ends[-1] + 2) // (16 * peers)) * 8 * peers
    input_part, send, keep = leave_back(
        (device % 2)[None].astype(jnp.int32), high, tokens, gain_one, cosine, sine, w_query, w_key,
        w_value, normed_attention, dq_t, dk_t, dv_t, more_dk, more_dv, w_out_gradient,
        router_gradient, second_gain_part[None, :],
    )
    part_one, part_two = jnp.split(input_part, 2, axis=0)
    own_one, other_one = both_parts(part_one)
    part_two, other_one = lax.optimization_barrier((part_two, other_one))
    own_two, other_two = both_parts(part_two)
    *shares[-2:], keep = lax.optimization_barrier((*shares[-2:], keep))
    mixed = (hidden + (mixture_own.astype(f32) + mixture_other.astype(f32))).astype(bf16)
    shares = [
        jnp.concatenate(shares[start : start + 2], axis=2) for start in range(0, len(shares), 2)
    ]
    experts_gradient = jnp.concatenate(shares, axis=0).astype(f32)
    up_gradient, down_gradient = experts_gradient[:, :2], experts_gradient[:, 2]
    input_sum = jnp.concatenate(
        [own_one.astype(f32) + other_one.astype(f32), own_two.astype(f32) + other_two.astype(f32)],
        axis=0,
    )
    tokens_gradient = (hidden_gradient + input_sum).astype(bf16)
    gradients, (_, mixed, up_gradient, down_gradient), tokens_gradient = summed_over_tokens(
        send, keep, (other_one, mixed, up_gradient, down_gradient), tokens_gradient
    )
    w_q, w_k, w_v, w_o = jnp.split(gradients[: ends[3]].astype(f32), ends[:3], axis=0)
    small = summed_parts(gradients[ends[3] : ends[4] + 2])
    router, gains = small[:EXPERTS], small[EXPERTS:]
    return (
        mixed, tokens_gradient, gains[1], w_q.T, w_k, w_v, w_o, gains[0], router.T,
        up_gradient, down_gradient,
    )


def solution(mesh):
    placed = (
        P("dp", None),
        P(),
        P("dp", None),
        P(),
        P(None, "tensor"),
        P("tensor", None),
        P("tensor", None),
        P("tensor", None),
        P(),
        P(),
        P(None, None, "tensor", None),
        P(None, "tensor", None),
        P("dp", None),
    )
    return jax.shard_map(
        on_device,
        mesh=mesh,
        in_specs=placed,
        out_specs=(
            P("dp", None),
            P("dp", None),
            P(),
            P(None, "tensor"),
            P("tensor", None),
            P("tensor", None),
            P("tensor", None),
            P(),
            P(),
            P("dp", None, "tensor", None),
            P("dp", "tensor", None),
        ),
        check_vma=False,
    )
```

```python
import functools

import jax
import jax.numpy as jnp
from jax import lax
from jax.experimental import pallas as pl
from jax.experimental.pallas import tpu as pltpu
from jax.sharding import PartitionSpec as P

HEAD_DIM = 64
EXPERTS = 32
SEQ_LEN = 2048
BLOCK = 256

epsilon = 1e-06
score_scale = 0.015625
residual_scale = 0.22
rope_base = 10000.0
masked_value = -1e30
vmem_bytes = 60 * 1024 * 1024
expert_vmem_bytes = 24 * 1024 * 1024
f32 = jnp.float32
bf16 = jnp.bfloat16


def dot(left, right, left_dim, right_dim):
    return lax.dot_general(
        left, right, (((left_dim,), (right_dim,)), ((), ())), preferred_element_type=f32
    )


def mm(left, right):
    return jnp.dot(left, right, preferred_element_type=f32)


def block_mask(lo, hi, start, lanes):
    place = start + lax.broadcasted_iota(jnp.int32, (BLOCK, lanes), 0)
    return (place >= lo) & (place <= hi)


def window_of(lo_ref, block, before, group):
    cut = pl.ds(block * BLOCK, BLOCK)
    lo = lo_ref[:, cut]
    hi = before + block * BLOCK + lax.broadcasted_iota(jnp.int32, (1, BLOCK), 1)
    return (
        jnp.concatenate([lo] * group, axis=1),
        jnp.concatenate([hi] * group, axis=1),
    )


def heads_side_by_side(ref, block, group):
    cut = pl.ds(block * BLOCK, BLOCK)
    return jnp.concatenate(
        [ref[h * HEAD_DIM : (h + 1) * HEAD_DIM, cut] for h in range(group)], axis=1
    )


def heads_one_above(ref, j, block, group):
    cut = pl.ds(block * BLOCK, BLOCK)
    return jnp.concatenate([ref[j, h, cut, :] for h in range(group)], axis=0)


def attend_kernel(
    group, first_ref, lo_ref, qt_ref, k_ref, vt_ref, old_k_ref, old_vt_ref, out_ref, log_ref
):
    lanes = group * BLOCK
    together, before, _ = old_k_ref.shape
    tall = group * HEAD_DIM
    passed = before // BLOCK
    for block in range(qt_ref.shape[1] // BLOCK):
        lo, hi = window_of(lo_ref, block, before, group)
        queries = [
            heads_side_by_side(qt_ref.at[pl.ds(j * tall, tall)], block, group)
            for j in range(together)
        ]

        def step(keys_ref, values_ref, offset, number, carry):
            start = pl.multiple_of(number * BLOCK, BLOCK)
            here = pl.ds(start, BLOCK)
            mask = block_mask(lo, hi, offset + start, lanes)
            result = []
            for j, (peak, total, acc) in enumerate(carry):
                scores = mm(keys_ref[j, here, :], queries[j])
                scores = jnp.where(mask, scores, masked_value)
                top = jnp.maximum(peak, jnp.max(scores, axis=0, keepdims=True))
                weights = jnp.exp(scores - top)
                fade = jnp.exp(peak - top)
                total = total * fade + jnp.sum(weights, axis=0, keepdims=True)
                values = values_ref[j * HEAD_DIM : (j + 1) * HEAD_DIM, here]
                result.append((top, total, acc * fade + mm(values, weights.astype(bf16))))
            return tuple(result)

        first = first_ref[block]
        nothing = (
            jnp.full((1, lanes), masked_value, f32),
            jnp.zeros((1, lanes), f32),
            jnp.zeros((HEAD_DIM, lanes), f32),
        )
        carry = lax.fori_loop(
            first, passed, functools.partial(step, old_k_ref, old_vt_ref, 0), (nothing,) * together
        )
        carry = lax.fori_loop(
            jnp.maximum(first - passed, 0),
            block + 1,
            functools.partial(step, k_ref, vt_ref, before),
            carry,
        )
        cut = pl.ds(block * BLOCK, BLOCK)
        for j, (peak, total, acc) in enumerate(carry):
            result = (acc / total).astype(bf16)
            logs = peak + jnp.log(total)
            for h in range(group):
                side = slice(h * BLOCK, (h + 1) * BLOCK)
                high = j * tall + h * HEAD_DIM
                out_ref[high : high + HEAD_DIM, cut] = result[:, side]
                log_ref[j, h : h + 1, cut] = logs[:, side]


def attend(first, lo, q_t, k, v_t, old_k, old_v_t, group, base, pair_heads):
    rows = k.shape[1]
    before = old_k.shape[1]
    together = 1
    start = base // together
    tall = together * group * HEAD_DIM
    split = together * HEAD_DIM
    by_head = lambda h, s: (start + h, 0, 0)
    flat = lambda h, s: (start + h, 0)
    return pl.pallas_call(
        functools.partial(attend_kernel, group),
        grid_spec=pltpu.PrefetchScalarGridSpec(
            num_scalar_prefetch=1,
            grid=(pair_heads // together,),
            in_specs=[
                pl.BlockSpec((1, rows), lambda h, s: (0, 0)),
                pl.BlockSpec((tall, rows), flat),
                pl.BlockSpec((together, rows, HEAD_DIM), by_head),
                pl.BlockSpec((split, rows), flat),
                pl.BlockSpec((together, before, HEAD_DIM), by_head),
                pl.BlockSpec((split, before), flat),
            ],
            out_specs=[
                pl.BlockSpec((tall, rows), lambda h, s: (h, 0)),
                pl.BlockSpec((together, group, rows), lambda h, s: (h, 0, 0)),
            ],
        ),
        out_shape=[
            jax.ShapeDtypeStruct((pair_heads * group * HEAD_DIM, rows), bf16),
            jax.ShapeDtypeStruct((pair_heads, group, rows), f32),
        ],
        compiler_params=pltpu.CompilerParams(vmem_limit_bytes=vmem_bytes),
        cost_estimate=pl.CostEstimate(
            flops=pair_heads * group * rows * (rows + before) * 512,
            bytes_accessed=8 * 1024 * 1024,
            transcendentals=pair_heads * group * rows * (rows + before),
        ),
        name="attend",
    )(first, lo, q_t, k, v_t, old_k, old_v_t)


def attend_back_kernel(
    group,
    first_ref, lo_ref, log_ref, spread_ref, qt_ref, dt_ref, q_ref, d_ref, k_ref, kt_ref, v_ref,
    old_k_ref, old_kt_ref, old_v_ref,
    dq_ref, dk_ref, dv_ref, old_dk_ref, old_dv_ref, pair_ref, old_pair_ref,
):
    lanes = group * BLOCK
    together, before, _ = old_k_ref.shape
    tall = group * HEAD_DIM
    passed = before // BLOCK
    pair_ref[...] = jnp.zeros_like(pair_ref)
    old_pair_ref[...] = jnp.zeros_like(old_pair_ref)
    for block in range(qt_ref.shape[1] // BLOCK):
        cut = pl.ds(block * BLOCK, BLOCK)
        lo, hi = window_of(lo_ref, block, before, group)
        heads = []
        for j in range(together):
            here = pl.ds(j * tall, tall)
            query_rows = heads_one_above(q_ref, j, block, group)
            upstream_rows = heads_one_above(d_ref, j, block, group)
            nothing = jnp.zeros_like(query_rows)
            both_rows = jnp.concatenate(
                [
                    jnp.concatenate([query_rows, nothing], axis=1),
                    jnp.concatenate([nothing, upstream_rows], axis=1),
                ],
                axis=0,
            )
            heads.append(
                (
                    heads_side_by_side(qt_ref.at[here], block, group),
                    heads_side_by_side(dt_ref.at[here], block, group),
                    both_rows,
                    jnp.concatenate([log_ref[j, h : h + 1, cut] for h in range(group)], axis=1),
                    jnp.concatenate([spread_ref[j, h : h + 1, cut] for h in range(group)], axis=1),
                )
            )

        def step(keys_ref, keys_t_ref, values_ref, sums_ref, offset, number, sums):
            start = pl.multiple_of(number * BLOCK, BLOCK)
            here = pl.ds(start, BLOCK)
            mask = block_mask(lo, hi, start + offset, lanes)
            result = []
            for j, (query, upstream, both_rows, logs, spread) in enumerate(heads):
                scores = mm(keys_ref[j, here, :], query)
                probs = jnp.exp(jnp.where(mask, scores - logs, masked_value))
                change = mm(values_ref[j, here, :], upstream)
                scores_change = (probs * (change - spread)).astype(bf16)
                sums_ref[j, here, :] += mm(
                    jnp.concatenate([scores_change, probs.astype(bf16)], axis=1), both_rows
                )
                keys_t = keys_t_ref[j * HEAD_DIM : (j + 1) * HEAD_DIM, here]
                result.append(sums[j] + mm(keys_t, scores_change))
            return tuple(result)

        first = first_ref[block]
        sums = (jnp.zeros((HEAD_DIM, lanes), f32),) * together
        earlier = functools.partial(step, old_k_ref, old_kt_ref, old_v_ref, old_pair_ref, 0)
        sums = lax.fori_loop(first, passed, earlier, sums)
        own = functools.partial(step, k_ref, kt_ref, v_ref, pair_ref, before)
        sums = lax.fori_loop(jnp.maximum(first - passed, 0), block + 1, own, sums)
        for j in range(together):
            for h in range(group):
                high = j * tall + h * HEAD_DIM
                dq_ref[high : high + HEAD_DIM, cut] = (
                    sums[j][:, h * BLOCK : (h + 1) * BLOCK] * score_scale
                )
    for j in range(together):
        side = slice(j * HEAD_DIM, (j + 1) * HEAD_DIM)
        pair_t = pair_ref[j].T
        dk_ref[side] = pair_t[:HEAD_DIM]
        dv_ref[side] = pair_t[HEAD_DIM:]
        pair_t = old_pair_ref[j].T
        old_dk_ref[side] = pair_t[:HEAD_DIM].astype(bf16)
        old_dv_ref[side] = pair_t[HEAD_DIM:].astype(bf16)


def attend_back(
    first, lo, logs, spread, q_t, d_t, q_rows, d_rows, k, k_t, v, old_k, old_k_t, old_v
):
    pair_heads, before, _ = old_k.shape
    group, rows = q_rows.shape[1:3]
    together = 2 if pair_heads % 2 == 0 else 1
    tall = together * group * HEAD_DIM
    split = together * HEAD_DIM
    by_head = lambda h, s: (h, 0, 0)
    flat = lambda h, s: (h, 0)
    return pl.pallas_call(
        functools.partial(attend_back_kernel, group),
        grid_spec=pltpu.PrefetchScalarGridSpec(
            num_scalar_prefetch=1,
            grid=(pair_heads // together,),
            in_specs=[
                pl.BlockSpec((1, rows), lambda h, s: (0, 0)),
                pl.BlockSpec((together, group, rows), by_head),
                pl.BlockSpec((together, group, rows), by_head),
                pl.BlockSpec((tall, rows), flat),
                pl.BlockSpec((tall, rows), flat),
                pl.BlockSpec((together, group, rows, HEAD_DIM), lambda h, s: (h, 0, 0, 0)),
                pl.BlockSpec((together, group, rows, HEAD_DIM), lambda h, s: (h, 0, 0, 0)),
                pl.BlockSpec((together, rows, HEAD_DIM), by_head),
                pl.BlockSpec((split, rows), flat),
                pl.BlockSpec((together, rows, HEAD_DIM), by_head),
                pl.BlockSpec((together, before, HEAD_DIM), by_head),
                pl.BlockSpec((split, before), flat),
                pl.BlockSpec((together, before, HEAD_DIM), by_head),
            ],
            out_specs=[
                pl.BlockSpec((tall, rows), flat),
                pl.BlockSpec((split, rows), flat),
                pl.BlockSpec((split, rows), flat),
                pl.BlockSpec((split, before), flat),
                pl.BlockSpec((split, before), flat),
            ],
            scratch_shapes=[
                pltpu.VMEM((together, rows, 2 * HEAD_DIM), f32),
                pltpu.VMEM((together, before, 2 * HEAD_DIM), f32),
            ],
        ),
        out_shape=[
            jax.ShapeDtypeStruct((pair_heads * group * HEAD_DIM, rows), f32),
            jax.ShapeDtypeStruct((pair_heads * HEAD_DIM, rows), f32),
            jax.ShapeDtypeStruct((pair_heads * HEAD_DIM, rows), f32),
            jax.ShapeDtypeStruct((pair_heads * HEAD_DIM, before), bf16),
            jax.ShapeDtypeStruct((pair_heads * HEAD_DIM, before), bf16),
        ],
        compiler_params=pltpu.CompilerParams(vmem_limit_bytes=vmem_bytes),
        cost_estimate=pl.CostEstimate(
            flops=pair_heads * group * rows * (rows + before) * 1280,
            bytes_accessed=16 * 1024 * 1024,
            transcendentals=pair_heads * group * rows * (rows + before),
        ),
        name="attend_back",
    )(first, lo, logs, spread, q_t, d_t, q_rows, d_rows, k, k_t, v, old_k, old_k_t, old_v)


def turn(tall, cosine, sine):
    half = HEAD_DIM // 2
    parts = []
    for start in range(0, tall.shape[0], HEAD_DIM):
        a, b = tall[start : start + half], tall[start + half : start + HEAD_DIM]
        parts += [a * cosine - b * sine, b * cosine + a * sine]
    return jnp.concatenate(parts, axis=0)


def put_heads(ref, rows_of_heads):
    for h in range(ref.shape[0]):
        ref[h] = rows_of_heads[:, h * HEAD_DIM : (h + 1) * HEAD_DIM]


def project_kernel(
    x_ref, gain_ref, cos_ref, sin_ref, wq_ref, wk_ref, wv_ref,
    normed_ref, qt_ref, q_ref, kt_ref, k_ref, vt_ref, v_ref,
):
    x = x_ref[...].astype(f32)
    normed = (x * scale_of(x) * gain_ref[...].astype(f32)).astype(bf16)
    normed_ref[...] = normed
    cosine, sine = cos_ref[...], sin_ref[...]
    q_t = turn(mm(normed, wq_ref[...]).T, cosine, sine).astype(bf16).astype(f32) * score_scale
    qt_ref[...] = q_t.astype(bf16)
    put_heads(q_ref, q_t.T.astype(bf16))
    k_t = turn(dot(wk_ref[...], normed, 1, 1), cosine, sine)
    kt_ref[...] = k_t.astype(bf16)
    put_heads(k_ref, k_t.T.astype(bf16))
    v_t = dot(wv_ref[...], normed, 1, 1)
    vt_ref[...] = v_t.astype(bf16)
    put_heads(v_ref, v_t.T.astype(bf16))


def project(tokens, gain, cosine, sine, w_query, w_key, w_value):
    rows, width = tokens.shape
    tall, split = w_query.shape[1], w_key.shape[0]
    heads, pair_heads = tall // HEAD_DIM, split // HEAD_DIM
    whole = lambda shape: pl.BlockSpec(shape, lambda t: (0,) * len(shape))
    down = lambda wide: pl.BlockSpec((BLOCK, wide), lambda t: (t, 0))
    across = lambda high: pl.BlockSpec((high, BLOCK), lambda t: (0, t))
    stacked = lambda count: pl.BlockSpec((count, BLOCK, HEAD_DIM), lambda t: (0, t, 0))
    return pl.pallas_call(
        project_kernel,
        grid=(rows // BLOCK,),
        in_specs=[
            down(width), whole((1, width)), across(HEAD_DIM // 2), across(HEAD_DIM // 2),
            whole((width, tall)), whole((split, width)), whole((split, width)),
        ],
        out_specs=[
            down(width), across(tall), stacked(heads), across(split), stacked(pair_heads),
            across(split), stacked(pair_heads),
        ],
        out_shape=[
            jax.ShapeDtypeStruct((rows, width), bf16),
            jax.ShapeDtypeStruct((tall, rows), bf16),
            jax.ShapeDtypeStruct((heads, rows, HEAD_DIM), bf16),
            jax.ShapeDtypeStruct((split, rows), bf16),
            jax.ShapeDtypeStruct((pair_heads, rows, HEAD_DIM), bf16),
            jax.ShapeDtypeStruct((split, rows), bf16),
            jax.ShapeDtypeStruct((pair_heads, rows, HEAD_DIM), bf16),
        ],
        compiler_params=pltpu.CompilerParams(vmem_limit_bytes=vmem_bytes),
        cost_estimate=pl.CostEstimate(
            flops=2 * rows * width * (tall + 2 * split),
            bytes_accessed=12 * 1024 * 1024,
            transcendentals=0,
        ),
        name="project",
    )(tokens, gain, cosine, sine, w_query, w_key, w_value)


def enter_mixture_kernel(count, x_ref, gain_ref, router_ref, routes_ref, *refs):
    pieces, (hidden_ref, normed_ref, normed_t_ref, gates_ref) = refs[: 2 * count], refs[2 * count :]
    products = [
        mm(context_ref[...].astype(f32).T.astype(bf16), w_ref[...])
        for context_ref, w_ref in zip(pieces[:count], pieces[count:])
    ]
    sides = max(1, count // 2)
    projected = functools.reduce(jnp.add, products[:sides])
    if count > sides:
        projected = projected + functools.reduce(jnp.add, products[sides:])
    hidden = x_ref[...].astype(f32) + residual_scale * projected
    hidden_ref[...] = hidden
    normed = hidden * scale_of(hidden) * gain_ref[...].astype(f32)
    normed_t_ref[...] = normed.T.astype(bf16)
    normed = normed.astype(bf16)
    normed_ref[...] = normed
    logits = dot(router_ref[...], normed, 1, 1)
    expert = lax.broadcasted_iota(jnp.int32, logits.shape, 0)
    chosen = expert == routes_ref[0:1, :]
    for k in range(1, routes_ref.shape[0]):
        chosen = chosen | (expert == routes_ref[k : k + 1, :])
    logits = jnp.where(chosen, logits, masked_value)
    weights = jnp.exp(logits - jnp.max(logits, axis=0, keepdims=True))
    weights = jnp.where(chosen, weights, 0.0)
    gates_ref[...] = weights / jnp.sum(weights, axis=0, keepdims=True)


def enter_mixture(tokens, gain, router_t, routes_t, contexts, weights):
    rows, width = tokens.shape
    whole = lambda shape: pl.BlockSpec(shape, lambda t: (0,) * len(shape))
    down = lambda wide: pl.BlockSpec((BLOCK, wide), lambda t: (t, 0))
    across = lambda high: pl.BlockSpec((high, BLOCK), lambda t: (0, t))
    return pl.pallas_call(
        functools.partial(enter_mixture_kernel, len(contexts)),
        grid=(rows // BLOCK,),
        in_specs=[
            down(width), whole((1, width)), whole(router_t.shape), across(routes_t.shape[0]),
            *[across(context.shape[0]) for context in contexts],
            *[whole(weight.shape) for weight in weights],
        ],
        out_specs=[down(width), down(width), across(width), across(EXPERTS)],
        out_shape=[
            jax.ShapeDtypeStruct((rows, width), f32),
            jax.ShapeDtypeStruct((rows, width), bf16),
            jax.ShapeDtypeStruct((width, rows), bf16),
            jax.ShapeDtypeStruct((EXPERTS, rows), f32),
        ],
        compiler_params=pltpu.CompilerParams(vmem_limit_bytes=expert_vmem_bytes),
        cost_estimate=pl.CostEstimate(
            flops=2 * rows * width * width, bytes_accessed=16 * 1024 * 1024, transcendentals=0
        ),
        name="enter_mixture",
    )(tokens, gain, router_t, routes_t, *contexts, *weights)


def enter_back_kernel(
    c_ref, own_ref, other_ref, wo_ref, ctx_ref, hidden_ref, dt_ref, d_ref, spread_ref, wo_grad_ref
):
    hidden_gradient = c_ref[...].astype(f32) + (
        own_ref[...].astype(f32) + other_ref[...].astype(f32)
    )
    hidden_ref[...] = hidden_gradient
    attention_gradient = (residual_scale * hidden_gradient).astype(bf16)
    d_t = dot(wo_ref[...], attention_gradient, 1, 1)
    dt_ref[...] = d_t.astype(bf16)
    put_heads(d_ref, d_t.T.astype(bf16))
    context_t = ctx_ref[...]
    weighed = d_t.astype(bf16).astype(f32) * context_t.astype(f32)
    for h in range(spread_ref.shape[0]):
        spread_ref[h : h + 1, :] = jnp.sum(
            weighed[h * HEAD_DIM : (h + 1) * HEAD_DIM], axis=0, keepdims=True
        )

    @pl.when(pl.program_id(0) == 0)
    def start():
        wo_grad_ref[...] = jnp.zeros_like(wo_grad_ref)

    wo_grad_ref[...] += mm(context_t, attention_gradient)


def enter_back(cotangent, own, other, w_out, context_t):
    rows, width = cotangent.shape
    tall = w_out.shape[0]
    heads = tall // HEAD_DIM
    whole = lambda shape: pl.BlockSpec(shape, lambda t: (0,) * len(shape))
    down = lambda wide: pl.BlockSpec((BLOCK, wide), lambda t: (t, 0))
    across = lambda high: pl.BlockSpec((high, BLOCK), lambda t: (0, t))
    return pl.pallas_call(
        enter_back_kernel,
        grid=(rows // BLOCK,),
        in_specs=[down(width), down(width), down(width), whole((tall, width)), across(tall)],
        out_specs=[
            down(width), across(tall),
            pl.BlockSpec((heads, BLOCK, HEAD_DIM), lambda t: (0, t, 0)),
            across(heads), whole((tall, width)),
        ],
        out_shape=[
            jax.ShapeDtypeStruct((rows, width), f32),
            jax.ShapeDtypeStruct((tall, rows), bf16),
            jax.ShapeDtypeStruct((heads, rows, HEAD_DIM), bf16),
            jax.ShapeDtypeStruct((heads, rows), f32),
            jax.ShapeDtypeStruct((tall, width), f32),
        ],
        compiler_params=pltpu.CompilerParams(vmem_limit_bytes=vmem_bytes),
        cost_estimate=pl.CostEstimate(
            flops=4 * rows * width * tall, bytes_accessed=20 * 1024 * 1024, transcendentals=0
        ),
        name="enter_back",
    )(cotangent, own, other, w_out, context_t)


def leave_back_kernel(
    core_ref, x_ref, gain_ref, cos_ref, sin_ref, wq_ref, wk_ref, wv_ref, normed_ref,
    dq_ref, dk_ref, dv_ref, more_dk_ref, more_dv_ref, wo_grad_ref, router_grad_ref, gain_two_grad_ref,
    part_ref, send_ref, keep_ref, sum_ref, gain_grad_ref,
):
    step = pl.program_id(0)
    cosine, sine = cos_ref[...], -sin_ref[...]
    dq_t = turn(dq_ref[...], cosine, sine).astype(bf16)
    dk_t = turn(dk_ref[...] + more_dk_ref[...].astype(f32), cosine, sine).astype(bf16)
    dv_t = (dv_ref[...] + more_dv_ref[...].astype(f32)).astype(bf16)
    normed = normed_ref[...]

    @pl.when(step == 0)
    def start():
        sum_ref[...] = jnp.zeros_like(sum_ref)
        gain_grad_ref[...] = jnp.zeros_like(gain_grad_ref)

    stacked = jnp.concatenate([dq_t, dk_t, dv_t], axis=0)
    sum_ref[: stacked.shape[0]] += mm(stacked, normed)
    rows_of = lambda tall: tall.astype(f32).T.astype(bf16)
    upstream = (
        dot(rows_of(dq_t), wq_ref[...], 1, 1)
        + mm(rows_of(dk_t), wk_ref[...])
        + mm(rows_of(dv_t), wv_ref[...])
    )
    x = x_ref[...].astype(f32)
    part, gain_part = norm_back(x, scale_of(x), gain_ref[...].astype(f32), upstream)
    part_ref[...] = part.astype(bf16)
    gain_grad_ref[...] += gain_part[None, :]

    @pl.when(step == pl.num_programs(0) - 1)
    def finish():
        place = stacked.shape[0]
        sum_ref[place : place + wo_grad_ref.shape[0]] = wo_grad_ref[...]
        place += wo_grad_ref.shape[0]
        sum_ref[place : place + EXPERTS] = router_grad_ref[...]
        place += EXPERTS
        sum_ref[place : place + 1] = gain_two_grad_ref[...]
        sum_ref[place + 1 : place + 2] = gain_grad_ref[...]
        high = keep_ref.shape[0]
        send_from = pl.multiple_of((1 - core_ref[0]) * high, 16)
        keep_from = pl.multiple_of(core_ref[0] * high, 16)
        send_ref[...] = sum_ref[pl.ds(send_from, high)].astype(bf16)
        keep_ref[...] = sum_ref[pl.ds(keep_from, high)].astype(bf16)


def leave_back(
    core, high, tokens, gain, cosine, sine, w_query, w_key, w_value, normed, dq_t, dk_t, dv_t,
    more_dk, more_dv, w_out_gradient, router_gradient, second_gain_gradient,
):
    rows, width = tokens.shape
    tall, split = w_query.shape[1], w_key.shape[0]
    whole = lambda shape: pl.BlockSpec(shape, lambda t, s: (0,) * len(shape))
    down = lambda wide: pl.BlockSpec((BLOCK, wide), lambda t, s: (t, 0))
    across = lambda high: pl.BlockSpec((high, BLOCK), lambda t, s: (0, t))
    return pl.pallas_call(
        leave_back_kernel,
        grid_spec=pltpu.PrefetchScalarGridSpec(
            num_scalar_prefetch=1,
            grid=(rows // BLOCK,),
            in_specs=[
                down(width), whole((1, width)), across(HEAD_DIM // 2), across(HEAD_DIM // 2),
                whole((width, tall)), whole((split, width)), whole((split, width)), down(width),
                across(tall), across(split), across(split), across(split), across(split),
                whole((tall, width)), whole((EXPERTS, width)), whole((1, width)),
            ],
            out_specs=[down(width), whole((high, width)), whole((high, width))],
            scratch_shapes=[pltpu.VMEM((2 * high, width), f32), pltpu.VMEM((1, width), f32)],
        ),
        out_shape=[
            jax.ShapeDtypeStruct((rows, width), bf16),
            jax.ShapeDtypeStruct((high, width), bf16),
            jax.ShapeDtypeStruct((high, width), bf16),
        ],
        compiler_params=pltpu.CompilerParams(vmem_limit_bytes=vmem_bytes),
        cost_estimate=pl.CostEstimate(
            flops=4 * rows * width * (tall + 2 * split),
            bytes_accessed=24 * 1024 * 1024,
            transcendentals=0,
        ),
        name="leave_back",
    )(
        core, tokens, gain, cosine, sine, w_query, w_key, w_value, normed, dq_t, dk_t, dv_t,
        more_dk, more_dv, w_out_gradient, router_gradient, second_gain_gradient,
    )


def expert_kernel(
    adds, ids_ref, gates_ref, xt_ref, ct_ref, x_ref, c_ref, up_ref, down_ref, *refs
):
    if adds:
        more_ref, *refs = refs
    _, _, _, grad_ref, up_grad_ref, act_ref, gate_grad_ref = refs
    rows = x_ref.shape[0]
    chunk = min(BLOCK, rows)
    for part in range(rows // chunk):
        cut = pl.ds(part * chunk, chunk)
        xt = xt_ref[:, cut]
        gate = mm(up_ref[0, 0], xt)
        up = mm(up_ref[0, 1], xt)
        active_grad = mm(down_ref[0], ct_ref[:, cut])
        share = 1.0 / (1.0 + jnp.exp(-gate))
        silu = gate * share
        active = silu * up
        weight = gates_ref[0, :, cut] * residual_scale
        gate_grad_ref[0, 0, :, cut] = residual_scale * jnp.sum(
            active * active_grad, axis=0, keepdims=True
        )
        for place in range(1, gate_grad_ref.shape[0]):
            gate_grad_ref[place, 0, :, cut] = jnp.zeros((1, chunk), f32)
        active_grad = active_grad * weight
        act_ref[0, :, cut] = (active * weight).astype(bf16)
        up_grad_ref[0, 0, :, cut] = (
            active_grad * up * (share + silu * (1.0 - share))
        ).astype(bf16)
        up_grad_ref[0, 1, :, cut] = (active_grad * silu).astype(bf16)

    def put(place, total):
        if adds:
            total = total + more_ref[0, place].astype(f32)
        grad_ref[0, place] = total.astype(bf16)

    x = x_ref[...]
    put(0, mm(up_grad_ref[0, 0], x))
    put(1, mm(up_grad_ref[0, 1], x))
    put(2, mm(act_ref[0], c_ref[...]))


def expert_step(ids, half, halves, gates, xt, x, ct, c, w_up, w_down, more, old):
    count = ids.shape[0]
    rows, width = x.shape
    units = w_down.shape[1] // 2 * halves
    any_place = pl.BlockSpec(memory_space=pl.ANY)
    whole = lambda shape: pl.BlockSpec(memory_space=pltpu.VMEM)
    fresh = old is None
    adds = more is not None
    each = pl.BlockSpec((1, 3, units, width), lambda e, s: (e, 0, 0, 0))
    if fresh:
        old = (jnp.zeros((8, 128), f32),) * 3
    return pl.pallas_call(
        functools.partial(expert_kernel, adds),
        grid_spec=pltpu.PrefetchScalarGridSpec(
            num_scalar_prefetch=1,
            grid=(count,),
            in_specs=[
                pl.BlockSpec((1, 1, rows), lambda e, s: (s[e], 0, 0)),
                whole((width, rows)),
                whole((width, rows)),
                whole((rows, width)),
                whole((rows, width)),
                pl.BlockSpec((1, 2, units, width), lambda e, s: (s[e], 0, half, 0)),
                pl.BlockSpec((1, units, width), lambda e, s: (s[e], half, 0)),
                *([each] if adds else []),
                any_place,
                any_place,
                any_place,
            ],
            out_specs=[
                each,
                pl.BlockSpec((1, 2, units, rows), lambda e, s: (s[e], 0, half, 0)),
                pl.BlockSpec((1, units, rows), lambda e, s: (s[e], half, 0)),
                pl.BlockSpec((halves, 1, 1, rows), lambda e, s: (half, s[e], 0, 0)),
            ],
        ),
        out_shape=[
            pltpu.HBM((count, 3, units, width), bf16),
            pltpu.HBM((EXPERTS, 2, w_down.shape[1], rows), bf16),
            pltpu.HBM((EXPERTS, w_down.shape[1], rows), bf16),
            jax.ShapeDtypeStruct((2, EXPERTS, 1, rows), f32),
        ],
        input_output_aliases={} if fresh else {8 + adds: 1, 9 + adds: 2, 10 + adds: 3},
        compiler_params=pltpu.CompilerParams(vmem_limit_bytes=expert_vmem_bytes),
        cost_estimate=pl.CostEstimate(
            flops=count * 12 * rows * width * units,
            bytes_accessed=count * units * width * 12 + 8 * rows * width,
            transcendentals=count * units * rows,
        ),
        name="experts",
    )(ids, gates, xt, ct, x, c, w_up, w_down, *([more] if adds else []), *old)


def from_other_half(shard):
    return lax.ppermute(shard, "tensor", [(0, 1), (1, 0)])


def gathered(shard):
    if lax.axis_size("tensor") != 2:
        return [lax.all_gather(shard, "tensor", axis=0, tiled=True)]
    return [shard, from_other_half(shard)]


def both_parts(part):
    if lax.axis_size("tensor") != 2:
        return lax.psum(part, "tensor"), jnp.zeros_like(part)
    return part, from_other_half(part)


def summed_parts(part):
    low = part.astype(bf16)
    if lax.axis_size("tensor") != 2:
        return lax.psum(low, "tensor").astype(f32)
    return low.astype(f32) + from_other_half(low).astype(f32)


def chip_order(chips):
    there = [2 * z for z in range(chips // 2)]
    return there + [chip + 1 for chip in reversed(there)]


def chunk_experts(device, peers, number):
    order = jnp.array(chip_order(peers // 2), jnp.int32)
    each = EXPERTS // peers
    core = device % 2

    def owned(side):
        chips = jnp.where(side == 0, order, order[::-1])
        return (2 * chips + side) * each + number

    return owned(1 - core).astype(jnp.int32), owned(core).astype(jnp.int32)


def chip_rings():
    order = chip_order(lax.axis_size("dp") // 2)
    return [[2 * chip for chip in order], [2 * chip + 1 for chip in reversed(order)]]


def to_owner(chip_sum):
    return lax.psum_scatter(
        chip_sum, "dp", scatter_dimension=0, axis_index_groups=chip_rings(), tiled=True
    )


def summed_over_tokens(send, keep, beside_one, beside_two):
    swap = [(i, i ^ 1) for i in range(lax.axis_size("dp"))]
    received = lax.ppermute(send, "dp", swap)
    half = (keep.astype(f32) + received.astype(f32)).astype(bf16)
    rings = chip_rings()
    half = lax.psum_scatter(half, "dp", scatter_dimension=0, axis_index_groups=rings, tiled=True)
    half, beside_one = lax.optimization_barrier((half, beside_one))
    half = lax.all_gather(half, "dp", axis=0, axis_index_groups=rings, tiled=True)
    half, beside_two = lax.optimization_barrier((half, beside_two))
    other = lax.ppermute(half, "dp", swap)
    is_first = lax.axis_index("dp") % 2 == 0
    low, high = jnp.where(is_first, half, other), jnp.where(is_first, other, half)
    return jnp.concatenate([low, high], axis=0), beside_one, beside_two


def angles(position):
    inverse = rope_base ** (-2.0 * jnp.arange(HEAD_DIM // 2, dtype=f32) / HEAD_DIM)
    angle = inverse[:, None] * position.astype(f32)[None, :]
    return jnp.cos(angle), jnp.sin(angle)


def scale_of(values):
    return lax.rsqrt(jnp.mean(values * values, axis=-1, keepdims=True) + epsilon)


def norm_back(values, scale, gain, upstream):
    pulled = gain * upstream
    slope = jnp.mean(pulled * values, axis=-1, keepdims=True)
    return (
        scale * pulled - values * (scale * scale * scale * slope),
        jnp.sum(upstream * values * scale, axis=0),
    )


def on_device(
    tokens, doc_ids, routes, attention_gain, w_query, w_key, w_value, w_out, mixture_gain,
    w_router, expert_gate_up, expert_down, out_cotangent,
):
    rows, width = tokens.shape
    peers = lax.axis_size("dp")
    device = lax.axis_index("dp")
    pair_heads = w_key.shape[0] // HEAD_DIM
    group = w_query.shape[1] // w_key.shape[0]
    first = device * rows
    chunks = EXPERTS // peers
    w_out_parts = gathered(w_out)

    docs = lax.dynamic_slice_in_dim(doc_ids, first, rows)
    docs_before = lax.dynamic_slice_in_dim(doc_ids, jnp.maximum(device - 1, 0) * rows, rows)
    docs_before = jnp.where(device > 0, docs_before, -1)
    docs_window = jnp.concatenate([docs_before, docs])
    lo = jnp.sum((docs_window[:, None] < docs[None, :]).astype(jnp.int32), axis=0)
    first_block = lo[::BLOCK] // BLOCK
    lo = lo[None, :]

    position = (first + jnp.arange(rows, dtype=jnp.int32)) % SEQ_LEN
    cosine, sine = angles(position)
    gain_one = attention_gain[None, :]
    normed_attention, q_t, q_rows, k_t, k_rows, v_t, v_rows = project(
        tokens, gain_one, cosine, sine, w_query, w_key, w_value
    )
    to_next = [(i, i + 1) for i in range(0, peers, 2)]
    before = SEQ_LEN - rows
    old_k_t = lax.ppermute(k_t, "dp", to_next)
    old_v_t = lax.ppermute(v_t, "dp", to_next)
    across = lambda tall: jnp.swapaxes(tall.reshape(pair_heads, HEAD_DIM, before), 1, 2)
    old_k_rows, old_v_rows = across(old_k_t), across(old_v_t)

    calls = 2 if pair_heads % 2 == 0 else 1
    here = pair_heads // calls
    pieces = [
        attend(
            first_block, lo, q_t, k_rows, v_t, old_k_rows, old_v_t, group, call * here, here
        )
        for call in range(calls)
    ]
    context_parts = [gathered(piece[0]) for piece in pieces]
    contexts = [parts[side] for side in range(len(context_parts[0])) for parts in context_parts]
    context_t = jnp.concatenate([piece[0] for piece in pieces], axis=0)
    logs = jnp.concatenate([piece[1] for piece in pieces], axis=0)
    w_out_pieces = [
        piece for part in w_out_parts for piece in jnp.split(part, calls, axis=0)
    ]
    hidden, normed_mixture, normed_t, gates = enter_mixture(
        tokens, mixture_gain[None, :], w_router.T, routes.T, contexts, w_out_pieces
    )
    gain_two = mixture_gain.astype(f32)
    scale_two = scale_of(hidden)

    upstream_t = out_cotangent.T
    swap_cores = [(i, i ^ 1) for i in range(peers)]
    shares, arrived, old = [], [], None
    pieces = [(number, half, 1) for number in range(chunks) for half in range(2)]

    def run_experts(piece, side, more):
        ids = chunk_experts(device, peers, piece[0])[side]
        return expert_step(
            ids, piece[1], piece[2], gates[:, None, :], normed_t, normed_mixture, upstream_t, out_cotangent,
            expert_gate_up, expert_down, more, old,
        )

    for number in range(len(pieces) + 1):
        if number < len(pieces):
            send, *old = run_experts(pieces[number], 0, None)
            arrived.append(lax.ppermute(send, "dp", swap_cores))
        if number > 0:
            chip_sum, *old = run_experts(pieces[number - 1], 1, arrived[number - 1])
            shares.append(to_owner(chip_sum))
    up_grad, act, gates_gradient = old
    gates_gradient = gates_gradient[0, :, 0] + gates_gradient[1, :, 0]
    units = expert_down.shape[1]
    wide = EXPERTS * units

    logits_gradient = gates * (
        gates_gradient - jnp.sum(gates * gates_gradient, axis=0, keepdims=True)
    )
    logits_low = logits_gradient.astype(bf16)
    router_gradient = mm(logits_low, normed_mixture)
    up_grad = up_grad.reshape(2 * wide, rows)
    w_up = expert_gate_up.reshape(2 * wide, width)
    own_parts, other_parts, gain_parts = [], [], []
    for start in range(0, rows, rows // 2):
        cut = slice(start, start + rows // 2)
        if start > 0:
            up_grad, own_parts[0] = lax.optimization_barrier((up_grad, own_parts[0]))
        normed_gradient = dot(up_grad[:, cut], w_up, 0, 0) + dot(logits_low[:, cut], w_router, 0, 1)
        part, gain_part = norm_back(hidden[cut], scale_two[cut], gain_two, normed_gradient)
        part = part.astype(bf16)
        if start > 0:
            part, act, other_parts[0] = lax.optimization_barrier((part, act, other_parts[0]))
        own, other = both_parts(part)
        own_parts.append(own)
        other_parts.append(other)
        gain_parts.append(gain_part)
    second_gain_part = gain_parts[0] + gain_parts[1]

    mixture_part = dot(act.reshape(wide, rows), expert_down.reshape(wide, width), 0, 0)
    mixture_low = mixture_part.astype(bf16)
    own_part = jnp.concatenate(own_parts, axis=0)
    other_part = jnp.concatenate(other_parts, axis=0)
    own_part, other_part, mixture_low = lax.optimization_barrier(
        (own_part, other_part, mixture_low)
    )
    mixture_own, mixture_other = both_parts(mixture_low)

    hidden_gradient, d_t, d_rows, spread, w_out_gradient = enter_back(
        out_cotangent, own_part, other_part, w_out, context_t
    )
    by_group = lambda rows_of_heads: rows_of_heads.reshape(pair_heads, group, rows, HEAD_DIM)
    dq_t, dk_t, dv_t, old_dk, old_dv = attend_back(
        first_block, lo, logs, spread.reshape(pair_heads, group, rows), q_t, d_t, by_group(q_rows),
        by_group(d_rows), k_rows, k_t, v_rows, old_k_rows, old_k_t, old_v_rows,
    )
    to_previous = [(i + 1, i) for i in range(0, peers, 2)]
    more_dk = lax.ppermute(old_dk, "dp", to_previous)
    more_dv = lax.ppermute(old_dv, "dp", to_previous)
    dq_t, mixture_other, *shares[:-2] = lax.optimization_barrier(
        (dq_t, mixture_other, *shares[:-2])
    )
    tall, split = w_query.shape[1], w_key.shape[0]
    ends = [tall, tall + split, tall + 2 * split, 2 * tall + 2 * split, 2 * tall + 2 * split + EXPERTS]
    high = -(-(ends[-1] + 2) // (8 * peers)) * 4 * peers
    input_part, send, keep = leave_back(
        (device % 2)[None].astype(jnp.int32), high, tokens, gain_one, cosine, sine, w_query, w_key,
        w_value, normed_attention, dq_t, dk_t, dv_t, more_dk, more_dv, w_out_gradient,
        router_gradient, second_gain_part[None, :],
    )
    part_one, part_two = jnp.split(input_part, 2, axis=0)
    own_one, other_one = both_parts(part_one)
    part_two, other_one = lax.optimization_barrier((part_two, other_one))
    own_two, other_two = both_parts(part_two)
    *shares[-2:], keep = lax.optimization_barrier((*shares[-2:], keep))
    mixed = (hidden + (mixture_own.astype(f32) + mixture_other.astype(f32))).astype(bf16)
    shares = [
        jnp.concatenate(shares[start : start + 2], axis=2) for start in range(0, len(shares), 2)
    ]
    experts_gradient = jnp.concatenate(shares, axis=0).astype(f32)
    up_gradient, down_gradient = experts_gradient[:, :2], experts_gradient[:, 2]
    input_sum = jnp.concatenate(
        [own_one.astype(f32) + other_one.astype(f32), own_two.astype(f32) + other_two.astype(f32)],
        axis=0,
    )
    tokens_gradient = (hidden_gradient + input_sum).astype(bf16)
    gradients, (_, mixed, up_gradient, down_gradient), tokens_gradient = summed_over_tokens(
        send, keep, (other_one, mixed, up_gradient, down_gradient), tokens_gradient
    )
    w_q, w_k, w_v, w_o = jnp.split(gradients[: ends[3]].astype(f32), ends[:3], axis=0)
    small = summed_parts(gradients[ends[3] : ends[4] + 2])
    router, gains = small[:EXPERTS], small[EXPERTS:]
    return (
        mixed, tokens_gradient, gains[1], w_q.T, w_k, w_v, w_o, gains[0], router.T,
        up_gradient, down_gradient,
    )


def solution(mesh):
    placed = (
        P("dp", None),
        P(),
        P("dp", None),
        P(),
        P(None, "tensor"),
        P("tensor", None),
        P("tensor", None),
        P("tensor", None),
        P(),
        P(),
        P(None, None, "tensor", None),
        P(None, "tensor", None),
        P("dp", None),
    )
    return jax.shard_map(
        on_device,
        mesh=mesh,
        in_specs=placed,
        out_specs=(
            P("dp", None),
            P("dp", None),
            P(),
            P(None, "tensor"),
            P("tensor", None),
            P("tensor", None),
            P("tensor", None),
            P(),
            P(),
            P("dp", None, "tensor", None),
            P("dp", "tensor", None),
        ),
        check_vma=False,
    )
```
